128 devices in a mesh: head: 16 (over x, y_hi, core), seq: 8 (over z, y_lo).
Axes of the slice: x: 4, y: 4 (y_hi: 2, y_lo: 2; y = y_hi * 2 + y_lo), z: 4, core: 2. Of those that a mesh axis runs over, the one named last changes fastest.
Arguments:
- hidden: bfloat16 [2048, 8, 2048], P('head', 'seq'), may hold values from -6 to 6
- memory: bfloat16 [50, 8, 2048], P(None, 'seq'), may hold values from -6 to 6
- counts: int32 [8, 2], P('seq'), may hold values from 20 to 50, as said below
- w_qkv: bfloat16 [2048, 3, 2048], P(None, None, 'head'), may hold values from -0.125 to 0.125
- b_query: float32 [2048], P('head'), may hold values from -3 to 3
- b_value: float32 [2048], P('head'), may hold values from -3 to 3
- output_weight: bfloat16 [2048, 2048], P('head'), may hold values from -1 to 1
- b_out: float32 [2048], replicated, may hold values from -2 to 2
- gain_one: float32 [2048], replicated, may hold values from 0.5 to 1.5
- shift_one: float32 [2048], replicated, may hold values from -2 to 2
- gain_two: float32 [2048], replicated, may hold values from 0.5 to 1.5
- shift_two: float32 [2048], replicated, may hold values from -2 to 2
- w_up: bfloat16 [2048, 8192], P(None, 'seq'), may hold values from -0.125 to 0.125
- up_bias: float32 [8192], replicated, may hold values from -3 to 3
- w_down: bfloat16 [8192, 2048], P('seq'), may hold values from -0.0625 to 0.0625
- b_down: float32 [2048], replicated, may hold values from -2 to 2
- cotangent: bfloat16 [2048, 8, 2048], P('head', 'seq'), may hold values from -6 to 6
Outputs:
- output: bfloat16 [2048, 8, 2048], P('head', 'seq')
- grad_hidden: float32 [2048, 8, 2048], P('head', 'seq')
- grad_memory: float32 [50, 8, 2048], P(None, 'seq')
- grad_w_qkv: float32 [2048, 3, 2048], P(None, None, 'head')
- grad_b_query: float32 [2048], P('head')
- grad_b_value: float32 [2048], P('head')
- output_weight_gradient: float32 [2048, 2048], P('head')
- grad_b_out: float32 [2048], replicated
- grad_gain_one: float32 [2048], replicated
- grad_shift_one: float32 [2048], replicated
- grad_gain_two: float32 [2048], replicated
- grad_shift_two: float32 [2048], replicated
- grad_w_up: float32 [2048, 8192], P('head', 'seq')
- grad_b_up: float32 [8192], replicated
- grad_w_down: float32 [8192, 2048], P('seq', 'head')
- grad_b_down: float32 [2048], replicated
The draws below stay inside these ranges and needn't reach their ends.
Inputs may be any that keep to these rules, and one draw needn't show every extreme that they name: counts[s, 0] is how many of the 50 earlier summary states of segment s are used, counts[s, 1] how many of its own 50 summary slots; the first ones in both cases.
All inputs are finite; a program needn't handle non-finite values.
Results may differ from the reference program's by a relative error of at most 0.025.
Values may be sent and summed in bfloat16 or wider, within the bound.
A program may use at most 384 MiB of HBM per device.

```python
import jax
import jax.numpy as jnp
from jax import lax

D = 2048
HEADS = 32
HDIM = 64
FF = 8192
NSUM = 50
LEN = 2048
S = 8


def draw_counts(key, part):
    key = jax.random.fold_in(key, 7)
    first_key, second_key = jax.random.split(key)
    drawn = jax.random.randint(first_key, (S * 2,), 20, 51).astype(jnp.int32)
    spots = jax.random.permutation(second_key, S * 2)
    drawn = drawn.at[spots[0]].set(50).at[spots[1]].set(20)
    return drawn.reshape(S, 2).astype(jnp.int32)


def levels(stream_key, extent, shards, least, high):
    def one(axis_at, blocks):
        draws = jax.random.uniform(jax.random.fold_in(jax.random.fold_in(stream_key, 6), axis_at), (blocks,), jnp.float32, least / len(shards), high / len(shards))
        return jnp.repeat(jnp.exp(draws), extent[axis_at] // blocks).reshape((-1,) + (1,) * (len(extent) - axis_at - 1))

    level = one(*shards[0])
    for cut in shards[1:]:
        level = level * one(*cut)
    return level


def normal_values(rng, extent, scale, most, cuts=(), held_as=jnp.bfloat16):
    values = scale * jax.random.normal(rng, extent, jnp.float32)
    if cuts:
        values = values * levels(rng, extent, cuts, -0.22, 0.18)
    return jnp.clip(values, -most, most).astype(held_as)


def setup_inputs(seed: int = 0) -> dict:
    streams_of = jax.random.split(jax.random.key(seed), 18)
    hidden = normal_values(streams_of[0], (LEN, S, D), 1.0, 6.0, ((0, 16), (1, 8)))
    memory = normal_values(streams_of[1], (NSUM, S, D), 1.0, 6.0, ((1, 8),))
    counts = draw_counts(jax.random.fold_in(streams_of[17], 71), 0)
    w_qkv = normal_values(streams_of[3], (D, 3, HEADS * HDIM), D ** -0.5, 0.125, ((2, 16),))
    b_query = normal_values(streams_of[4], (HEADS * HDIM,), 0.5, 3.0, ((0, 16),), jnp.float32)
    b_value = normal_values(streams_of[5], (HEADS * HDIM,), 0.5, 3.0, ((0, 16),), jnp.float32)
    output_weight = normal_values(streams_of[6], (HEADS * HDIM, D), (D // 64) ** -0.5, 1.0, ((0, 16),))
    b_out = normal_values(streams_of[7], (D,), 0.3, 2.0, (), jnp.float32)
    gain_one = jnp.clip(jax.random.uniform(streams_of[8], (D,), jnp.float32, 0.5, 1.5), 0.5, 1.5)
    shift_one = normal_values(streams_of[9], (D,), 0.3, 2.0, (), jnp.float32)
    gain_two = jnp.clip(jax.random.uniform(streams_of[10], (D,), jnp.float32, 0.5, 1.5), 0.5, 1.5)
    shift_two = normal_values(streams_of[11], (D,), 0.3, 2.0, (), jnp.float32)
    w_up = normal_values(streams_of[12], (D, FF), D ** -0.5, 0.125, ((1, 8),))
    up_bias = normal_values(streams_of[13], (FF,), 0.5, 3.0, (), jnp.float32)
    w_down = normal_values(streams_of[14], (FF, D), FF ** -0.5, 0.0625, ((0, 8),))
    b_down = normal_values(streams_of[15], (D,), 0.3, 2.0, (), jnp.float32)
    cotangent = normal_values(streams_of[16], (LEN, S, D), 1.0, 6.0, ((0, 16), (1, 8)))
    return dict(hidden=hidden, memory=memory, counts=counts, w_qkv=w_qkv, b_query=b_query, b_value=b_value, output_weight=output_weight, b_out=b_out, gain_one=gain_one, shift_one=shift_one, gain_two=gain_two, shift_two=shift_two, w_up=w_up, up_bias=up_bias, w_down=w_down, b_down=b_down, cotangent=cotangent)


EPSILON = 1e-05
NEGATIVE = -1e+30
HIGHEST = lax.Precision.HIGHEST

@jax.custom_vjp
def low(v):
    return lax.optimization_barrier(v.astype(jnp.bfloat16)).astype(jnp.float32)

@jax.custom_vjp
def low_back(v):
    return v

def low_keep(v):
    return (low(v), None)

def low_pass(kept, grad):
    return (grad,)

def back_keep(v):
    return (v, None)

def back_low(kept, grad):
    return (low(grad),)
low.defvjp(low_keep, low_pass)
low_back.defvjp(back_keep, back_low)

def matmul(left, right):
    return jnp.dot(left, right, precision=HIGHEST, preferred_element_type=jnp.float32)

def layer_norm(values, gain_vec, shift_vec):
    row_mean = lax.optimization_barrier(jnp.mean(values, axis=-1, keepdims=True))
    centered = values - row_mean
    row_var = lax.optimization_barrier(jnp.mean(centered * centered, axis=-1, keepdims=True))
    return centered * lax.rsqrt(row_var + EPSILON) * gain_vec + shift_vec

def key_allowed(count_row, row_start, block_rows):
    query_pos = row_start + jnp.arange(block_rows, dtype=jnp.int32)
    key_pos = jnp.arange(NSUM + LEN, dtype=jnp.int32) - NSUM
    text_rows = LEN - NSUM
    memory_ok = (key_pos < 0) & (key_pos + NSUM < count_row[0])
    own_ok = (key_pos >= 0) & ((key_pos < text_rows) | (key_pos - text_rows < count_row[1]))
    return (memory_ok | own_ok)[None, :] & (key_pos[None, :] <= query_pos[:, None])

def attend_block(query_block, row_start, key_rows, value_rows, count_row):
    block_rows = query_block.shape[0]
    scores = jnp.einsum('qhe,khe->hqk', query_block, key_rows, precision=HIGHEST) * HDIM ** (-0.5)
    scores = low_back(scores)
    allowed = key_allowed(count_row, row_start, block_rows)
    scores = jnp.where(allowed[None], scores, NEGATIVE)
    weights = low(jax.nn.softmax(scores, axis=-1))
    return jnp.einsum('hqk,khe->qhe', weights, value_rows, precision=HIGHEST)

def sequence_forward(param_set, rows_in, memory_in, count_row):
    w_qkv, b_query, b_value, output_weight, b_out, gain_one, shift_one, gain_two, shift_two, w_up, up_bias, w_down, b_down = param_set
    normed = low(layer_norm(rows_in, gain_one, shift_one))
    mem_normed = low(layer_norm(memory_in, gain_one, shift_one))
    queries = low(low_back(matmul(normed, w_qkv[:, 0]) + b_query))
    own_keys = low(low_back(matmul(normed, w_qkv[:, 1])))
    own_values = low(low_back(matmul(normed, w_qkv[:, 2]) + b_value))
    mem_keys = low(low_back(matmul(mem_normed, w_qkv[:, 1])))
    mem_values = low(low_back(matmul(mem_normed, w_qkv[:, 2]) + b_value))
    key_rows = jnp.concatenate([mem_keys, own_keys], axis=0).reshape(NSUM + LEN, HEADS, HDIM)
    value_rows = jnp.concatenate([mem_values, own_values], axis=0).reshape(NSUM + LEN, HEADS, HDIM)
    block_rows = min(512, LEN)
    block_total = LEN // block_rows
    query_blocks = queries.reshape(block_total, block_rows, HEADS, HDIM)
    block_starts = jnp.arange(block_total, dtype=jnp.int32) * block_rows
    checked = jax.checkpoint(attend_block)
    attended = lax.map(lambda block_item: checked(block_item[0], block_item[1], key_rows, value_rows, count_row), (query_blocks, block_starts))
    attended = low(low_back(attended.reshape(LEN, HEADS * HDIM)))
    resid = rows_in + low_back(matmul(attended, output_weight)) + b_out
    second_normed_rows = low(layer_norm(resid, gain_two, shift_two))
    preactivation_hidden = low_back(matmul(second_normed_rows, w_up)) + up_bias
    activated_hidden = low(jax.nn.gelu(preactivation_hidden, approximate=True))
    return resid + matmul(activated_hidden, w_down) + b_down

def reference(hidden, memory, counts, w_qkv, b_query, b_value, output_weight, b_out, gain_one, shift_one, gain_two, shift_two, w_up, up_bias, w_down, b_down, cotangent):
    param_set = jax.tree.map(lambda weight_leaf: weight_leaf.astype(jnp.float32), (w_qkv, b_query, b_value, output_weight, b_out, gain_one, shift_one, gain_two, shift_two, w_up, up_bias, w_down, b_down))
    rows_seq = jnp.moveaxis(hidden.astype(jnp.float32), 1, 0)
    mem_seq = jnp.moveaxis(memory.astype(jnp.float32), 1, 0)
    cot_seq = jnp.moveaxis(cotangent.astype(jnp.float32), 1, 0)
    totals = jax.tree.map(jnp.zeros_like, param_set)

    def per_sequence(running, inputs):
        rows_in, memory_in, count_row, cot_rows = inputs

        def forward(params_arg, rows_arg, memory_arg):
            return sequence_forward(params_arg, rows_arg, memory_arg, count_row)
        result, pullback = jax.vjp(forward, param_set, rows_in, memory_in)
        grad_params, grad_rows, grad_mem = pullback(cot_rows)
        running = jax.tree.map(jnp.add, running, grad_params)
        return (running, (result.astype(jnp.bfloat16), grad_rows, grad_mem))
    totals, (outs_seq, grad_rows_seq, grad_mem_seq) = lax.scan(per_sequence, totals, (rows_seq, mem_seq, counts, cot_seq))
    return (jnp.moveaxis(outs_seq, 0, 1), jnp.moveaxis(grad_rows_seq, 0, 1), jnp.moveaxis(grad_mem_seq, 0, 1), totals[0], totals[1], totals[2], totals[3], totals[4], totals[5], totals[6], totals[7], totals[8], totals[9], totals[10], totals[11], totals[12])
```

```python
import jax
import jax.numpy as jnp
from jax import lax
from jax.experimental import pallas as pl
from jax.experimental.pallas import tpu as pltpu
from jax.sharding import PartitionSpec as P

HDIM = 64
EPSILON = 1e-05
NEGATIVE = -1e30
LOW = jnp.bfloat16
WIDE = jnp.float32
QROWS = 256
KROWS = 512
MEMROWS = 64
BLOCK = 128
NEAR_FIRST = ((0, 0), (-1, 0), (1, 0), (0, 1), (2, 0), (-1, 1), (1, 1), (2, 1))
FAR_FIRST = ((2, 1), (2, 0), (1, 1), (-1, 1), (1, 0), (-1, 0), (0, 1), (0, 0))
MESH = pl.DeviceIdType.MESH
VMEM = pl.BlockSpec(memory_space=pltpu.VMEM)
ANY = pl.BlockSpec(memory_space=pl.ANY)
VMEM_LIMIT = 60 * 2**20


def dot(left, right):
    return jnp.dot(left, right, preferred_element_type=WIDE)


def dot_nt(left, right):
    return lax.dot_general(left, right, (((1,), (1,)), ((), ())), preferred_element_type=WIDE)


def dot_tn(left, right):
    return lax.dot_general(left, right, (((0,), (0,)), ((), ())), preferred_element_type=WIDE)


def row_tiles(rows, body, step=16):
    def run(i, carry):
        body(pl.ds(pl.multiple_of(i * step, step), step))
        return carry

    lax.fori_loop(0, rows // step, run, 0)


class Group:
    def __init__(self, axis):
        self.axis = axis
        index = lax.axis_index(axis)
        self.cores = 2 if axis == "head" else 1
        self.core = index % self.cores
        self.pair = index // self.cores % 2
        self.ring = index // (2 * self.cores)

    def chip(self, dr, dp):
        pair = 1 - self.pair if dp else self.pair
        return (self.ring + (dr + 4)) % 4 * 2 + pair

    def block(self, dr, dp, dc=0):
        core = 1 - self.core if dc else self.core
        return self.chip(dr, dp) * self.cores + core

    def device(self, dr, dp, dc=0):
        return {self.axis: self.block(dr, dp, dc)}

    def greet(self, barrier):
        peers = [(1, 0, 0), (-1, 0, 0), (0, 1, 0)] + ([(0, 0, 1)] if self.cores == 2 else [])
        for peer in peers:
            pl.semaphore_signal(barrier, 1, device_id=self.device(*peer), device_id_type=MESH)
        return len(peers)


def greet_all(*groups):
    barrier = pltpu.get_barrier_semaphore()
    pl.semaphore_wait(barrier, sum(group.greet(barrier) for group in groups))


class Gather:
    COPIES = 21

    def __init__(self, group, buf, send, recv, cut=BLOCK):
        self.group, self.buf, self.send, self.recv = group, buf, send, recv
        half = BLOCK // 2
        low = (cut // 2 + 15) // 16 * 16
        every, upper = (0, BLOCK), (cut, BLOCK - cut)
        ops = {
            "v0": ((0, 0), (1, 0, 0), every, (-1, 0)),
            "n0": ((0, 0), (-1, 0, 0), every, (1, 0)),
            "pair": ((0, 0), (0, 1, 0), every, (0, 1)),
            "v0h": ((-1, 0), (1, 0, 0), (0, half), (2, 0)),
            "n0h": ((1, 0), (-1, 0, 0), (half, half), (2, 0)),
            "v1": ((0, 1), (1, 0, 0), (0, cut), (-1, 1)),
            "n1": ((0, 1), (-1, 0, 0), (0, cut), (1, 1)),
            "v1h": ((-1, 1), (1, 0, 0), (0, low), (2, 1)),
            "n1h": ((1, 1), (-1, 0, 0), (low, cut - low), (2, 1)),
            "bv": ((-1, 0), (0, 1, 0), upper, (-1, 1)),
            "bn": ((1, 0), (0, 1, 0), upper, (1, 1)),
            "b2": ((2, 0), (0, 1, 0), upper, (2, 1)),
        }
        if group.cores == 2:
            for place in NEAR_FIRST:
                ops["s%d%d" % place] = (place, (0, 0, 1), every, place)
        self.ops = {name: (i,) + op for i, (name, op) in enumerate(ops.items()) if op[2][1] > 0}
        self.started = []
        self.inward = {
            (0, 0): (),
            (-1, 0): ("v0",),
            (1, 0): ("n0",),
            (0, 1): ("pair",),
            (2, 0): ("v0h", "n0h"),
            (-1, 1): ("v1", "bv"),
            (1, 1): ("n1", "bn"),
            (2, 1): ("v1h", "n1h", "b2"),
        }
        self.outward = {
            (0, 0): ("v0", "n0", "pair"),
            (-1, 0): ("v0h", "bv"),
            (1, 0): ("n0h", "bn"),
            (0, 1): ("v1", "n1"),
            (2, 0): ("b2",),
            (-1, 1): ("v1h",),
            (1, 1): ("n1h",),
            (2, 1): (),
        }

    def copy(self, name, arriving):
        i, place, peer, (start, count), source = self.ops[name]
        sibling = 1 if arriving and name[0] == "s" else 0
        block = self.group.block(*(source if arriving else place), sibling)
        view = self.buf.at[block] if count == BLOCK else self.buf.at[block, pl.ds(start, count)]
        return pltpu.make_async_remote_copy(
            src_ref=view,
            dst_ref=view,
            send_sem=self.send.at[i],
            recv_sem=self.recv.at[i],
            device_id=self.group.device(*peer),
            device_id_type=MESH,
        )

    def arrive(self, *place):
        for name in self.inward[place]:
            if name in self.ops:
                self.copy(name, True).wait_recv()
        names = self.outward[place]
        if self.group.cores == 2:
            names += ("s%d%d" % place,)
        for name in names:
            if name in self.ops:
                self.copy(name, False).start()
                self.started.append(name)

    def sibling(self, *place):
        if self.group.cores == 2:
            self.copy("s%d%d" % place, True).wait_recv()

    def drain(self):
        for name in self.started:
            self.copy(name, False).wait_send()


class Reduce:
    COPIES = 21

    def __init__(self, group, total, stage, land, send, recv, cut=BLOCK, near=None, result=None):
        self.group, self.total, self.land = group, total, land
        self.stage = total if stage is None else stage
        self.staged = stage is not None
        self.send, self.recv, self.near, self.result = send, recv, near, result
        half = BLOCK // 2
        low = (cut // 2 + 15) // 16 * 16
        every, upper = (0, BLOCK), (cut, BLOCK - cut)
        ops = {
            "b2": ((2, 1), (0, 1, 0), upper, 0),
            "n1h": ((2, 1), (1, 0, 0), (0, low), 1),
            "v1h": ((2, 1), (-1, 0, 0), (low, cut - low), 1),
            "n0h": ((2, 0), (1, 0, 0), (0, half), 2),
            "v0h": ((2, 0), (-1, 0, 0), (half, half), 2),
            "bn": ((1, 1), (0, 1, 0), upper, 3),
            "bv": ((-1, 1), (0, 1, 0), upper, 4),
            "n1": ((1, 1), (1, 0, 0), (0, cut), 3),
            "v1": ((-1, 1), (-1, 0, 0), (0, cut), 4),
            "n0": ((1, 0), (1, 0, 0), every, 5),
            "v0": ((-1, 0), (-1, 0, 0), every, 6),
            "pu": ((0, 1), (0, 1, 0), upper, 7),
            "pl": ((0, 1), (0, 1, 0), (0, cut), 7),
        }
        self.ops = {name: (i,) + op for i, (name, op) in enumerate(ops.items()) if op[2][1] > 0}
        self.cut = cut
        self.started = []
        self.early = {(1, 1): "bn", (-1, 1): "bv", (0, 1): "pu"}
        self.inward = {
            (2, 1): (),
            (2, 0): ("b2",),
            (1, 1): ("n1h",),
            (-1, 1): ("v1h",),
            (1, 0): ("bn", "n0h"),
            (-1, 0): ("bv", "v0h"),
            (0, 1): ("n1", "v1"),
            (0, 0): ("pu", "n0", "v0", "pl"),
        }
        self.outward = {
            (2, 1): ("b2", "n1h", "v1h"),
            (2, 0): ("n0h", "v0h"),
            (1, 1): ("n1",),
            (-1, 1): ("v1",),
            (1, 0): ("n0",),
            (-1, 0): ("v0",),
            (0, 1): ("pl",),
            (0, 0): (),
        }

    def copy(self, name):
        i, place, peer, (start, count), slot = self.ops[name]
        return pltpu.make_async_remote_copy(
            src_ref=self.stage.at[FAR_FIRST.index(place), pl.ds(start, count)],
            dst_ref=self.land.at[slot, pl.ds(start, count)],
            send_sem=self.send.at[i],
            recv_sem=self.recv.at[i],
            device_id=self.group.device(*peer),
            device_id_type=MESH,
        )

    def near_copy(self, k):
        return pltpu.make_async_remote_copy(
            src_ref=self.near[0].at[k],
            dst_ref=self.near[1].at[k],
            send_sem=self.send.at[13 + k],
            recv_sem=self.recv.at[13 + k],
            device_id=self.group.device(0, 0, 1),
            device_id_type=MESH,
        )

    def begin(self, name):
        self.copy(name).start()
        self.started.append(name)

    def blend(self, place, start, count, names):
        k = FAR_FIRST.index(place)
        spans = [self.ops[name][3] + (self.ops[name][4],) for name in names]
        marks = {start, start + count}
        for first, size, _ in spans:
            marks |= {m for m in (first, first + size) if start < m < start + count}
        marks = sorted(marks)
        for low, high in zip(marks, marks[1:]):
            slots = [slot for first, size, slot in spans if first <= low and high <= first + size]
            if not (slots or self.near or self.staged or place == (0, 0)):
                continue

            def body(rows):
                at = pl.ds(pl.multiple_of(rows.start + low, 16), 16)
                value = self.total[k, at].astype(WIDE)
                if self.near is not None:
                    value += self.near[1][k, at].astype(WIDE)
                for slot in slots:
                    value += self.land[slot, at].astype(WIDE)
                if place == (0, 0):
                    self.result[at] = value
                else:
                    self.stage[k, at] = value.astype(LOW)

            row_tiles(high - low, body)

    def settle(self, *place):
        if self.near is not None:
            self.near_copy(FAR_FIRST.index(place)).wait_recv()
        rest = BLOCK
        early = self.early.get(place)
        if early in self.ops:
            rest = self.cut
            self.blend(place, self.cut, BLOCK - self.cut, ())
            self.begin(early)
        names = [name for name in self.inward[place] if name in self.ops]
        for name in names:
            self.copy(name).wait_recv()
        self.blend(place, 0, rest, names)
        for name in self.outward[place]:
            if name in self.ops:
                self.begin(name)

    def drain(self):
        for name in self.started:
            self.copy(name).wait_send()
        if self.near is not None:
            for k in range(8):
                self.near_copy(k).wait_send()

    @staticmethod
    def scratch(columns, staged, near):
        part = pltpu.VMEM((8, BLOCK, columns), LOW)
        shapes = [pltpu.VMEM((8, BLOCK, columns), WIDE), part] if staged else [part]
        shapes += [part] + [pltpu.SemaphoreType.DMA((Reduce.COPIES,))] * 2
        return shapes + [part] * 2 if near else shapes


def normal_of(values):
    mean = jnp.mean(values, axis=-1, keepdims=True)
    centered = values - mean
    var = jnp.mean(centered * centered, axis=-1, keepdims=True)
    rstd = lax.rsqrt(var + EPSILON)
    return centered * rstd, rstd


def stack_heads(rows):
    lane = lax.broadcasted_iota(jnp.int32, rows.shape, 1)
    zero = jnp.zeros_like(rows)
    return jnp.concatenate(
        [jnp.where(lane < HDIM, rows, zero), jnp.where(lane < HDIM, zero, rows)], axis=0
    )


def causal_bias(chunk, block, tail_bias):
    key = block * KROWS + lax.broadcasted_iota(jnp.int32, (KROWS, 2 * QROWS), 0)
    lane = lax.broadcasted_iota(jnp.int32, (KROWS, 2 * QROWS), 1)
    query = chunk * QROWS + jnp.where(lane < QROWS, lane, lane - QROWS)
    own = jnp.where(block == 2048 // KROWS - 1, tail_bias, jnp.zeros_like(tail_bias))
    return jnp.where(key <= query, jnp.broadcast_to(own, key.shape), NEGATIVE)


def transpose_into(dst_ref, src_ref):
    rows = src_ref.shape[0]
    if rows <= 256:
        dst_ref[...] = src_ref[...].T
        return

    def body(i, carry):
        at = pl.multiple_of(i * 256, 256)
        dst_ref[:, pl.ds(at, 256)] = src_ref[pl.ds(at, 256), :].T
        return carry

    lax.fori_loop(0, rows // 256, body, 0)


def attend_chunk(chunk, q_ref, k_ref, vt_ref, mk_ref, mvt_ref, mem_bias, tail_bias):
    start = pl.multiple_of(chunk * QROWS, QROWS)
    q2 = stack_heads(q_ref[pl.ds(start, QROWS), :] * HDIM ** (-0.5))

    def values_times(values_t, probs):
        low = probs.astype(LOW)
        return (
            dot(values_t[:HDIM], low[:, :QROWS]),
            dot(values_t[HDIM:], low[:, QROWS:]),
        )

    scores = dot_nt(mk_ref[...], q2) + mem_bias
    peak = jnp.max(scores, axis=0, keepdims=True)
    raised = jnp.exp(scores - peak)
    total = jnp.sum(raised, axis=0, keepdims=True)
    first, second = values_times(mvt_ref[...], raised)

    def update(block, scores, carry):
        peak, total, first, second = carry
        at = pl.multiple_of(block * KROWS, KROWS)
        new_peak = jnp.maximum(peak, jnp.max(scores, axis=0, keepdims=True))
        scale = jnp.exp(peak - new_peak)
        raised = jnp.exp(scores - new_peak)
        total = total * scale + jnp.sum(raised, axis=0, keepdims=True)
        add_first, add_second = values_times(vt_ref[:, pl.ds(at, KROWS)], raised)
        return (
            new_peak,
            total,
            first * scale[:, :QROWS] + add_first,
            second * scale[:, QROWS:] + add_second,
        )

    def block_scores(block):
        at = pl.multiple_of(block * KROWS, KROWS)
        return dot_nt(k_ref[pl.ds(at, KROWS), :], q2)

    full = chunk * QROWS // KROWS
    carry = lax.fori_loop(
        0, full, lambda b, c: update(b, block_scores(b), c), (peak, total, first, second)
    )
    scores = block_scores(full) + causal_bias(chunk, full, tail_bias)
    peak, total, first, second = update(full, scores, carry)
    inverse = 1.0 / total
    attended = jnp.concatenate([first * inverse[:, :QROWS], second * inverse[:, QROWS:]], axis=0)
    return attended, peak + jnp.log(total)


def chip_at(group, order, step):
    return sum(jnp.where(step == j, group.chip(*place), 0) for j, place in enumerate(order))


def open_kernel(
    hidden_ref, cot_ref, memory_ref, gain_ref, shift_ref, w_ref, bias_ref,
    q_ref, k_ref, v_ref, mk_ref, mv_ref, mem_normed_ref, normed_out, cot_out,
    rows_buf, cot_buf, send, recv, cot_send, cot_recv, out_sem,
):
    head, seq = Group("head"), Group("seq")
    gather = Gather(head, rows_buf, send, recv)
    cot_gather = Gather(seq, cot_buf, cot_send, cot_recv)
    own, cot_own = head.block(0, 0), seq.block(0, 0)

    def norm_rows(rows):
        normal, _ = normal_of(hidden_ref[rows].astype(WIDE))
        rows_buf[own, rows] = (normal * gain_ref[...] + shift_ref[...]).astype(LOW)
        cot_buf[cot_own, rows] = cot_ref[rows]

    row_tiles(BLOCK, norm_rows, 32)
    greet_all(head, seq)
    gather.arrive(0, 0)
    cot_gather.arrive(0, 0)

    def norm_memory(rows):
        normal, _ = normal_of(memory_ref[rows].astype(WIDE))
        mem_normed_ref[rows] = (normal * gain_ref[...] + shift_ref[...]).astype(LOW)

    row_tiles(MEMROWS, norm_memory, 32)
    width = q_ref.shape[1]
    mem = (dot(mem_normed_ref[...], w_ref[:, width:]) + bias_ref[:, width:]).astype(LOW)
    mk_ref[...] = mem[:, :width]
    mv_ref[...] = mem[:, width:]
    copies = []

    def project(*place):
        gather.sibling(*place)
        chip = head.chip(*place)
        out = pltpu.make_async_copy(
            rows_buf.at[pl.ds(chip * 2, 2)], normed_out.at[pl.ds(chip * 2, 2)], out_sem.at[len(copies)]
        )
        out.start()
        copies.append(out)
        rows = rows_buf[pl.ds(chip * 2, 2)].reshape(2 * BLOCK, rows_buf.shape[2])
        at = pl.ds(pl.multiple_of(chip * 2 * BLOCK, 2 * BLOCK), 2 * BLOCK)
        for i, ref in enumerate((q_ref, k_ref, v_ref)):
            part = slice(i * width, (i + 1) * width)
            ref[at, :] = (dot(rows, w_ref[:, part]) + bias_ref[:, part]).astype(LOW)

    def keep_cot(*place):
        block = seq.block(*place)
        out = pltpu.make_async_copy(cot_buf.at[block], cot_out.at[block], out_sem.at[len(copies)])
        out.start()
        copies.append(out)

    project(0, 0)
    keep_cot(0, 0)
    gather.arrive(-1, 0)
    gather.arrive(1, 0)
    cot_gather.arrive(-1, 0)
    cot_gather.arrive(1, 0)
    gather.arrive(0, 1)
    cot_gather.arrive(0, 1)
    project(-1, 0)
    project(1, 0)
    gather.arrive(2, 0)
    cot_gather.arrive(2, 0)
    project(0, 1)
    gather.arrive(-1, 1)
    gather.arrive(1, 1)
    cot_gather.arrive(-1, 1)
    cot_gather.arrive(1, 1)
    project(2, 0)
    project(-1, 1)
    project(1, 1)
    gather.arrive(2, 1)
    cot_gather.arrive(2, 1)
    project(2, 1)
    for place in NEAR_FIRST[1:]:
        keep_cot(*place)
    gather.drain()
    cot_gather.drain()
    for out in copies:
        out.wait()


def open_layer(hidden, cot, memory, gain, shift, w, bias):
    rows, model = hidden.shape
    width = w.shape[1] // 3
    part = jax.ShapeDtypeStruct((16 * rows, width), LOW)
    mem_part = jax.ShapeDtypeStruct((MEMROWS, width), LOW)
    sems = [pltpu.SemaphoreType.DMA((Gather.COPIES,))] * 4
    return pl.pallas_call(
        open_kernel,
        out_shape=(
            part, part, part, mem_part, mem_part,
            jax.ShapeDtypeStruct((MEMROWS, model), LOW),
            jax.ShapeDtypeStruct((16, rows, model), LOW),
            jax.ShapeDtypeStruct((8, rows, model), LOW),
        ),
        in_specs=[VMEM] * 7,
        out_specs=(VMEM,) * 6 + (ANY,) * 2,
        scratch_shapes=[pltpu.VMEM((16, rows, model), LOW), pltpu.VMEM((8, rows, model), LOW)]
        + sems + [pltpu.SemaphoreType.DMA((16,))],
        compiler_params=pltpu.CompilerParams(
            collective_id=0, has_side_effects=True, vmem_limit_bytes=VMEM_LIMIT
        ),
        name="open_layer",
    )(hidden, cot, memory, gain, shift, w, bias)


def attend_kernel(
    q_ref, k_ref, v_ref, mk_ref, mv_ref, mem_bias_ref, tail_bias_ref, wo_ref,
    hidden_ref, b_out_ref, gain_ref, shift_ref,
    attn_t_ref, lse_ref, resid_ref, second_ref,
    vt_ref, mvt_ref, attn_ref, total, stage, land, send, recv, near_stage, near_land,
):
    head = Group("head")
    reduce = Reduce(head, total, stage, land, send, recv, 64, (near_stage, near_land), resid_ref)
    transpose_into(vt_ref, v_ref)
    transpose_into(mvt_ref, mv_ref)
    greet_all(head)

    def step(k, carry):
        chip = chip_at(head, FAR_FIRST, k)
        start = pl.multiple_of(chip * QROWS, QROWS)
        attended, lse = attend_chunk(
            chip, q_ref, k_ref, vt_ref, mk_ref, mvt_ref, mem_bias_ref[...], tail_bias_ref[...]
        )
        attn_t_ref[:, pl.ds(start, QROWS)] = attended.astype(LOW)
        attn_ref[...] = attended.T.astype(LOW)
        lse_ref[chip] = lse
        mine = attn_ref[pl.ds(pl.multiple_of(head.core * BLOCK, BLOCK), BLOCK), :]
        other = attn_ref[pl.ds(pl.multiple_of((1 - head.core) * BLOCK, BLOCK), BLOCK), :]
        for at in range(0, total.shape[2], 512):
            near_stage[k, :, at : at + 512] = dot(other, wo_ref[:, at : at + 512]).astype(LOW)
        reduce.near_copy(k).start()
        for at in range(0, total.shape[2], 512):
            total[k, :, at : at + 512] = dot(mine, wo_ref[:, at : at + 512])
        for j, place in enumerate(FAR_FIRST[:-1]):
            @pl.when(k == j + 1)
            def _():
                reduce.settle(*place)
        return carry

    lax.fori_loop(0, 8, step, 0)
    reduce.settle(0, 0)

    def finish(rows):
        resid = hidden_ref[rows].astype(WIDE) + resid_ref[rows] + b_out_ref[...]
        resid_ref[rows] = resid
        normal, _ = normal_of(resid)
        second_ref[rows] = (normal * gain_ref[...] + shift_ref[...]).astype(LOW)

    row_tiles(BLOCK, finish, 32)
    reduce.drain()


def attend_layer(q, k, v, mk, mv, mem_bias, tail_bias, wo, hidden, b_out, gain, shift):
    length, width = q.shape
    rows, model = hidden.shape
    return pl.pallas_call(
        attend_kernel,
        out_shape=(
            jax.ShapeDtypeStruct((width, length), LOW),
            jax.ShapeDtypeStruct((length // QROWS, 1, 2 * QROWS), WIDE),
            jax.ShapeDtypeStruct((rows, model), WIDE),
            jax.ShapeDtypeStruct((rows, model), LOW),
        ),
        in_specs=[VMEM] * 12,
        out_specs=(VMEM,) * 4,
        scratch_shapes=[
            pltpu.VMEM((width, length), LOW),
            pltpu.VMEM((width, MEMROWS), LOW),
            pltpu.VMEM((QROWS, width), LOW),
        ] + Reduce.scratch(model, True, True),
        compiler_params=pltpu.CompilerParams(
            collective_id=1, has_side_effects=True, vmem_limit_bytes=VMEM_LIMIT
        ),
        name="attend_layer",
    )(q, k, v, mk, mv, mem_bias, tail_bias, wo, hidden, b_out, gain, shift)


def gelu_parts(u):
    square = u * u
    t = jnp.tanh(0.7978845608 * (u + 0.044715 * (square * u)))
    half = 0.5 * (1.0 + t)
    slope = half + 0.5 * u * (1.0 - t * t) * (0.7978845608 * (1.0 + 0.134145 * square))
    return u * half, slope


def fold_rows(values):
    return jnp.sum(values.reshape(values.shape[0] // 8, 8, values.shape[1]), axis=0)


def feed_kernel(
    second_ref, w_up_hbm, w_down_hbm, up_bias_ref, cot_hbm, resid_ref, gain_ref, cot_ref,
    grad_resid_ref, sums_ref, branch_hbm, grad_w_ref, grad_b_up_ref,
    rows_buf, wu_ref, wd_ref, cot_buf, act_ref, back_ref, pre_ref, fold_ref, sum_fold, branch_buf,
    load_sem, branch_sem, send, recv,
    total, stage, land, rsend, rrecv,
    w_total, w_land, w_send, w_recv, w_near_stage, w_near_land,
):
    head, seq = Group("head"), Group("seq")
    gather = Gather(seq, rows_buf, send, recv, 64)
    reduce = Reduce(seq, total, stage, land, rsend, rrecv, 128, None, grad_resid_ref)
    w_reduce = Reduce(head, w_total, None, w_land, w_send, w_recv, 128, (w_near_stage, w_near_land), grad_w_ref)
    loads = [
        pltpu.make_async_copy(src, dst, load_sem.at[i])
        for i, (src, dst) in enumerate(
            ((cot_hbm, cot_buf), (w_down_hbm, wd_ref), (w_up_hbm, wu_ref))
        )
    ]
    for load in loads:
        load.start()
    own = seq.block(0, 0)
    rows_buf[own] = second_ref[...]
    fold_ref[...] = jnp.zeros_like(fold_ref)
    greet_all(head, seq)
    gather.arrive(0, 0)
    loads[0].wait()
    loads[1].wait()
    units = act_ref.shape[2]
    model = rows_buf.shape[2]

    def cot_times(i):
        pairs = cot_buf[pl.ds(2 * i, 2)].reshape(2 * BLOCK, model)
        for at in range(0, units, 256):
            part = dot_nt(pairs, wd_ref[at : at + 256, :]).astype(LOW)
            back_ref[pl.ds(2 * i, 2), :, at : at + 256] = part.reshape(2, BLOCK, 256)

    def feed(*place):
        block = seq.block(*place)
        pre_ref[...] = dot(rows_buf[block], wu_ref[...]) + up_bias_ref[...]

        def bend(rows):
            activated, slope = gelu_parts(pre_ref[rows])
            grad_pre = back_ref[block, rows].astype(WIDE) * slope
            act_ref[block, rows] = activated.astype(LOW)
            back_ref[block, rows] = grad_pre.astype(LOW)
            fold_ref[...] += fold_rows(grad_pre)

        row_tiles(BLOCK, bend)
        k = FAR_FIRST.index(place)
        for at in range(0, model, 512):
            total[k, :, at : at + 512] = dot_nt(back_ref[block], wu_ref[at : at + 512, :])

    cot_times(0)
    cot_times(1)
    loads[2].wait()
    cot_times(2)
    cot_times(3)
    feed(0, 0)
    gather.arrive(-1, 0)
    gather.arrive(1, 0)
    gather.arrive(0, 1)
    feed(-1, 0)
    gather.arrive(2, 0)
    feed(1, 0)
    gather.arrive(-1, 1)
    gather.arrive(1, 1)
    feed(0, 1)
    feed(2, 0)
    feed(-1, 1)
    feed(1, 1)
    gather.arrive(2, 1)
    feed(2, 1)
    reduce.settle(2, 1)
    reduce.settle(2, 0)
    grad_b_up_ref[...] = jnp.sum(fold_ref[...], axis=0, keepdims=True)

    def weights(k, carry):
        chip = chip_at(head, FAR_FIRST, k)

        def part(core):
            at = pl.ds(pl.multiple_of(chip * 2 * BLOCK + core * BLOCK, BLOCK), BLOCK)
            length = 8 * BLOCK
            up = dot_tn(
                rows_buf[:, :, at].reshape(length, BLOCK), back_ref[...].reshape(length, units)
            )
            down = dot_tn(
                cot_buf[:, :, at].reshape(length, BLOCK), act_ref[...].reshape(length, units)
            )
            return up.astype(LOW), down.astype(LOW)

        w_near_stage[k, :, :units], w_near_stage[k, :, units:] = part(1 - head.core)
        w_reduce.near_copy(k).start()
        w_total[k, :, :units], w_total[k, :, units:] = part(head.core)
        for j, place in enumerate(FAR_FIRST[:6]):
            @pl.when(k == j + 1)
            def _():
                w_reduce.settle(*place)

        @pl.when(k == 2)
        def _():
            reduce.settle(1, 1)
            reduce.settle(-1, 1)

        @pl.when(k == 5)
        def _():
            reduce.settle(1, 0)
            reduce.settle(-1, 0)

        return carry

    lax.fori_loop(0, 8, weights, 0)
    branch_copies = []

    def branch(i):
        slot = i % 2
        if i >= 2:
            branch_copies[i - 2].wait()
        for at in range(0, model, 512):
            branch_buf[slot, :, at : at + 512] = dot(act_ref[i], wd_ref[:, at : at + 512]).astype(LOW)
        copy = pltpu.make_async_copy(branch_buf.at[slot], branch_hbm.at[i], branch_sem.at[i])
        copy.start()
        branch_copies.append(copy)

    for i in range(4):
        branch(i)
    reduce.settle(0, 1)
    w_reduce.settle(0, 1)
    for i in range(4, 8):
        branch(i)
    reduce.settle(0, 0)
    sum_fold[...] = jnp.zeros_like(sum_fold)

    def back(rows):
        normal, rstd = normal_of(resid_ref[rows])
        incoming = grad_resid_ref[rows]
        scaled = incoming * gain_ref[...]
        inner = jnp.mean(scaled, axis=-1, keepdims=True)
        along = jnp.mean(scaled * normal, axis=-1, keepdims=True)
        cot = cot_ref[rows].astype(WIDE)
        grad = cot + rstd * (scaled - inner - normal * along)
        grad_resid_ref[rows] = grad
        for i, value in enumerate((grad, incoming * normal, incoming, cot)):
            sum_fold[i] += fold_rows(value)

    row_tiles(BLOCK, back)
    sums_ref[...] = jnp.sum(sum_fold[...], axis=1)
    w_reduce.settle(0, 0)
    for copy in branch_copies[-2:]:
        copy.wait()
    gather.drain()
    reduce.drain()
    w_reduce.drain()


def feed_layer(second, w_up, w_down, up_bias, cot_all, resid, gain, cot):
    rows, model = second.shape
    units = w_up.shape[1]
    gather_sems = [pltpu.SemaphoreType.DMA((Gather.COPIES,))] * 2
    return pl.pallas_call(
        feed_kernel,
        out_shape=(
            jax.ShapeDtypeStruct((rows, model), WIDE),
            jax.ShapeDtypeStruct((4, model), WIDE),
            jax.ShapeDtypeStruct((8, rows, model), LOW),
            jax.ShapeDtypeStruct((rows, 2 * units), WIDE),
            jax.ShapeDtypeStruct((1, units), WIDE),
        ),
        in_specs=[VMEM, ANY, ANY, VMEM, ANY, VMEM, VMEM, VMEM],
        out_specs=(VMEM, VMEM, ANY, VMEM, VMEM),
        scratch_shapes=[
            pltpu.VMEM((8, rows, model), LOW),
            pltpu.VMEM((model, units), LOW),
            pltpu.VMEM((units, model), LOW),
            pltpu.VMEM((8, rows, model), LOW),
            pltpu.VMEM((8, rows, units), LOW),
            pltpu.VMEM((8, rows, units), LOW),
            pltpu.VMEM((rows, units), WIDE),
            pltpu.VMEM((8, units), WIDE),
            pltpu.VMEM((4, 8, model), WIDE),
            pltpu.VMEM((2, rows, model), LOW),
            pltpu.SemaphoreType.DMA((3,)),
            pltpu.SemaphoreType.DMA((8,)),
        ] + gather_sems + Reduce.scratch(model, True, False) + Reduce.scratch(2 * units, False, True),
        compiler_params=pltpu.CompilerParams(
            collective_id=2, has_side_effects=True, vmem_limit_bytes=VMEM_LIMIT
        ),
        name="feed_layer",
    )(second, w_up, w_down, up_bias, cot_all, resid, gain, cot)


def attend_back_chunk(
    chunk, q_ref, k_ref, kt_ref, v_ref, mk_ref, mkt_ref, mv_ref, mem_bias, tail_bias,
    attn_t_ref, lse_ref, grad_rows, dk_ref, dv_ref, dmk_ref, dmv_ref,
):
    start = pl.multiple_of(chunk * QROWS, QROWS)
    q2 = stack_heads(q_ref[pl.ds(start, QROWS), :] * HDIM ** (-0.5))
    g2 = stack_heads(grad_rows)
    product = grad_rows.astype(WIDE).T * attn_t_ref[:, pl.ds(start, QROWS)].astype(WIDE)
    inner = jnp.concatenate(
        [
            jnp.sum(product[:HDIM], axis=0, keepdims=True),
            jnp.sum(product[HDIM:], axis=0, keepdims=True),
        ],
        axis=1,
    )
    lse = lse_ref[chunk]

    def piece(scores, values, keys_t):
        probs = jnp.exp(scores - lse)
        grad_probs = dot_nt(values, g2)
        grad_scores = (probs * (grad_probs - inner)).astype(LOW)
        return (
            dot(probs.astype(LOW), g2),
            dot(grad_scores, q2),
            dot(keys_t[:HDIM], grad_scores[:, :QROWS]),
            dot(keys_t[HDIM:], grad_scores[:, QROWS:]),
        )

    dv, dk, first, second = piece(
        dot_nt(mk_ref[...], q2) + mem_bias, mv_ref[...], mkt_ref[...]
    )
    dmv_ref[...] += dv
    dmk_ref[...] += dk

    def block_step(block, bias, carry):
        first, second = carry
        at = pl.multiple_of(block * KROWS, KROWS)
        scores = dot_nt(k_ref[pl.ds(at, KROWS), :], q2)
        if bias is not None:
            scores = scores + bias
        dv, dk, add_first, add_second = piece(
            scores, v_ref[pl.ds(at, KROWS), :], kt_ref[:, pl.ds(at, KROWS)]
        )
        dv_ref[pl.ds(at, KROWS), :] += dv
        dk_ref[pl.ds(at, KROWS), :] += dk
        return first + add_first, second + add_second

    full = chunk * QROWS // KROWS
    carry = lax.fori_loop(0, full, lambda b, c: block_step(b, None, c), (first, second))
    first, second = block_step(full, causal_bias(chunk, full, tail_bias), carry)
    return jnp.concatenate([first, second], axis=0) * HDIM ** (-0.5)


def grad_kernel(
    grad_resid_ref, resid_ref, b_down_ref, branch_hbm, wo_ref,
    q_ref, k_ref, v_ref, mk_ref, mv_ref, mem_bias_ref, tail_bias_ref, attn_t_ref, lse_ref,
    out_ref, own_ref, own_t_ref, mem_ref, mem_t_ref, grad_wo_ref, sums_ref,
    rows_buf, kt_ref, mkt_ref, dk_ref, dv_ref, dmk_ref, dmv_ref, wo_sum, branch_sum, fold_ref,
    load_sem, send, recv, total, land, rsend, rrecv,
):
    head, seq = Group("head"), Group("seq")
    gather = Gather(head, rows_buf, send, recv, 112)
    reduce = Reduce(seq, total, None, land, rsend, rrecv, 128, None, branch_sum)
    loads = [
        pltpu.make_async_copy(branch_hbm.at[seq.block(*place)], total.at[k], load_sem.at[k])
        for k, place in enumerate(FAR_FIRST)
    ]
    for load in loads:
        load.start()
    own = head.block(0, 0)
    rows_buf[own] = grad_resid_ref[...].astype(LOW)
    greet_all(head, seq)
    gather.arrive(0, 0)
    loads[0].wait()
    reduce.settle(2, 1)
    loads[1].wait()
    reduce.settle(2, 0)
    transpose_into(kt_ref, k_ref)
    transpose_into(mkt_ref, mk_ref)
    for ref in (dk_ref, dv_ref, dmk_ref, dmv_ref, wo_sum, fold_ref):
        ref[...] = jnp.zeros_like(ref)
    width, model = wo_ref.shape
    for load in loads[2:]:
        load.wait()

    def step(k, carry):
        @pl.when(k == 0)
        def _():
            gather.sibling(0, 0)

        @pl.when(k == 1)
        def _():
            gather.arrive(-1, 0)
            gather.arrive(1, 0)
            reduce.settle(1, 1)
            reduce.settle(-1, 1)
            gather.arrive(0, 1)
            gather.sibling(-1, 0)

        @pl.when(k == 2)
        def _():
            reduce.settle(1, 0)
            reduce.settle(-1, 0)
            gather.sibling(1, 0)

        @pl.when(k == 3)
        def _():
            gather.arrive(2, 0)
            gather.sibling(0, 1)

        @pl.when(k == 4)
        def _():
            gather.arrive(-1, 1)
            gather.arrive(1, 1)
            gather.sibling(2, 0)

        @pl.when(k == 5)
        def _():
            reduce.settle(0, 1)
            gather.sibling(-1, 1)

        @pl.when(k == 6)
        def _():
            gather.arrive(2, 1)
            gather.sibling(1, 1)

        @pl.when(k == 7)
        def _():
            gather.sibling(2, 1)

        chip = chip_at(head, NEAR_FIRST, k)
        at = pl.ds(pl.multiple_of(chip * QROWS, QROWS), QROWS)
        rows = rows_buf[pl.ds(chip * 2, 2)].reshape(QROWS, model)
        grad_rows = dot_nt(rows, wo_ref[...]).astype(LOW)
        wo_sum[...] += dot(attn_t_ref[:, at], rows)
        dq = attend_back_chunk(
            chip, q_ref, k_ref, kt_ref, v_ref, mk_ref, mkt_ref, mv_ref,
            mem_bias_ref[...], tail_bias_ref[...], attn_t_ref, lse_ref,
            grad_rows, dk_ref, dv_ref, dmk_ref, dmv_ref,
        ).astype(LOW)
        own_t_ref[:width, at] = dq
        own_ref[at, :width] = dq.T
        return carry

    lax.fori_loop(0, 8, step, 0)

    def finish_keys(i, carry):
        at = pl.ds(pl.multiple_of(i * 256, 256), 256)
        dk = dk_ref[at, :].astype(LOW)
        dv = dv_ref[at, :].astype(LOW)
        own_ref[at, width : 2 * width] = dk
        own_ref[at, 2 * width :] = dv
        own_t_ref[width : 2 * width, at] = dk.T
        own_t_ref[2 * width :, at] = dv.T
        fold_ref[...] += fold_rows(own_ref[at, :].astype(WIDE))
        return carry

    lax.fori_loop(0, q_ref.shape[0] // 256, finish_keys, 0)
    for i, ref in enumerate((dmk_ref, dmv_ref)):
        low = ref[...].astype(LOW)
        mem_ref[:, i * width : (i + 1) * width] = low
        mem_t_ref[i * width : (i + 1) * width, :] = low.T
    fold_ref[:, width:] += fold_rows(mem_ref[...].astype(WIDE))
    sums_ref[...] = jnp.sum(fold_ref[...], axis=0, keepdims=True)
    grad_wo_ref[...] = wo_sum[...].astype(LOW)
    reduce.settle(0, 0)

    def finish(rows):
        out_ref[rows] = (resid_ref[rows] + branch_sum[rows] + b_down_ref[...]).astype(LOW)

    row_tiles(BLOCK, finish)
    gather.drain()
    reduce.drain()


def grad_layer(
    grad_resid, resid, b_down, branch, wo, q, k, v, mk, mv, mem_bias, tail_bias, attn_t, lse
):
    rows, model = grad_resid.shape
    length, width = q.shape
    return pl.pallas_call(
        grad_kernel,
        out_shape=(
            jax.ShapeDtypeStruct((rows, model), LOW),
            jax.ShapeDtypeStruct((length, 3 * width), LOW),
            jax.ShapeDtypeStruct((3 * width, length), LOW),
            jax.ShapeDtypeStruct((MEMROWS, 2 * width), LOW),
            jax.ShapeDtypeStruct((2 * width, MEMROWS), LOW),
            jax.ShapeDtypeStruct((width, model), LOW),
            jax.ShapeDtypeStruct((1, 3 * width), WIDE),
        ),
        in_specs=[VMEM] * 3 + [ANY] + [VMEM] * 10,
        out_specs=(VMEM,) * 7,
        scratch_shapes=[
            pltpu.VMEM((16, rows, model), LOW),
            pltpu.VMEM((width, length), LOW),
            pltpu.VMEM((width, MEMROWS), LOW),
            pltpu.VMEM((length, width), WIDE),
            pltpu.VMEM((length, width), WIDE),
            pltpu.VMEM((MEMROWS, width), WIDE),
            pltpu.VMEM((MEMROWS, width), WIDE),
            pltpu.VMEM((width, model), WIDE),
            pltpu.VMEM((rows, model), WIDE),
            pltpu.VMEM((8, 3 * width), WIDE),
            pltpu.SemaphoreType.DMA((8,)),
        ] + [pltpu.SemaphoreType.DMA((Gather.COPIES,))] * 2 + Reduce.scratch(model, False, False),
        compiler_params=pltpu.CompilerParams(
            collective_id=3, has_side_effects=True, vmem_limit_bytes=VMEM_LIMIT
        ),
        name="grad_layer",
    )(grad_resid, resid, b_down, branch, wo, q, k, v, mk, mv, mem_bias, tail_bias, attn_t, lse)


def close_kernel(
    own_ref, own_t_ref, mem_t_ref, grad_wo_ref, mem_normed_ref, normed_hbm, w_ref,
    hidden_ref, gain_ref, grad_resid_ref,
    grad_hidden_ref, grad_w_ref, sums_ref,
    rows_buf, mem_pad, sum_fold, load_sem,
    total, stage, land, send, recv, near_stage, near_land,
    w_total, w_stage, w_land, w_send, w_recv, w_buf, g_send, g_recv,
):
    head, seq = Group("head"), Group("seq")
    reduce = Reduce(head, total, stage, land, send, recv, 112, (near_stage, near_land), grad_hidden_ref)
    w_reduce = Reduce(seq, w_total, w_stage, w_land, w_send, w_recv, 128, None, w_total.at[7])
    gather = Gather(seq, w_buf, g_send, g_recv, 96)
    load = pltpu.make_async_copy(normed_hbm, rows_buf, load_sem)
    load.start()
    width = grad_wo_ref.shape[0]
    model = rows_buf.shape[2]
    length = own_ref.shape[0]
    wide = model // 2
    mem_pad[...] = jnp.zeros_like(mem_pad)
    mem_pad[pl.ds(width, 2 * width), :] = mem_t_ref[...]
    greet_all(head, seq)

    def chunk(k):
        chip = chip_at(head, FAR_FIRST, k)

        def part(core):
            at = pl.ds(pl.multiple_of(chip * QROWS + core * BLOCK, BLOCK), BLOCK)
            return own_ref[at, :]

        mine, other = part(head.core), part(1 - head.core)
        for at in range(0, model, 512):
            near_stage[k, :, at : at + 512] = dot_nt(other, w_ref[at : at + 512, :]).astype(LOW)
        reduce.near_copy(k).start()
        for at in range(0, model, 512):
            total[k, :, at : at + 512] = dot_nt(mine, w_ref[at : at + 512, :])

    def weights(k):
        target = chip_at(seq, FAR_FIRST, k)
        part, side = target // 2, target % 2
        columns = pl.ds(pl.multiple_of(side * wide, wide), wide)

        @pl.when(part < 3)
        def _():
            at = pl.ds(pl.multiple_of(part * width, width), width)
            w_total[k] = dot(
                own_t_ref[at, :], rows_buf[:, :, columns].reshape(length, wide)
            ) + dot(mem_pad[at, :], mem_normed_ref[:, columns])

        @pl.when(part == 3)
        def _():
            w_total[k] = grad_wo_ref[:, columns].astype(WIDE)

    def step(k, carry):
        chunk(k)

        @pl.when(k == 0)
        def _():
            load.wait()

        weights(k)
        for j, place in enumerate(FAR_FIRST[:6]):
            @pl.when(k == j + 1)
            def _():
                reduce.settle(*place)
                if j < 4:
                    w_reduce.settle(*place)
        return carry

    lax.fori_loop(0, 8, step, 0)
    w_reduce.settle(1, 0)
    w_reduce.settle(-1, 0)
    w_reduce.settle(0, 1)
    reduce.settle(0, 1)
    w_reduce.settle(0, 0)
    own = seq.block(0, 0)
    w_buf[own] = w_total[7].astype(LOW)
    gather.arrive(0, 0)
    gather.arrive(-1, 0)
    gather.arrive(1, 0)
    gather.arrive(0, 1)
    reduce.settle(0, 0)
    sum_fold[...] = jnp.zeros_like(sum_fold)

    def back(rows):
        normal, rstd = normal_of(hidden_ref[rows].astype(WIDE))
        incoming = grad_hidden_ref[rows]
        scaled = incoming * gain_ref[...]
        inner = jnp.mean(scaled, axis=-1, keepdims=True)
        along = jnp.mean(scaled * normal, axis=-1, keepdims=True)
        grad_hidden_ref[rows] = grad_resid_ref[rows] + rstd * (scaled - inner - normal * along)
        for i, value in enumerate((incoming * normal, incoming)):
            sum_fold[i] += fold_rows(value)

    row_tiles(BLOCK, back)
    sums_ref[...] = jnp.sum(sum_fold[...], axis=1)
    for place in NEAR_FIRST[4:]:
        gather.arrive(*place)
    grad_w_ref[...] = w_buf[...]
    gather.drain()
    w_reduce.drain()
    reduce.drain()


def close_layer(own, own_t, mem_t, grad_wo, mem_normed, normed_all, w, hidden, gain, grad_resid):
    rows, model = hidden.shape
    width = grad_wo.shape[0]
    sems = [pltpu.SemaphoreType.DMA((Gather.COPIES,))] * 2
    return pl.pallas_call(
        close_kernel,
        out_shape=(
            jax.ShapeDtypeStruct((rows, model), WIDE),
            jax.ShapeDtypeStruct((8, width, model // 2), LOW),
            jax.ShapeDtypeStruct((2, model), WIDE),
        ),
        in_specs=[VMEM] * 5 + [ANY] + [VMEM] * 4,
        out_specs=(VMEM,) * 3,
        scratch_shapes=[
            pltpu.VMEM((16, rows, model), LOW),
            pltpu.VMEM((3 * width, MEMROWS), LOW),
            pltpu.VMEM((2, 8, model), WIDE),
            pltpu.SemaphoreType.DMA,
        ] + Reduce.scratch(model, True, True) + Reduce.scratch(model // 2, True, False)
        + [pltpu.VMEM((8, width, model // 2), LOW)] + sems,
        compiler_params=pltpu.CompilerParams(
            collective_id=4, has_side_effects=True, vmem_limit_bytes=VMEM_LIMIT
        ),
        name="close_layer",
    )(own, own_t, mem_t, grad_wo, mem_normed, normed_all, w, hidden, gain, grad_resid)


def norm_back(values, gain, incoming):
    normal, rstd = normal_of(values)
    scaled = incoming * gain
    inner = jnp.mean(scaled, axis=-1, keepdims=True)
    along = jnp.mean(scaled * normal, axis=-1, keepdims=True)
    return (
        rstd * (scaled - inner - normal * along),
        jnp.sum(incoming * normal, axis=0),
        jnp.sum(incoming, axis=0),
    )


def on_device(
    hidden, memory, counts, w_qkv, b_query, b_value, output_weight, b_out,
    gain_one, shift_one, gain_two, shift_two, w_up, up_bias, w_down, b_down, cotangent,
):
    hidden, memory, cot = hidden[:, 0], memory[:, 0], cotangent[:, 0]
    slots, model = memory.shape
    width, units = w_qkv.shape[2], w_up.shape[1]
    seq_index = lax.axis_index("seq")
    memory = jnp.pad(memory, ((0, MEMROWS - slots), (0, 0)))
    flat_w = w_qkv.reshape(model, 3 * width)
    flat_bias = jnp.concatenate([b_query, jnp.zeros_like(b_query), b_value])[None]
    gain_one, shift_one, gain_two, shift_two, b_out, b_down = (
        vector[None] for vector in (gain_one, shift_one, gain_two, shift_two, b_out, b_down)
    )
    slot = jnp.arange(MEMROWS, dtype=jnp.int32)
    mem_bias = jnp.where(slot < counts[0, 0], 0.0, NEGATIVE).astype(WIDE)[:, None]
    length = 16 * hidden.shape[0]
    position = length - KROWS + jnp.arange(KROWS, dtype=jnp.int32)
    text_rows = length - slots
    own_ok = (position < text_rows) | (position - text_rows < counts[0, 1])
    tail_bias = jnp.where(own_ok, 0.0, NEGATIVE).astype(WIDE)[:, None]
    up_bias_own = lax.dynamic_slice(up_bias, (seq_index * units,), (units,))[None]

    q, k, v, mk, mv, mem_normed, normed_all, cot_all = open_layer(
        hidden, cot, memory, gain_one, shift_one, flat_w, flat_bias
    )
    attn_t, lse, resid, second = attend_layer(
        q, k, v, mk, mv, mem_bias, tail_bias, output_weight, hidden, b_out, gain_two, shift_two
    )
    grad_resid, feed_sums, branch, grad_w, grad_b_up = feed_layer(
        second, w_up, w_down, up_bias_own, cot_all, resid, gain_two, cot
    )
    output, own, own_t, mem, mem_t, grad_wo, bias_sums = grad_layer(
        grad_resid, resid, b_down, branch, output_weight,
        q, k, v, mk, mv, mem_bias, tail_bias, attn_t, lse,
    )
    grad_mem_normed = dot_nt(mem, flat_w[:, width:])
    memory_back, gain_states, shift_states = norm_back(
        memory.astype(WIDE), gain_one, grad_mem_normed
    )
    grad_memory = lax.psum(memory_back[:slots].astype(LOW), "head").astype(WIDE)
    bias_sums = lax.psum(bias_sums[0].astype(LOW), "seq").astype(WIDE)
    grad_hidden, grad_heads, norm_sums = close_layer(
        own, own_t, mem_t, grad_wo, mem_normed, normed_all, flat_w, hidden, gain_one, grad_resid
    )
    grad_heads = grad_heads.reshape(4, 2, width, model // 2).transpose(1, 3, 0, 2)
    grad_heads = grad_heads.reshape(model, 4, width).astype(WIDE)
    grad_b_up = lax.dynamic_update_slice(
        jnp.zeros(up_bias.shape, WIDE), grad_b_up[0], (seq_index * units,)
    )
    totals = lax.psum(
        jnp.concatenate(
            [
                feed_sums[0],
                norm_sums[0] + gain_states,
                norm_sums[1] + shift_states,
                feed_sums[1],
                feed_sums[2],
                feed_sums[3],
                grad_b_up,
            ]
        ),
        ("head", "seq"),
    )
    sums = [totals[i * model : (i + 1) * model] for i in range(6)]
    return (
        output[:, None],
        grad_hidden[:, None],
        grad_memory[:, None],
        grad_heads[:, :3],
        bias_sums[:width],
        bias_sums[2 * width :],
        grad_heads[:, 3].T,
        sums[0],
        sums[1],
        sums[2],
        sums[3],
        sums[4],
        grad_w[:, :units],
        totals[6 * model :],
        grad_w[:, units:].T,
        sums[5],
    )


def solution(mesh):
    return jax.shard_map(
        on_device,
        mesh=mesh,
        in_specs=(
            P("head", "seq", None),
            P(None, "seq", None),
            P("seq", None),
            P(None, None, "head"),
            P("head"),
            P("head"),
            P("head", None),
            P(),
            P(),
            P(),
            P(),
            P(),
            P(None, "seq"),
            P(),
            P("seq", None),
            P(),
            P("head", "seq", None),
        ),
        out_specs=(
            P("head", "seq", None),
            P("head", "seq", None),
            P(None, "seq", None),
            P(None, None, "head"),
            P("head"),
            P("head"),
            P("head", None),
            P(),
            P(),
            P(),
            P(),
            P(),
            P("head", "seq"),
            P(),
            P("seq", "head"),
            P(),
        ),
        check_vma=False,
    )
```

```python
import jax
import jax.numpy as jnp
from jax import lax
from jax.experimental import pallas as pl
from jax.experimental.pallas import tpu as pltpu
from jax.sharding import PartitionSpec as P

HDIM = 64
EPSILON = 1e-05
NEGATIVE = -1e30
LOW = jnp.bfloat16
WIDE = jnp.float32
QROWS = 256
KROWS = 512
MEMROWS = 64
BLOCK = 128
NEAR_FIRST = ((0, 0), (-1, 0), (1, 0), (0, 1), (2, 0), (-1, 1), (1, 1), (2, 1))
FAR_FIRST = ((2, 1), (2, 0), (1, 1), (-1, 1), (1, 0), (-1, 0), (0, 1), (0, 0))
MESH = pl.DeviceIdType.MESH
VMEM = pl.BlockSpec(memory_space=pltpu.VMEM)
ANY = pl.BlockSpec(memory_space=pl.ANY)
VMEM_LIMIT = 60 * 2**20


def dot(left, right):
    return jnp.dot(left, right, preferred_element_type=WIDE)


def dot_nt(left, right):
    return lax.dot_general(left, right, (((1,), (1,)), ((), ())), preferred_element_type=WIDE)


def dot_tn(left, right):
    return lax.dot_general(left, right, (((0,), (0,)), ((), ())), preferred_element_type=WIDE)


def row_tiles(rows, body, step=16):
    def run(i, carry):
        body(pl.ds(pl.multiple_of(i * step, step), step))
        return carry

    lax.fori_loop(0, rows // step, run, 0)


class Group:
    def __init__(self, axis):
        self.axis = axis
        index = lax.axis_index(axis)
        self.me = index
        self.cores = 2 if axis == "head" else 1
        self.size = 8 * self.cores
        self.core = index % self.cores
        self.pair = index // self.cores % 2
        self.ring = index // (2 * self.cores)

    def chip(self, dr, dp):
        pair = 1 - self.pair if dp else self.pair
        return (self.ring + (dr + 4)) % 4 * 2 + pair

    def block(self, dr, dp, dc=0):
        core = 1 - self.core if dc else self.core
        return self.chip(dr, dp) * self.cores + core

    def device(self, dr, dp, dc=0):
        return {self.axis: self.block(dr, dp, dc)}

    def ahead(self, step):
        return (self.me + step) % self.size

    def away(self, step):
        return {self.axis: self.ahead(step)}

    def greet(self, barrier):
        peers = [(1, 0, 0), (-1, 0, 0), (0, 1, 0)] + ([(0, 0, 1)] if self.cores == 2 else [])
        for peer in peers:
            pl.semaphore_signal(barrier, 1, device_id=self.device(*peer), device_id_type=MESH)
        return len(peers)


def greet_all(*groups):
    barrier = pltpu.get_barrier_semaphore()
    pl.semaphore_wait(barrier, sum(group.greet(barrier) for group in groups))


class Gather:
    COPIES = 21

    def __init__(self, group, buf, send, recv, cut=BLOCK):
        self.group, self.buf, self.send, self.recv = group, buf, send, recv
        half = BLOCK // 2
        low = (cut // 2 + 15) // 16 * 16
        every, upper = (0, BLOCK), (cut, BLOCK - cut)
        ops = {
            "v0": ((0, 0), (1, 0, 0), every, (-1, 0)),
            "n0": ((0, 0), (-1, 0, 0), every, (1, 0)),
            "pair": ((0, 0), (0, 1, 0), every, (0, 1)),
            "v0h": ((-1, 0), (1, 0, 0), (0, half), (2, 0)),
            "n0h": ((1, 0), (-1, 0, 0), (half, half), (2, 0)),
            "v1": ((0, 1), (1, 0, 0), (0, cut), (-1, 1)),
            "n1": ((0, 1), (-1, 0, 0), (0, cut), (1, 1)),
            "v1h": ((-1, 1), (1, 0, 0), (0, low), (2, 1)),
            "n1h": ((1, 1), (-1, 0, 0), (low, cut - low), (2, 1)),
            "bv": ((-1, 0), (0, 1, 0), upper, (-1, 1)),
            "bn": ((1, 0), (0, 1, 0), upper, (1, 1)),
            "b2": ((2, 0), (0, 1, 0), upper, (2, 1)),
        }
        if group.cores == 2:
            for place in NEAR_FIRST:
                ops["s%d%d" % place] = (place, (0, 0, 1), every, place)
        self.ops = {name: (i,) + op for i, (name, op) in enumerate(ops.items()) if op[2][1] > 0}
        self.started = []
        self.inward = {
            (0, 0): (),
            (-1, 0): ("v0",),
            (1, 0): ("n0",),
            (0, 1): ("pair",),
            (2, 0): ("v0h", "n0h"),
            (-1, 1): ("v1", "bv"),
            (1, 1): ("n1", "bn"),
            (2, 1): ("v1h", "n1h", "b2"),
        }
        self.outward = {
            (0, 0): ("v0", "n0", "pair"),
            (-1, 0): ("v0h", "bv"),
            (1, 0): ("n0h", "bn"),
            (0, 1): ("v1", "n1"),
            (2, 0): ("b2",),
            (-1, 1): ("v1h",),
            (1, 1): ("n1h",),
            (2, 1): (),
        }

    def copy(self, name, arriving):
        i, place, peer, (start, count), source = self.ops[name]
        sibling = 1 if arriving and name[0] == "s" else 0
        block = self.group.block(*(source if arriving else place), sibling)
        view = self.buf.at[block] if count == BLOCK else self.buf.at[block, pl.ds(start, count)]
        return pltpu.make_async_remote_copy(
            src_ref=view,
            dst_ref=view,
            send_sem=self.send.at[i],
            recv_sem=self.recv.at[i],
            device_id=self.group.device(*peer),
            device_id_type=MESH,
        )

    def arrive(self, *place):
        for name in self.inward[place]:
            if name in self.ops:
                self.copy(name, True).wait_recv()
        names = self.outward[place]
        if self.group.cores == 2:
            names += ("s%d%d" % place,)
        for name in names:
            if name in self.ops:
                self.copy(name, False).start()
                self.started.append(name)

    def sibling(self, *place):
        if self.group.cores == 2:
            self.copy("s%d%d" % place, True).wait_recv()

    def drain(self):
        for name in self.started:
            self.copy(name, False).wait_send()


class Reduce:
    COPIES = 21

    def __init__(self, group, total, stage, land, send, recv, cut=BLOCK, near=None, result=None):
        self.group, self.total, self.land = group, total, land
        self.stage = total if stage is None else stage
        self.staged = stage is not None
        self.send, self.recv, self.near, self.result = send, recv, near, result
        half = BLOCK // 2
        low = (cut // 2 + 15) // 16 * 16
        every, upper = (0, BLOCK), (cut, BLOCK - cut)
        ops = {
            "b2": ((2, 1), (0, 1, 0), upper, 0),
            "n1h": ((2, 1), (1, 0, 0), (0, low), 1),
            "v1h": ((2, 1), (-1, 0, 0), (low, cut - low), 1),
            "n0h": ((2, 0), (1, 0, 0), (0, half), 2),
            "v0h": ((2, 0), (-1, 0, 0), (half, half), 2),
            "bn": ((1, 1), (0, 1, 0), upper, 3),
            "bv": ((-1, 1), (0, 1, 0), upper, 4),
            "n1": ((1, 1), (1, 0, 0), (0, cut), 3),
            "v1": ((-1, 1), (-1, 0, 0), (0, cut), 4),
            "n0": ((1, 0), (1, 0, 0), every, 5),
            "v0": ((-1, 0), (-1, 0, 0), every, 6),
            "pu": ((0, 1), (0, 1, 0), upper, 7),
            "pl": ((0, 1), (0, 1, 0), (0, cut), 7),
        }
        self.ops = {name: (i,) + op for i, (name, op) in enumerate(ops.items()) if op[2][1] > 0}
        self.cut = cut
        self.started = []
        self.early = {(1, 1): "bn", (-1, 1): "bv", (0, 1): "pu"}
        self.inward = {
            (2, 1): (),
            (2, 0): ("b2",),
            (1, 1): ("n1h",),
            (-1, 1): ("v1h",),
            (1, 0): ("bn", "n0h"),
            (-1, 0): ("bv", "v0h"),
            (0, 1): ("n1", "v1"),
            (0, 0): ("pu", "n0", "v0", "pl"),
        }
        self.outward = {
            (2, 1): ("b2", "n1h", "v1h"),
            (2, 0): ("n0h", "v0h"),
            (1, 1): ("n1",),
            (-1, 1): ("v1",),
            (1, 0): ("n0",),
            (-1, 0): ("v0",),
            (0, 1): ("pl",),
            (0, 0): (),
        }

    def copy(self, name):
        i, place, peer, (start, count), slot = self.ops[name]
        return pltpu.make_async_remote_copy(
            src_ref=self.stage.at[FAR_FIRST.index(place), pl.ds(start, count)],
            dst_ref=self.land.at[slot, pl.ds(start, count)],
            send_sem=self.send.at[i],
            recv_sem=self.recv.at[i],
            device_id=self.group.device(*peer),
            device_id_type=MESH,
        )

    def near_copy(self, k):
        return pltpu.make_async_remote_copy(
            src_ref=self.near[0].at[k],
            dst_ref=self.near[1].at[k],
            send_sem=self.send.at[13 + k],
            recv_sem=self.recv.at[13 + k],
            device_id=self.group.device(0, 0, 1),
            device_id_type=MESH,
        )

    def begin(self, name):
        self.copy(name).start()
        self.started.append(name)

    def blend(self, place, start, count, names):
        k = FAR_FIRST.index(place)
        spans = [self.ops[name][3] + (self.ops[name][4],) for name in names]
        marks = {start, start + count}
        for first, size, _ in spans:
            marks |= {m for m in (first, first + size) if start < m < start + count}
        marks = sorted(marks)
        for low, high in zip(marks, marks[1:]):
            slots = [slot for first, size, slot in spans if first <= low and high <= first + size]
            if not (slots or self.near or self.staged or place == (0, 0)):
                continue

            def body(rows):
                at = pl.ds(pl.multiple_of(rows.start + low, 16), 16)
                value = self.total[k, at].astype(WIDE)
                if self.near is not None:
                    value += self.near[1][k, at].astype(WIDE)
                for slot in slots:
                    value += self.land[slot, at].astype(WIDE)
                if place == (0, 0):
                    self.result[at] = value
                else:
                    self.stage[k, at] = value.astype(LOW)

            row_tiles(high - low, body)

    def settle(self, *place):
        if self.near is not None:
            self.near_copy(FAR_FIRST.index(place)).wait_recv()
        rest = BLOCK
        early = self.early.get(place)
        if early in self.ops:
            rest = self.cut
            self.blend(place, self.cut, BLOCK - self.cut, ())
            self.begin(early)
        names = [name for name in self.inward[place] if name in self.ops]
        for name in names:
            self.copy(name).wait_recv()
        self.blend(place, 0, rest, names)
        for name in self.outward[place]:
            if name in self.ops:
                self.begin(name)

    def drain(self):
        for name in self.started:
            self.copy(name).wait_send()
        if self.near is not None:
            for k in range(8):
                self.near_copy(k).wait_send()

    @staticmethod
    def scratch(columns, staged, near):
        part = pltpu.VMEM((8, BLOCK, columns), LOW)
        shapes = [pltpu.VMEM((8, BLOCK, columns), WIDE), part] if staged else [part]
        shapes += [part] + [pltpu.SemaphoreType.DMA((Reduce.COPIES,))] * 2
        return shapes + [part] * 2 if near else shapes


def greet_everyone(*groups):
    barrier = pltpu.get_barrier_semaphore()
    for group in groups:
        def signal(step, carry):
            pl.semaphore_signal(barrier, 1, device_id=group.away(step), device_id_type=MESH)
            return carry

        lax.fori_loop(1, group.size, signal, 0)
    pl.semaphore_wait(barrier, sum(group.size - 1 for group in groups))


class Spread:
    def __init__(self, group, send, recv):
        self.group, self.send, self.recv = group, send, recv

    def copy(self, step, src, dst):
        return pltpu.make_async_remote_copy(
            src_ref=src,
            dst_ref=dst,
            send_sem=self.send.at[step],
            recv_sem=self.recv.at[step],
            device_id=self.group.away(step),
            device_id_type=MESH,
        )

    def each(self, body):
        def run(step, carry):
            body(step)
            return carry

        lax.fori_loop(1, self.group.size, run, 0)

    def start(self, src_of, land):
        self.each(lambda step: self.copy(step, src_of(self.group.ahead(step)), land.at[self.group.me]).start())

    def wait(self, land):
        def one(step):
            slot = land.at[self.group.ahead(self.group.size - step)]
            self.copy(step, slot, slot).wait_recv()

        self.each(one)

    def drain(self, src_of, land):
        self.each(lambda step: self.copy(step, src_of(self.group.ahead(step)), land.at[self.group.me]).wait_send())


def normal_of(values):
    mean = jnp.mean(values, axis=-1, keepdims=True)
    centered = values - mean
    var = jnp.mean(centered * centered, axis=-1, keepdims=True)
    rstd = lax.rsqrt(var + EPSILON)
    return centered * rstd, rstd


def stack_heads(rows):
    lane = lax.broadcasted_iota(jnp.int32, rows.shape, 1)
    zero = jnp.zeros_like(rows)
    return jnp.concatenate(
        [jnp.where(lane < HDIM, rows, zero), jnp.where(lane < HDIM, zero, rows)], axis=0
    )


def causal_bias(chunk, block, tail_bias):
    key = block * KROWS + lax.broadcasted_iota(jnp.int32, (KROWS, 2 * QROWS), 0)
    lane = lax.broadcasted_iota(jnp.int32, (KROWS, 2 * QROWS), 1)
    query = chunk * QROWS + jnp.where(lane < QROWS, lane, lane - QROWS)
    own = jnp.where(block == 2048 // KROWS - 1, tail_bias, jnp.zeros_like(tail_bias))
    return jnp.where(key <= query, jnp.broadcast_to(own, key.shape), NEGATIVE)


def transpose_into(dst_ref, src_ref):
    rows = src_ref.shape[0]
    if rows <= 256:
        dst_ref[...] = src_ref[...].T
        return

    def body(i, carry):
        at = pl.multiple_of(i * 256, 256)
        dst_ref[:, pl.ds(at, 256)] = src_ref[pl.ds(at, 256), :].T
        return carry

    lax.fori_loop(0, rows // 256, body, 0)


def attend_chunk(chunk, q_ref, k_ref, vt_ref, mk_ref, mvt_ref, mem_bias, tail_bias):
    start = pl.multiple_of(chunk * QROWS, QROWS)
    q2 = stack_heads(q_ref[pl.ds(start, QROWS), :] * HDIM ** (-0.5))

    def values_times(values_t, probs):
        low = probs.astype(LOW)
        return (
            dot(values_t[:HDIM], low[:, :QROWS]),
            dot(values_t[HDIM:], low[:, QROWS:]),
        )

    scores = dot_nt(mk_ref[...], q2) + mem_bias
    peak = jnp.max(scores, axis=0, keepdims=True)
    raised = jnp.exp(scores - peak)
    total = jnp.sum(raised, axis=0, keepdims=True)
    first, second = values_times(mvt_ref[...], raised)

    def update(block, scores, carry):
        peak, total, first, second = carry
        at = pl.multiple_of(block * KROWS, KROWS)
        new_peak = jnp.maximum(peak, jnp.max(scores, axis=0, keepdims=True))
        scale = jnp.exp(peak - new_peak)
        raised = jnp.exp(scores - new_peak)
        total = total * scale + jnp.sum(raised, axis=0, keepdims=True)
        add_first, add_second = values_times(vt_ref[:, pl.ds(at, KROWS)], raised)
        return (
            new_peak,
            total,
            first * scale[:, :QROWS] + add_first,
            second * scale[:, QROWS:] + add_second,
        )

    def block_scores(block):
        at = pl.multiple_of(block * KROWS, KROWS)
        return dot_nt(k_ref[pl.ds(at, KROWS), :], q2)

    full = chunk * QROWS // KROWS
    carry = lax.fori_loop(
        0, full, lambda b, c: update(b, block_scores(b), c), (peak, total, first, second)
    )
    scores = block_scores(full) + causal_bias(chunk, full, tail_bias)
    peak, total, first, second = update(full, scores, carry)
    inverse = 1.0 / total
    attended = jnp.concatenate([first * inverse[:, :QROWS], second * inverse[:, QROWS:]], axis=0)
    return attended, peak + jnp.log(total)


def chip_at(group, order, step):
    return sum(jnp.where(step == j, group.chip(*place), 0) for j, place in enumerate(order))


def open_kernel(
    hidden_ref, cot_ref, memory_ref, counts_ref, gain_ref, shift_ref, w_ref, b_query_ref, b_value_ref,
    q_ref, k_ref, v_ref, mk_ref, mv_ref, mem_normed_ref, mem_bias_ref, tail_bias_ref, w_t_ref,
    normed_out, cot_out,
    rows_buf, cot_buf, flat_w, mem_wide, send, recv, cot_send, cot_recv, out_sem,
):
    head, seq = Group("head"), Group("seq")
    gather = Gather(head, rows_buf, send, recv, 112)
    cot_gather = Gather(seq, cot_buf, cot_send, cot_recv, 112)
    own, cot_own = head.block(0, 0), seq.block(0, 0)

    def norm_rows(rows):
        normal, _ = normal_of(hidden_ref[rows].astype(WIDE))
        rows_buf[own, rows] = (normal * gain_ref[...] + shift_ref[...]).astype(LOW)
        cot_buf[cot_own, rows] = cot_ref[rows]

    row_tiles(BLOCK, norm_rows, 32)
    greet_all(head, seq)
    gather.arrive(0, 0)
    cot_gather.arrive(0, 0)
    width = q_ref.shape[1]
    slots = memory_ref.shape[0]
    for i in range(3):
        flat_w[:, i * width : (i + 1) * width] = w_ref[i]
    copies = []

    def project(*place):
        gather.sibling(*place)
        chip = head.chip(*place)
        out = pltpu.make_async_copy(
            rows_buf.at[pl.ds(chip * 2, 2)], normed_out.at[pl.ds(chip * 2, 2)], out_sem.at[len(copies)]
        )
        out.start()
        copies.append(out)
        rows = rows_buf[pl.ds(chip * 2, 2)].reshape(2 * BLOCK, rows_buf.shape[2])
        at = pl.ds(pl.multiple_of(chip * 2 * BLOCK, 2 * BLOCK), 2 * BLOCK)
        all_parts = dot(rows, flat_w[...])
        q_ref[at, :] = (all_parts[:, :width] + b_query_ref[...]).astype(LOW)
        k_ref[at, :] = all_parts[:, width : 2 * width].astype(LOW)
        v_ref[at, :] = (all_parts[:, 2 * width :] + b_value_ref[...]).astype(LOW)

    def keep_cot(*place):
        block = seq.block(*place)
        out = pltpu.make_async_copy(cot_buf.at[block], cot_out.at[block], out_sem.at[len(copies)])
        out.start()
        copies.append(out)

    def side_work():
        mem_wide[...] = jnp.zeros_like(mem_wide)
        mem_wide[:slots, :] = memory_ref[...].astype(WIDE)

        def norm_memory(rows):
            normal, _ = normal_of(mem_wide[rows])
            mem_normed_ref[rows] = (normal * gain_ref[...] + shift_ref[...]).astype(LOW)

        row_tiles(MEMROWS, norm_memory, 32)
        mem = dot(mem_normed_ref[...], flat_w[:, width:])
        mk_ref[...] = mem[:, :width].astype(LOW)
        mv_ref[...] = (mem[:, width:] + b_value_ref[...]).astype(LOW)
        slot = lax.broadcasted_iota(jnp.int32, mem_bias_ref.shape, 0)
        mem_bias_ref[...] = jnp.where(slot < counts_ref[0, 0], 0.0, NEGATIVE)
        tail = slots - KROWS + lax.broadcasted_iota(jnp.int32, tail_bias_ref.shape, 0)
        tail_bias_ref[...] = jnp.where((tail < 0) | (tail < counts_ref[0, 1]), 0.0, NEGATIVE)
        for i in range(3):
            transpose_into(w_t_ref.at[pl.ds(i * width, width)], w_ref.at[i])

    side_work()
    project(0, 0)
    keep_cot(0, 0)
    gather.arrive(-1, 0)
    gather.arrive(1, 0)
    cot_gather.arrive(-1, 0)
    cot_gather.arrive(1, 0)
    gather.arrive(0, 1)
    cot_gather.arrive(0, 1)
    project(-1, 0)
    project(1, 0)
    gather.arrive(2, 0)
    cot_gather.arrive(2, 0)
    project(0, 1)
    gather.arrive(-1, 1)
    gather.arrive(1, 1)
    cot_gather.arrive(-1, 1)
    cot_gather.arrive(1, 1)
    project(2, 0)
    project(-1, 1)
    project(1, 1)
    gather.arrive(2, 1)
    cot_gather.arrive(2, 1)
    project(2, 1)
    for place in NEAR_FIRST[1:]:
        keep_cot(*place)
    gather.drain()
    cot_gather.drain()
    for out in copies:
        out.wait()


def open_layer(hidden, cot, memory, counts, gain, shift, w, b_query, b_value):
    rows, model = hidden.shape
    width = w.shape[2]
    part = jax.ShapeDtypeStruct((16 * rows, width), LOW)
    mem_part = jax.ShapeDtypeStruct((MEMROWS, width), LOW)
    sems = [pltpu.SemaphoreType.DMA((Gather.COPIES,))] * 4
    smem = pl.BlockSpec(memory_space=pltpu.SMEM)
    return pl.pallas_call(
        open_kernel,
        out_shape=(
            part, part, part, mem_part, mem_part,
            jax.ShapeDtypeStruct((MEMROWS, model), LOW),
            jax.ShapeDtypeStruct((MEMROWS, 1), WIDE),
            jax.ShapeDtypeStruct((KROWS, 1), WIDE),
            jax.ShapeDtypeStruct((3 * width, model), LOW),
            jax.ShapeDtypeStruct((16, rows, model), LOW),
            jax.ShapeDtypeStruct((8, rows, model), LOW),
        ),
        in_specs=[VMEM] * 3 + [smem] + [VMEM] * 5,
        out_specs=(VMEM,) * 9 + (ANY,) * 2,
        scratch_shapes=[
            pltpu.VMEM((16, rows, model), LOW),
            pltpu.VMEM((8, rows, model), LOW),
            pltpu.VMEM((model, 3 * width), LOW),
            pltpu.VMEM((MEMROWS, model), WIDE),
        ] + sems + [pltpu.SemaphoreType.DMA((16,))],
        compiler_params=pltpu.CompilerParams(
            collective_id=0, has_side_effects=True, vmem_limit_bytes=VMEM_LIMIT
        ),
        name="open_layer",
    )(hidden, cot, memory, counts, gain, shift, w, b_query, b_value)


def attend_kernel(
    q_ref, k_ref, v_ref, mk_ref, mv_ref, mem_bias_ref, tail_bias_ref, wo_ref,
    hidden_ref, b_out_ref, gain_ref, shift_ref, cot_hbm, w_down_hbm, w_up_hbm,
    attn_t_ref, lse_ref, resid_ref, second_ref, back_ref, w_up_t_ref,
    vt_ref, mvt_ref, attn_ref, cot_buf, wd_ref, wu_ref, load_sem,
    total, stage, land, send, recv, near_stage, near_land,
):
    head = Group("head")
    reduce = Reduce(head, total, stage, land, send, recv, 96, (near_stage, near_land), resid_ref)
    loads = [
        pltpu.make_async_copy(src, dst, load_sem.at[i])
        for i, (src, dst) in enumerate(
            ((cot_hbm, cot_buf), (w_down_hbm, wd_ref), (w_up_hbm, wu_ref))
        )
    ]
    for load in loads:
        load.start()
    transpose_into(vt_ref, v_ref)
    transpose_into(mvt_ref, mv_ref)
    greet_all(head)

    def step(k, carry):
        chip = chip_at(head, FAR_FIRST, k)
        start = pl.multiple_of(chip * QROWS, QROWS)
        attended, lse = attend_chunk(
            chip, q_ref, k_ref, vt_ref, mk_ref, mvt_ref, mem_bias_ref[...], tail_bias_ref[...]
        )
        attn_t_ref[:, pl.ds(start, QROWS)] = attended.astype(LOW)
        attn_ref[...] = attended.T.astype(LOW)
        lse_ref[chip] = lse
        mine = attn_ref[pl.ds(pl.multiple_of(head.core * BLOCK, BLOCK), BLOCK), :]
        other = attn_ref[pl.ds(pl.multiple_of((1 - head.core) * BLOCK, BLOCK), BLOCK), :]
        for at in range(0, total.shape[2], 512):
            near_stage[k, :, at : at + 512] = dot(other, wo_ref[:, at : at + 512]).astype(LOW)
        reduce.near_copy(k).start()
        for at in range(0, total.shape[2], 512):
            total[k, :, at : at + 512] = dot(mine, wo_ref[:, at : at + 512])
        for j, place in enumerate(FAR_FIRST[:-1]):
            @pl.when(k == j + 1)
            def _():
                reduce.settle(*place)
        return carry

    lax.fori_loop(0, 8, step, 0)
    units = wd_ref.shape[0]
    model = hidden_ref.shape[1]
    for load in loads:
        load.wait()

    def cot_times(i, carry):
        pairs = cot_buf[pl.ds(2 * i, 2)].reshape(2 * BLOCK, model)
        for at in range(0, units, 256):
            part = dot_nt(pairs, wd_ref[at : at + 256, :]).astype(LOW)
            back_ref[pl.ds(2 * i, 2), :, at : at + 256] = part.reshape(2, BLOCK, 256)
        return carry

    lax.fori_loop(0, 4, cot_times, 0)
    transpose_into(w_up_t_ref, wu_ref)
    reduce.settle(0, 0)

    def finish(rows):
        resid = hidden_ref[rows].astype(WIDE) + resid_ref[rows] + b_out_ref[...]
        resid_ref[rows] = resid
        normal, _ = normal_of(resid)
        second_ref[rows] = (normal * gain_ref[...] + shift_ref[...]).astype(LOW)

    row_tiles(BLOCK, finish, 32)
    reduce.drain()


def attend_layer(
    q, k, v, mk, mv, mem_bias, tail_bias, wo, hidden, b_out, gain, shift, cot_all, w_down, w_up
):
    length, width = q.shape
    rows, model = hidden.shape
    units = w_up.shape[1]
    return pl.pallas_call(
        attend_kernel,
        out_shape=(
            jax.ShapeDtypeStruct((width, length), LOW),
            jax.ShapeDtypeStruct((length // QROWS, 1, 2 * QROWS), WIDE),
            jax.ShapeDtypeStruct((rows, model), WIDE),
            jax.ShapeDtypeStruct((rows, model), LOW),
            jax.ShapeDtypeStruct((8, rows, units), LOW),
            jax.ShapeDtypeStruct((units, model), LOW),
        ),
        in_specs=[VMEM] * 12 + [ANY] * 3,
        out_specs=(VMEM,) * 6,
        scratch_shapes=[
            pltpu.VMEM((width, length), LOW),
            pltpu.VMEM((width, MEMROWS), LOW),
            pltpu.VMEM((QROWS, width), LOW),
            pltpu.VMEM((8, rows, model), LOW),
            pltpu.VMEM((units, model), LOW),
            pltpu.VMEM((model, units), LOW),
            pltpu.SemaphoreType.DMA((3,)),
        ] + Reduce.scratch(model, True, True),
        compiler_params=pltpu.CompilerParams(
            collective_id=1, has_side_effects=True, vmem_limit_bytes=VMEM_LIMIT
        ),
        name="attend_layer",
    )(
        q, k, v, mk, mv, mem_bias, tail_bias, wo, hidden, b_out, gain, shift,
        cot_all, w_down, w_up,
    )


def gelu_parts(u):
    square = u * u
    t = jnp.tanh(0.7978845608 * (u + 0.044715 * (square * u)))
    half = 0.5 * (1.0 + t)
    slope = half + 0.5 * u * (1.0 - t * t) * (0.7978845608 * (1.0 + 0.134145 * square))
    return u * half, slope


def fold_rows(values):
    return jnp.sum(values.reshape(values.shape[0] // 8, 8, values.shape[1]), axis=0)


def feed_kernel(
    second_ref, w_up_hbm, w_up_t_hbm, back_hbm, w_down_hbm, cot_hbm, up_bias_ref, resid_ref, gain_ref,
    cot_ref,
    grad_resid_ref, sums_ref, branch_hbm, grad_w_ref, grad_b_up_ref,
    rows_buf, wu_ref, wut_ref, wd_ref, cot_buf, act_ref, back_ref, pre_ref, fold_ref, sum_fold, branch_buf,
    load_sem, branch_sem, send, recv,
    total, land, rsend, rrecv,
    w_total, w_land, w_send, w_recv, w_near_stage, w_near_land,
):
    head, seq = Group("head"), Group("seq")
    gather = Gather(seq, rows_buf, send, recv, 64)
    reduce = Reduce(seq, total, None, land, rsend, rrecv, 112, None, grad_resid_ref)
    w_reduce = Reduce(head, w_total, None, w_land, w_send, w_recv, 96, (w_near_stage, w_near_land), grad_w_ref)
    loads = [
        pltpu.make_async_copy(src, dst, load_sem.at[i])
        for i, (src, dst) in enumerate(
            (
                (w_up_hbm, wu_ref), (back_hbm, back_ref), (w_up_t_hbm, wut_ref),
                (cot_hbm, cot_buf), (w_down_hbm, wd_ref),
            )
        )
    ]
    for load in loads:
        load.start()
    own = seq.block(0, 0)
    rows_buf[own] = second_ref[...]
    fold_ref[...] = jnp.zeros_like(fold_ref)
    greet_all(head, seq)
    gather.arrive(0, 0)
    for load in loads[:3]:
        load.wait()
    units = act_ref.shape[2]
    model = rows_buf.shape[2]
    bias_at = pl.ds(pl.multiple_of(own * units, units), units)

    def feed(*place):
        block = seq.block(*place)
        pre_ref[...] = dot(rows_buf[block], wu_ref[...]) + up_bias_ref[:, bias_at]

        def bend(rows):
            activated, slope = gelu_parts(pre_ref[rows])
            grad_pre = back_ref[block, rows].astype(WIDE) * slope
            act_ref[block, rows] = activated.astype(LOW)
            back_ref[block, rows] = grad_pre.astype(LOW)
            fold_ref[...] += fold_rows(grad_pre)

        row_tiles(BLOCK, bend)
        k = FAR_FIRST.index(place)
        for at in range(0, model, 512):
            total[k, :, at : at + 512] = dot(back_ref[block], wut_ref[:, at : at + 512]).astype(LOW)

    feed(0, 0)
    gather.arrive(-1, 0)
    gather.arrive(1, 0)
    gather.arrive(0, 1)
    feed(-1, 0)
    gather.arrive(2, 0)
    feed(1, 0)
    gather.arrive(-1, 1)
    gather.arrive(1, 1)
    feed(0, 1)
    feed(2, 0)
    feed(-1, 1)
    feed(1, 1)
    gather.arrive(2, 1)
    feed(2, 1)
    reduce.settle(2, 1)
    reduce.settle(2, 0)
    for load in loads[3:]:
        load.wait()
    grad_b_up_ref[...] = jnp.sum(fold_ref[...], axis=0, keepdims=True)

    def weights(k, carry):
        chip = chip_at(head, FAR_FIRST, k)

        def part(core):
            at = pl.ds(pl.multiple_of(chip * 2 * BLOCK + core * BLOCK, BLOCK), BLOCK)
            length = 8 * BLOCK
            up = dot_tn(
                rows_buf[:, :, at].reshape(length, BLOCK), back_ref[...].reshape(length, units)
            )
            down = dot_tn(
                cot_buf[:, :, at].reshape(length, BLOCK), act_ref[...].reshape(length, units)
            )
            return up.astype(LOW), down.astype(LOW)

        w_near_stage[k, :, :units], w_near_stage[k, :, units:] = part(1 - head.core)
        w_reduce.near_copy(k).start()
        w_total[k, :, :units], w_total[k, :, units:] = part(head.core)
        for j, place in enumerate(FAR_FIRST[:6]):
            @pl.when(k == j + 1)
            def _():
                w_reduce.settle(*place)

        @pl.when(k == 2)
        def _():
            reduce.settle(1, 1)
            reduce.settle(-1, 1)

        @pl.when(k == 5)
        def _():
            reduce.settle(1, 0)
            reduce.settle(-1, 0)

        return carry

    lax.fori_loop(0, 8, weights, 0)
    branch_copies = []

    def branch(i):
        slot = i % 2
        if i >= 2:
            branch_copies[i - 2].wait()
        for at in range(0, model, 512):
            branch_buf[slot, :, at : at + 512] = dot(act_ref[i], wd_ref[:, at : at + 512]).astype(LOW)
        copy = pltpu.make_async_copy(branch_buf.at[slot], branch_hbm.at[i], branch_sem.at[i])
        copy.start()
        branch_copies.append(copy)

    for i in range(4):
        branch(i)
    reduce.settle(0, 1)
    w_reduce.settle(0, 1)
    for i in range(4, 8):
        branch(i)
    reduce.settle(0, 0)
    sum_fold[...] = jnp.zeros_like(sum_fold)

    def back(rows):
        normal, rstd = normal_of(resid_ref[rows])
        incoming = grad_resid_ref[rows]
        scaled = incoming * gain_ref[...]
        inner = jnp.mean(scaled, axis=-1, keepdims=True)
        along = jnp.mean(scaled * normal, axis=-1, keepdims=True)
        cot = cot_ref[rows].astype(WIDE)
        grad = cot + rstd * (scaled - inner - normal * along)
        grad_resid_ref[rows] = grad
        for i, value in enumerate((grad, incoming * normal, incoming, cot)):
            sum_fold[i] += fold_rows(value)

    row_tiles(BLOCK, back)
    sums_ref[...] = jnp.sum(sum_fold[...], axis=1)
    w_reduce.settle(0, 0)
    for copy in branch_copies[-2:]:
        copy.wait()
    gather.drain()
    reduce.drain()
    w_reduce.drain()


def feed_layer(second, w_up, w_up_t, back, w_down, cot_all, up_bias, resid, gain, cot):
    rows, model = second.shape
    units = w_up.shape[1]
    gather_sems = [pltpu.SemaphoreType.DMA((Gather.COPIES,))] * 2
    return pl.pallas_call(
        feed_kernel,
        out_shape=(
            jax.ShapeDtypeStruct((rows, model), WIDE),
            jax.ShapeDtypeStruct((4, model), WIDE),
            jax.ShapeDtypeStruct((8, rows, model), LOW),
            jax.ShapeDtypeStruct((rows, 2 * units), WIDE),
            jax.ShapeDtypeStruct((1, units), WIDE),
        ),
        in_specs=[VMEM] + [ANY] * 5 + [VMEM] * 4,
        out_specs=(VMEM, VMEM, ANY, VMEM, VMEM),
        scratch_shapes=[
            pltpu.VMEM((8, rows, model), LOW),
            pltpu.VMEM((model, units), LOW),
            pltpu.VMEM((units, model), LOW),
            pltpu.VMEM((units, model), LOW),
            pltpu.VMEM((8, rows, model), LOW),
            pltpu.VMEM((8, rows, units), LOW),
            pltpu.VMEM((8, rows, units), LOW),
            pltpu.VMEM((rows, units), WIDE),
            pltpu.VMEM((8, units), WIDE),
            pltpu.VMEM((4, 8, model), WIDE),
            pltpu.VMEM((2, rows, model), LOW),
            pltpu.SemaphoreType.DMA((5,)),
            pltpu.SemaphoreType.DMA((8,)),
        ] + gather_sems + Reduce.scratch(model, False, False) + Reduce.scratch(2 * units, False, True),
        compiler_params=pltpu.CompilerParams(
            collective_id=2, has_side_effects=True, vmem_limit_bytes=VMEM_LIMIT
        ),
        name="feed_layer",
    )(second, w_up, w_up_t, back, w_down, cot_all, up_bias, resid, gain, cot)


def attend_back_chunk(
    chunk, q_ref, k_ref, kt_ref, v_ref, mk_ref, mkt_ref, mv_ref, mem_bias, tail_bias,
    attn_t_ref, lse_ref, grad_rows, dk_ref, dv_ref, dmk_ref, dmv_ref,
):
    start = pl.multiple_of(chunk * QROWS, QROWS)
    q2 = stack_heads(q_ref[pl.ds(start, QROWS), :] * HDIM ** (-0.5))
    g2 = stack_heads(grad_rows)
    product = grad_rows.astype(WIDE).T * attn_t_ref[:, pl.ds(start, QROWS)].astype(WIDE)
    inner = jnp.concatenate(
        [
            jnp.sum(product[:HDIM], axis=0, keepdims=True),
            jnp.sum(product[HDIM:], axis=0, keepdims=True),
        ],
        axis=1,
    )
    lse = lse_ref[chunk]

    def piece(scores, values, keys_t):
        probs = jnp.exp(scores - lse)
        grad_probs = dot_nt(values, g2)
        grad_scores = (probs * (grad_probs - inner)).astype(LOW)
        return (
            dot(probs.astype(LOW), g2),
            dot(grad_scores, q2),
            dot(keys_t[:HDIM], grad_scores[:, :QROWS]),
            dot(keys_t[HDIM:], grad_scores[:, QROWS:]),
        )

    dv, dk, first, second = piece(
        dot_nt(mk_ref[...], q2) + mem_bias, mv_ref[...], mkt_ref[...]
    )
    dmv_ref[...] += dv
    dmk_ref[...] += dk

    def block_step(block, bias, carry):
        first, second = carry
        at = pl.multiple_of(block * KROWS, KROWS)
        scores = dot_nt(k_ref[pl.ds(at, KROWS), :], q2)
        if bias is not None:
            scores = scores + bias
        dv, dk, add_first, add_second = piece(
            scores, v_ref[pl.ds(at, KROWS), :], kt_ref[:, pl.ds(at, KROWS)]
        )
        dv_ref[pl.ds(at, KROWS), :] += dv
        dk_ref[pl.ds(at, KROWS), :] += dk
        return first + add_first, second + add_second

    full = chunk * QROWS // KROWS
    carry = lax.fori_loop(0, full, lambda b, c: block_step(b, None, c), (first, second))
    first, second = block_step(full, causal_bias(chunk, full, tail_bias), carry)
    return jnp.concatenate([first, second], axis=0) * HDIM ** (-0.5)


def grad_kernel(
    grad_resid_ref, resid_ref, b_down_ref, branch_hbm, wo_ref,
    q_ref, k_ref, v_ref, mk_ref, mv_ref, mem_bias_ref, tail_bias_ref, attn_t_ref, lse_ref,
    out_ref, own_ref, own_t_ref, mem_ref, mem_t_ref, grad_wo_ref, sums_ref,
    rows_buf, kt_ref, mkt_ref, dk_ref, dv_ref, dmk_ref, dmv_ref, wo_sum, branch_sum, fold_ref,
    load_sem, send, recv, total, land, rsend, rrecv,
):
    head, seq = Group("head"), Group("seq")
    gather = Gather(head, rows_buf, send, recv, 112)
    reduce = Reduce(seq, total, None, land, rsend, rrecv, 128, None, branch_sum)
    loads = [
        pltpu.make_async_copy(branch_hbm.at[seq.block(*place)], total.at[k], load_sem.at[k])
        for k, place in enumerate(FAR_FIRST)
    ]
    for load in loads:
        load.start()
    own = head.block(0, 0)
    rows_buf[own] = grad_resid_ref[...].astype(LOW)
    greet_all(head, seq)
    gather.arrive(0, 0)
    loads[0].wait()
    reduce.settle(2, 1)
    loads[1].wait()
    reduce.settle(2, 0)
    transpose_into(kt_ref, k_ref)
    transpose_into(mkt_ref, mk_ref)
    for ref in (dk_ref, dv_ref, dmk_ref, dmv_ref, wo_sum, fold_ref):
        ref[...] = jnp.zeros_like(ref)
    width, model = wo_ref.shape
    for load in loads[2:]:
        load.wait()

    def step(k, carry):
        @pl.when(k == 0)
        def _():
            gather.sibling(0, 0)

        @pl.when(k == 1)
        def _():
            gather.arrive(-1, 0)
            gather.arrive(1, 0)
            reduce.settle(1, 1)
            reduce.settle(-1, 1)
            gather.arrive(0, 1)
            gather.sibling(-1, 0)

        @pl.when(k == 2)
        def _():
            reduce.settle(1, 0)
            reduce.settle(-1, 0)
            gather.sibling(1, 0)

        @pl.when(k == 3)
        def _():
            gather.arrive(2, 0)
            gather.sibling(0, 1)

        @pl.when(k == 4)
        def _():
            gather.arrive(-1, 1)
            gather.arrive(1, 1)
            gather.sibling(2, 0)

        @pl.when(k == 5)
        def _():
            reduce.settle(0, 1)
            gather.sibling(-1, 1)

        @pl.when(k == 6)
        def _():
            gather.arrive(2, 1)
            gather.sibling(1, 1)

        @pl.when(k == 7)
        def _():
            gather.sibling(2, 1)

        chip = chip_at(head, NEAR_FIRST, k)
        at = pl.ds(pl.multiple_of(chip * QROWS, QROWS), QROWS)
        rows = rows_buf[pl.ds(chip * 2, 2)].reshape(QROWS, model)
        grad_rows = dot_nt(rows, wo_ref[...]).astype(LOW)
        wo_sum[...] += dot(attn_t_ref[:, at], rows)
        dq = attend_back_chunk(
            chip, q_ref, k_ref, kt_ref, v_ref, mk_ref, mkt_ref, mv_ref,
            mem_bias_ref[...], tail_bias_ref[...], attn_t_ref, lse_ref,
            grad_rows, dk_ref, dv_ref, dmk_ref, dmv_ref,
        ).astype(LOW)
        own_t_ref[:width, at] = dq
        own_ref[at, :width] = dq.T
        return carry

    lax.fori_loop(0, 8, step, 0)

    def finish_keys(i, carry):
        at = pl.ds(pl.multiple_of(i * 256, 256), 256)
        dk = dk_ref[at, :].astype(LOW)
        dv = dv_ref[at, :].astype(LOW)
        own_ref[at, width : 2 * width] = dk
        own_ref[at, 2 * width :] = dv
        own_t_ref[width : 2 * width, at] = dk.T
        own_t_ref[2 * width :, at] = dv.T
        fold_ref[...] += fold_rows(own_ref[at, :].astype(WIDE))
        return carry

    lax.fori_loop(0, q_ref.shape[0] // 256, finish_keys, 0)
    for i, ref in enumerate((dmk_ref, dmv_ref)):
        low = ref[...].astype(LOW)
        mem_ref[:, i * width : (i + 1) * width] = low
        mem_t_ref[i * width : (i + 1) * width, :] = low.T
    fold_ref[:, width:] += fold_rows(mem_ref[...].astype(WIDE))
    sums_ref[...] = jnp.sum(fold_ref[...], axis=0, keepdims=True)
    grad_wo_ref[...] = wo_sum[...].astype(LOW)
    reduce.settle(0, 0)

    def finish(rows):
        out_ref[rows] = (resid_ref[rows] + branch_sum[rows] + b_down_ref[...]).astype(LOW)

    row_tiles(BLOCK, finish)
    gather.drain()
    reduce.drain()


def grad_layer(
    grad_resid, resid, b_down, branch, wo, q, k, v, mk, mv, mem_bias, tail_bias, attn_t, lse,
):
    rows, model = grad_resid.shape
    length, width = q.shape
    return pl.pallas_call(
        grad_kernel,
        out_shape=(
            jax.ShapeDtypeStruct((rows, model), LOW),
            jax.ShapeDtypeStruct((length, 3 * width), LOW),
            jax.ShapeDtypeStruct((3 * width, length), LOW),
            jax.ShapeDtypeStruct((MEMROWS, 2 * width), LOW),
            jax.ShapeDtypeStruct((2 * width, MEMROWS), LOW),
            jax.ShapeDtypeStruct((width, model), LOW),
            jax.ShapeDtypeStruct((1, 3 * width), WIDE),
        ),
        in_specs=[VMEM] * 3 + [ANY] + [VMEM] * 10,
        out_specs=(VMEM,) * 7,
        scratch_shapes=[
            pltpu.VMEM((16, rows, model), LOW),
            pltpu.VMEM((width, length), LOW),
            pltpu.VMEM((width, MEMROWS), LOW),
            pltpu.VMEM((length, width), WIDE),
            pltpu.VMEM((length, width), WIDE),
            pltpu.VMEM((MEMROWS, width), WIDE),
            pltpu.VMEM((MEMROWS, width), WIDE),
            pltpu.VMEM((width, model), WIDE),
            pltpu.VMEM((rows, model), WIDE),
            pltpu.VMEM((8, 3 * width), WIDE),
            pltpu.SemaphoreType.DMA((8,)),
        ] + [pltpu.SemaphoreType.DMA((Gather.COPIES,))] * 2 + Reduce.scratch(model, False, False),
        compiler_params=pltpu.CompilerParams(
            collective_id=3, has_side_effects=True, vmem_limit_bytes=VMEM_LIMIT
        ),
        name="grad_layer",
    )(
        grad_resid, resid, b_down, branch, wo, q, k, v, mk, mv, mem_bias, tail_bias, attn_t, lse,
    )


SUM_ROWS = 16


def close_kernel(
    own_ref, own_t_ref, mem_ref, mem_t_ref, grad_wo_ref, mem_normed_ref, normed_hbm, w_t_ref,
    gain_ref, shift_ref, bias_sums_ref, feed_sums_ref, b_up_ref,
    grad_normed_ref, grad_w_ref, small_ref,
    rows_buf, mem_pad, norm_sums, pay_ref, pay_land, seq_land,
    pay_send, pay_recv, seq_send, seq_recv, all_send, all_recv, load_sem,
    total, stage, land, send, recv, near_stage, near_land,
    w_total, w_stage, w_land, w_send, w_recv, g_send, g_recv,
):
    head, seq = Group("head"), Group("seq")
    reduce = Reduce(head, total, stage, land, send, recv, 96, (near_stage, near_land), grad_normed_ref)
    w_reduce = Reduce(seq, w_total, w_stage, w_land, w_send, w_recv, 128, None, w_total.at[7])
    gather = Gather(seq, grad_w_ref, g_send, g_recv, 112)
    pay = Spread(head, pay_send, pay_recv)
    across = Spread(seq, seq_send, seq_recv)
    back = Spread(head, all_send, all_recv)
    load = pltpu.make_async_copy(normed_hbm, rows_buf, load_sem)
    load.start()
    width = grad_wo_ref.shape[0]
    model = rows_buf.shape[2]
    length = own_ref.shape[0]
    wide = model // 2
    share = model // head.size
    mem_pad[...] = jnp.zeros_like(mem_pad)
    mem_pad[pl.ds(width, 2 * width), :] = mem_t_ref[...]
    norm_sums[...] = jnp.zeros_like(norm_sums)
    greet_everyone(head, seq)

    def chunk(k):
        chip = head.chip(*FAR_FIRST[k])

        def part(core):
            at = pl.ds(pl.multiple_of(chip * QROWS + core * BLOCK, BLOCK), BLOCK)
            return own_ref[at, :]

        mine, other = part(head.core), part(1 - head.core)
        for at in range(0, model, 512):
            near_stage[k, :, at : at + 512] = dot(other, w_t_ref[:, at : at + 512]).astype(LOW)
        reduce.near_copy(k).start()
        for at in range(0, model, 512):
            total[k, :, at : at + 512] = dot(mine, w_t_ref[:, at : at + 512])

    def weights(k, carry):
        target = chip_at(seq, FAR_FIRST, k)
        part, side = target // 2, target % 2
        columns = pl.ds(pl.multiple_of(side * wide, wide), wide)

        @pl.when(part < 3)
        def _():
            at = pl.ds(pl.multiple_of(part * width, width), width)
            term = dot(
                own_t_ref[at, :], rows_buf[:, :, columns].reshape(length, wide)
            ) + dot(mem_pad[at, :], mem_normed_ref[:, columns])
            w_total[k] = term
            flat = w_t_ref[at, columns].astype(WIDE)
            norm_sums[0:1, columns] += jnp.sum(flat * term, axis=0, keepdims=True)

        @pl.when(part == 3)
        def _():
            w_total[k] = grad_wo_ref[:, columns].astype(WIDE)

        return carry

    def shift_sums():
        sums = bias_sums_ref[...]
        high = sums.astype(LOW)
        rest = (sums - high.astype(WIDE)).astype(LOW)
        pair = jnp.concatenate([high, rest, jnp.zeros((14, sums.shape[1]), LOW)], axis=0)
        both = dot(pair, w_t_ref[...])
        norm_sums[1:2, :] = both[0:1] + both[1:2]

    def pay_part(i):
        return pay_ref.at[:, pl.ds(pl.multiple_of(i * share, share), share)]

    def pay_start():
        pay_ref[:MEMROWS, :] = dot(mem_ref[...], w_t_ref[width:, :]).astype(LOW)
        at_gain = norm_sums[0:1, :] - shift_ref[...] * norm_sums[1:2, :]
        rows = [at_gain / gain_ref[...], norm_sums[1:2, :], feed_sums_ref[...]]
        units = b_up_ref.shape[1]
        per_row = model // units
        for r in range(8 // per_row):
            row = [jnp.where(seq.me == r * per_row + c, b_up_ref[...], 0.0) for c in range(per_row)]
            rows.append(jnp.concatenate(row, axis=1))
        rows.append(jnp.zeros((SUM_ROWS - 6 - 8 // per_row, model), WIDE))
        pay_ref[MEMROWS:, :] = jnp.concatenate(rows, axis=0).astype(LOW)
        pay_land[head.me] = pay_part(head.me)[...]
        pay.start(pay_part, pay_land)

    def pay_sum():
        pay.wait(pay_land)
        sums = pay_land[0].astype(WIDE)
        for i in range(1, 16):
            sums += pay_land[i].astype(WIDE)
        small_ref[head.me, :MEMROWS, :] = sums[:MEMROWS].astype(LOW)
        used = 6 + 8 * b_up_ref.shape[1] // model
        rows = [sums[MEMROWS : MEMROWS + used]]
        rows += [bias_sums_ref[:, i * width : (i + 1) * width] for i in range(3)]
        rows.append(jnp.zeros((SUM_ROWS - 3 - used, share), WIDE))
        seq_land[seq.me] = jnp.concatenate(rows, axis=0).astype(LOW)
        across.start(lambda i: seq_land.at[seq.me], seq_land)

    def pay_back():
        across.wait(seq_land)
        sums = seq_land[0].astype(WIDE)
        for i in range(1, 8):
            sums += seq_land[i].astype(WIDE)
        small_ref[head.me, MEMROWS:, :] = sums.astype(LOW)
        back.start(lambda i: small_ref.at[head.me], small_ref)

    chunk(0)
    chunk(1)
    reduce.settle(2, 1)
    chunk(2)
    reduce.settle(2, 0)
    load.wait()
    lax.fori_loop(0, 2, weights, 0)
    w_reduce.settle(2, 1)
    w_reduce.settle(2, 0)
    lax.fori_loop(2, 8, weights, 0)
    shift_sums()
    chunk(3)
    reduce.settle(1, 1)
    w_reduce.settle(1, 1)
    w_reduce.settle(-1, 1)
    chunk(4)
    reduce.settle(-1, 1)
    pay_start()
    w_reduce.settle(1, 0)
    w_reduce.settle(-1, 0)
    chunk(5)
    reduce.settle(1, 0)
    chunk(6)
    reduce.settle(-1, 0)
    chunk(7)
    w_reduce.settle(0, 1)
    pay_sum()
    reduce.settle(0, 1)
    w_reduce.settle(0, 0)
    grad_w_ref[seq.me] = w_total[7].astype(LOW)
    gather.arrive(0, 0)
    pay_back()
    gather.arrive(-1, 0)
    gather.arrive(1, 0)
    gather.arrive(0, 1)
    gather.arrive(2, 0)
    gather.arrive(-1, 1)
    gather.arrive(1, 1)
    reduce.settle(0, 0)
    gather.arrive(2, 1)
    back.wait(small_ref)
    pay.drain(pay_part, pay_land)
    across.drain(lambda i: seq_land.at[seq.me], seq_land)
    back.drain(lambda i: small_ref.at[head.me], small_ref)
    gather.drain()
    w_reduce.drain()
    reduce.drain()


def close_layer(
    own, own_t, mem, mem_t, grad_wo, mem_normed, normed_all, w_t, gain, shift, bias_sums,
    feed_sums, b_up,
):
    rows, model = normed_all.shape[1:]
    width = grad_wo.shape[0]
    sems = [pltpu.SemaphoreType.DMA((Gather.COPIES,))] * 2
    pay_rows = MEMROWS + SUM_ROWS
    return pl.pallas_call(
        close_kernel,
        out_shape=(
            jax.ShapeDtypeStruct((rows, model), WIDE),
            jax.ShapeDtypeStruct((8, width, model // 2), LOW),
            jax.ShapeDtypeStruct((16, pay_rows, model // 16), LOW),
        ),
        in_specs=[VMEM] * 6 + [ANY] + [VMEM] * 6,
        out_specs=(VMEM,) * 3,
        scratch_shapes=[
            pltpu.VMEM((16, rows, model), LOW),
            pltpu.VMEM((3 * width, MEMROWS), LOW),
            pltpu.VMEM((8, model), WIDE),
            pltpu.VMEM((pay_rows, model), LOW),
            pltpu.VMEM((16, pay_rows, model // 16), LOW),
            pltpu.VMEM((8, SUM_ROWS, model // 16), LOW),
            pltpu.SemaphoreType.DMA((16,)),
            pltpu.SemaphoreType.DMA((16,)),
            pltpu.SemaphoreType.DMA((8,)),
            pltpu.SemaphoreType.DMA((8,)),
            pltpu.SemaphoreType.DMA((16,)),
            pltpu.SemaphoreType.DMA((16,)),
            pltpu.SemaphoreType.DMA,
        ] + Reduce.scratch(model, True, True) + Reduce.scratch(model // 2, True, False) + sems,
        compiler_params=pltpu.CompilerParams(
            collective_id=4, has_side_effects=True, vmem_limit_bytes=VMEM_LIMIT
        ),
        name="close_layer",
    )(
        own, own_t, mem, mem_t, grad_wo, mem_normed, normed_all, w_t, gain, shift, bias_sums,
        feed_sums, b_up,
    )


def finish_kernel(
    grad_normed_ref, hidden_ref, grad_resid_ref, gain_ref, grad_w_ref, small_ref, memory_ref,
    feed_w_ref, output_ref,
    out_ref, grad_hidden_ref, grad_memory_ref, grad_qkv_ref, b_query_ref, b_value_ref, grad_wo_ref,
    b_out_ref, gain_one_ref, shift_one_ref, gain_two_ref, shift_two_ref,
    w_up_ref, b_up_ref, w_down_ref, b_down_ref,
    mem_wide, spread_ref,
):
    share = small_ref.shape[2]
    for i in range(small_ref.shape[0]):
        spread_ref[:, i * share : (i + 1) * share] = small_ref[i].astype(WIDE)

    def norm_back(values, incoming):
        normal, rstd = normal_of(values)
        scaled = incoming * gain_ref[...]
        inner = jnp.mean(scaled, axis=-1, keepdims=True)
        along = jnp.mean(scaled * normal, axis=-1, keepdims=True)
        return rstd * (scaled - inner - normal * along)

    def back(rows):
        grad_hidden_ref[rows] = grad_resid_ref[rows] + norm_back(
            hidden_ref[rows].astype(WIDE), grad_normed_ref[rows]
        )

    row_tiles(hidden_ref.shape[0], back, 32)
    slots = memory_ref.shape[0]
    mem_wide[...] = jnp.zeros_like(mem_wide)
    mem_wide[:slots, :] = memory_ref[...].astype(WIDE)

    def back_memory(rows):
        mem_wide[rows] = norm_back(mem_wide[rows], spread_ref[rows])

    row_tiles(MEMROWS, back_memory, 32)
    grad_memory_ref[...] = mem_wide[:slots, :]
    out_ref[...] = output_ref[...]
    wide, units = grad_w_ref.shape[2], w_up_ref.shape[1]
    for i in range(3):
        for j in range(2):
            grad_qkv_ref[i, j * wide : (j + 1) * wide, :] = grad_w_ref[2 * i + j].astype(WIDE).T
    for j in range(2):
        grad_wo_ref[:, j * wide : (j + 1) * wide] = grad_w_ref[6 + j].astype(WIDE)
    w_up_ref[...] = feed_w_ref[:, :units]
    w_down_ref[...] = feed_w_ref[:, units:].T
    sums = [spread_ref[MEMROWS + i : MEMROWS + i + 1, :] for i in range(SUM_ROWS)]
    ordered = (gain_one_ref, shift_one_ref, b_out_ref, gain_two_ref, shift_two_ref, b_down_ref)
    for ref, row in zip(ordered, sums):
        ref[...] = row
    model = b_out_ref.shape[1]
    for i in range(4):
        b_up_ref[:, i * model : (i + 1) * model] = sums[6 + i]
    mine = small_ref[lax.axis_index("head")].astype(WIDE)
    b_query_ref[...] = mine[MEMROWS + 10 : MEMROWS + 11, :]
    b_value_ref[...] = mine[MEMROWS + 12 : MEMROWS + 13, :]


def finish_layer(
    grad_normed, hidden, grad_resid, gain, grad_w, small, memory, feed_w, output
):
    rows, model = hidden.shape
    width, units = grad_w.shape[1], feed_w.shape[1] // 2
    wide = lambda *shape: jax.ShapeDtypeStruct(shape, WIDE)
    return pl.pallas_call(
        finish_kernel,
        out_shape=(
            jax.ShapeDtypeStruct((rows, model), LOW), wide(rows, model), wide(*memory.shape),
            wide(3, model, width), wide(1, width), wide(1, width), wide(width, model),
            wide(1, model), wide(1, model), wide(1, model), wide(1, model), wide(1, model),
            wide(rows, units), wide(1, 8 * units), wide(units, rows), wide(1, model),
        ),
        in_specs=[VMEM] * 9,
        out_specs=(VMEM,) * 16,
        scratch_shapes=[
            pltpu.VMEM((MEMROWS, model), WIDE),
            pltpu.VMEM((MEMROWS + SUM_ROWS, model), WIDE),
        ],
        compiler_params=pltpu.CompilerParams(vmem_limit_bytes=VMEM_LIMIT),
        name="finish_layer",
    )(grad_normed, hidden, grad_resid, gain, grad_w, small, memory, feed_w, output)


def on_device(
    hidden, memory, counts, w_qkv, b_query, b_value, output_weight, b_out,
    gain_one, shift_one, gain_two, shift_two, w_up, up_bias, w_down, b_down, cotangent,
):
    hidden, memory, cot = hidden[:, 0], memory[:, 0], cotangent[:, 0]
    model = hidden.shape[1]
    width = w_qkv.shape[2]
    w_parts = jnp.transpose(w_qkv, (1, 0, 2))
    gain_one, shift_one, gain_two, shift_two, b_out, b_down, b_query, b_value, up_bias = (
        vector[None]
        for vector in (
            gain_one, shift_one, gain_two, shift_two, b_out, b_down, b_query, b_value, up_bias
        )
    )
    q, k, v, mk, mv, mem_normed, mem_bias, tail_bias, w_t, normed_all, cot_all = open_layer(
        hidden, cot, memory, counts, gain_one, shift_one, w_parts, b_query, b_value
    )
    attn_t, lse, resid, second, back, w_up_t = attend_layer(
        q, k, v, mk, mv, mem_bias, tail_bias, output_weight, hidden, b_out, gain_two, shift_two,
        cot_all, w_down, w_up,
    )
    grad_resid, feed_sums, branch, feed_w, grad_b_up = feed_layer(
        second, w_up, w_up_t, back, w_down, cot_all, up_bias, resid, gain_two, cot
    )
    output, own, own_t, mem, mem_t, grad_wo, bias_sums = grad_layer(
        grad_resid, resid, b_down, branch, output_weight,
        q, k, v, mk, mv, mem_bias, tail_bias, attn_t, lse,
    )
    grad_normed, grad_w, small = close_layer(
        own, own_t, mem, mem_t, grad_wo, mem_normed, normed_all, w_t, gain_one, shift_one,
        bias_sums, feed_sums, grad_b_up,
    )
    outs = finish_layer(
        grad_normed, hidden, grad_resid, gain_one, grad_w, small, memory, feed_w, output
    )
    output, grad_hidden, grad_memory, grad_w_qkv, *rest = outs
    rest = [part[0] if part.shape[0] == 1 else part for part in rest]
    return (
        output[:, None],
        grad_hidden[:, None],
        grad_memory[:, None],
        jnp.transpose(grad_w_qkv, (1, 0, 2)),
        *rest,
    )


def solution(mesh):
    return jax.shard_map(
        on_device,
        mesh=mesh,
        in_specs=(
            P("head", "seq", None),
            P(None, "seq", None),
            P("seq", None),
            P(None, None, "head"),
            P("head"),
            P("head"),
            P("head", None),
            P(),
            P(),
            P(),
            P(),
            P(),
            P(None, "seq"),
            P(),
            P("seq", None),
            P(),
            P("head", "seq", None),
        ),
        out_specs=(
            P("head", "seq", None),
            P("head", "seq", None),
            P(None, "seq", None),
            P(None, None, "head"),
            P("head"),
            P("head"),
            P("head", None),
            P(),
            P(),
            P(),
            P(),
            P(),
            P("head", "seq"),
            P(),
            P("seq", "head"),
            P(),
        ),
        check_vma=False,
    )
```

```python
import jax
import jax.numpy as jnp
from jax import lax
from jax.experimental import pallas as pl
from jax.experimental.pallas import tpu as pltpu
from jax.sharding import PartitionSpec as P

HDIM = 64
EPSILON = 1e-05
NEGATIVE = -1e30
LOW = jnp.bfloat16
WIDE = jnp.float32
QROWS = 256
KROWS = 512
MEMROWS = 64
BLOCK = 128
NEAR_FIRST = ((0, 0), (-1, 0), (1, 0), (0, 1), (2, 0), (-1, 1), (1, 1), (2, 1))
FAR_FIRST = ((2, 1), (2, 0), (1, 1), (-1, 1), (1, 0), (-1, 0), (0, 1), (0, 0))
MESH = pl.DeviceIdType.MESH
VMEM = pl.BlockSpec(memory_space=pltpu.VMEM)
ANY = pl.BlockSpec(memory_space=pl.ANY)
VMEM_LIMIT = 60 * 2**20


def dot(left, right):
    return jnp.dot(left, right, preferred_element_type=WIDE)


def dot_nt(left, right):
    return lax.dot_general(left, right, (((1,), (1,)), ((), ())), preferred_element_type=WIDE)


def dot_tn(left, right):
    return lax.dot_general(left, right, (((0,), (0,)), ((), ())), preferred_element_type=WIDE)


def row_tiles(rows, body, step=16):
    def run(i, carry):
        body(pl.ds(pl.multiple_of(i * step, step), step))
        return carry

    lax.fori_loop(0, rows // step, run, 0)


class Group:
    def __init__(self, axis):
        self.axis = axis
        index = lax.axis_index(axis)
        self.me = index
        self.cores = 2 if axis == "head" else 1
        self.size = 8 * self.cores
        self.core = index % self.cores
        self.pair = index // self.cores % 2
        self.ring = index // (2 * self.cores)

    def chip(self, dr, dp):
        pair = 1 - self.pair if dp else self.pair
        return (self.ring + (dr + 4)) % 4 * 2 + pair

    def block(self, dr, dp, dc=0):
        core = 1 - self.core if dc else self.core
        return self.chip(dr, dp) * self.cores + core

    def device(self, dr, dp, dc=0):
        return {self.axis: self.block(dr, dp, dc)}

    def ahead(self, step):
        return (self.me + step) % self.size

    def away(self, step):
        return {self.axis: self.ahead(step)}

    def greet(self, barrier):
        peers = [(1, 0, 0), (-1, 0, 0), (0, 1, 0)] + ([(0, 0, 1)] if self.cores == 2 else [])
        for peer in peers:
            pl.semaphore_signal(barrier, 1, device_id=self.device(*peer), device_id_type=MESH)
        return len(peers)


def greet_all(*groups):
    barrier = pltpu.get_barrier_semaphore()
    pl.semaphore_wait(barrier, sum(group.greet(barrier) for group in groups))


class Gather:
    COPIES = 21

    def __init__(self, group, buf, send, recv, cut=BLOCK):
        self.group, self.buf, self.send, self.recv = group, buf, send, recv
        half = BLOCK // 2
        low = (cut // 2 + 15) // 16 * 16
        every, upper = (0, BLOCK), (cut, BLOCK - cut)
        ops = {
            "v0": ((0, 0), (1, 0, 0), every, (-1, 0)),
            "n0": ((0, 0), (-1, 0, 0), every, (1, 0)),
            "pair": ((0, 0), (0, 1, 0), every, (0, 1)),
            "v0h": ((-1, 0), (1, 0, 0), (0, half), (2, 0)),
            "n0h": ((1, 0), (-1, 0, 0), (half, half), (2, 0)),
            "v1": ((0, 1), (1, 0, 0), (0, cut), (-1, 1)),
            "n1": ((0, 1), (-1, 0, 0), (0, cut), (1, 1)),
            "v1h": ((-1, 1), (1, 0, 0), (0, low), (2, 1)),
            "n1h": ((1, 1), (-1, 0, 0), (low, cut - low), (2, 1)),
            "bv": ((-1, 0), (0, 1, 0), upper, (-1, 1)),
            "bn": ((1, 0), (0, 1, 0), upper, (1, 1)),
            "b2": ((2, 0), (0, 1, 0), upper, (2, 1)),
        }
        if group.cores == 2:
            for place in NEAR_FIRST:
                ops["s%d%d" % place] = (place, (0, 0, 1), every, place)
        self.ops = {name: (i,) + op for i, (name, op) in enumerate(ops.items()) if op[2][1] > 0}
        self.started = []
        self.inward = {
            (0, 0): (),
            (-1, 0): ("v0",),
            (1, 0): ("n0",),
            (0, 1): ("pair",),
            (2, 0): ("v0h", "n0h"),
            (-1, 1): ("v1", "bv"),
            (1, 1): ("n1", "bn"),
            (2, 1): ("v1h", "n1h", "b2"),
        }
        self.outward = {
            (0, 0): ("v0", "n0", "pair"),
            (-1, 0): ("v0h", "bv"),
            (1, 0): ("n0h", "bn"),
            (0, 1): ("v1", "n1"),
            (2, 0): ("b2",),
            (-1, 1): ("v1h",),
            (1, 1): ("n1h",),
            (2, 1): (),
        }

    def copy(self, name, arriving):
        i, place, peer, (start, count), source = self.ops[name]
        sibling = 1 if arriving and name[0] == "s" else 0
        block = self.group.block(*(source if arriving else place), sibling)
        view = self.buf.at[block] if count == BLOCK else self.buf.at[block, pl.ds(start, count)]
        return pltpu.make_async_remote_copy(
            src_ref=view,
            dst_ref=view,
            send_sem=self.send.at[i],
            recv_sem=self.recv.at[i],
            device_id=self.group.device(*peer),
            device_id_type=MESH,
        )

    def arrive(self, *place):
        for name in self.inward[place]:
            if name in self.ops:
                self.copy(name, True).wait_recv()
        names = self.outward[place]
        if self.group.cores == 2:
            names += ("s%d%d" % place,)
        for name in names:
            if name in self.ops:
                self.copy(name, False).start()
                self.started.append(name)

    def sibling(self, *place):
        if self.group.cores == 2:
            self.copy("s%d%d" % place, True).wait_recv()

    def drain(self):
        for name in self.started:
            self.copy(name, False).wait_send()


class Reduce:
    COPIES = 21

    def __init__(self, group, total, stage, land, send, recv, cut=BLOCK, near=None, result=None):
        self.group, self.total, self.land = group, total, land
        self.stage = total if stage is None else stage
        self.staged = stage is not None
        self.send, self.recv, self.near, self.result = send, recv, near, result
        half = BLOCK // 2
        low = (cut // 2 + 15) // 16 * 16
        every, upper = (0, BLOCK), (cut, BLOCK - cut)
        ops = {
            "b2": ((2, 1), (0, 1, 0), upper, 0),
            "n1h": ((2, 1), (1, 0, 0), (0, low), 1),
            "v1h": ((2, 1), (-1, 0, 0), (low, cut - low), 1),
            "n0h": ((2, 0), (1, 0, 0), (0, half), 2),
            "v0h": ((2, 0), (-1, 0, 0), (half, half), 2),
            "bn": ((1, 1), (0, 1, 0), upper, 3),
            "bv": ((-1, 1), (0, 1, 0), upper, 4),
            "n1": ((1, 1), (1, 0, 0), (0, cut), 3),
            "v1": ((-1, 1), (-1, 0, 0), (0, cut), 4),
            "n0": ((1, 0), (1, 0, 0), every, 5),
            "v0": ((-1, 0), (-1, 0, 0), every, 6),
            "pu": ((0, 1), (0, 1, 0), upper, 7),
            "pl": ((0, 1), (0, 1, 0), (0, cut), 7),
        }
        self.ops = {name: (i,) + op for i, (name, op) in enumerate(ops.items()) if op[2][1] > 0}
        self.cut = cut
        self.started = []
        self.early = {(1, 1): "bn", (-1, 1): "bv", (0, 1): "pu"}
        self.inward = {
            (2, 1): (),
            (2, 0): ("b2",),
            (1, 1): ("n1h",),
            (-1, 1): ("v1h",),
            (1, 0): ("bn", "n0h"),
            (-1, 0): ("bv", "v0h"),
            (0, 1): ("n1", "v1"),
            (0, 0): ("pu", "n0", "v0", "pl"),
        }
        self.outward = {
            (2, 1): ("b2", "n1h", "v1h"),
            (2, 0): ("n0h", "v0h"),
            (1, 1): ("n1",),
            (-1, 1): ("v1",),
            (1, 0): ("n0",),
            (-1, 0): ("v0",),
            (0, 1): ("pl",),
            (0, 0): (),
        }

    def copy(self, name):
        i, place, peer, (start, count), slot = self.ops[name]
        return pltpu.make_async_remote_copy(
            src_ref=self.stage.at[FAR_FIRST.index(place), pl.ds(start, count)],
            dst_ref=self.land.at[slot, pl.ds(start, count)],
            send_sem=self.send.at[i],
            recv_sem=self.recv.at[i],
            device_id=self.group.device(*peer),
            device_id_type=MESH,
        )

    def near_copy(self, k):
        return pltpu.make_async_remote_copy(
            src_ref=self.near[0].at[k],
            dst_ref=self.near[1].at[k],
            send_sem=self.send.at[13 + k],
            recv_sem=self.recv.at[13 + k],
            device_id=self.group.device(0, 0, 1),
            device_id_type=MESH,
        )

    def begin(self, name):
        self.copy(name).start()
        self.started.append(name)

    def blend(self, place, start, count, names):
        k = FAR_FIRST.index(place)
        spans = [self.ops[name][3] + (self.ops[name][4],) for name in names]
        marks = {start, start + count}
        for first, size, _ in spans:
            marks |= {m for m in (first, first + size) if start < m < start + count}
        marks = sorted(marks)
        for low, high in zip(marks, marks[1:]):
            slots = [slot for first, size, slot in spans if first <= low and high <= first + size]
            if not (slots or self.near or self.staged or place == (0, 0)):
                continue

            def body(rows):
                at = pl.ds(pl.multiple_of(rows.start + low, 16), 16)
                value = self.total[k, at].astype(WIDE)
                if self.near is not None:
                    value += self.near[1][k, at].astype(WIDE)
                for slot in slots:
                    value += self.land[slot, at].astype(WIDE)
                if place == (0, 0):
                    self.result[at] = value
                else:
                    self.stage[k, at] = value.astype(LOW)

            row_tiles(high - low, body)

    def settle(self, *place):
        if self.near is not None:
            self.near_copy(FAR_FIRST.index(place)).wait_recv()
        rest = BLOCK
        early = self.early.get(place)
        if early in self.ops:
            rest = self.cut
            self.blend(place, self.cut, BLOCK - self.cut, ())
            self.begin(early)
        names = [name for name in self.inward[place] if name in self.ops]
        for name in names:
            self.copy(name).wait_recv()
        self.blend(place, 0, rest, names)
        for name in self.outward[place]:
            if name in self.ops:
                self.begin(name)

    def drain(self):
        for name in self.started:
            self.copy(name).wait_send()
        if self.near is not None:
            for k in range(8):
                self.near_copy(k).wait_send()

    @staticmethod
    def scratch(columns, staged, near):
        part = pltpu.VMEM((8, BLOCK, columns), LOW)
        shapes = [pltpu.VMEM((8, BLOCK, columns), WIDE), part] if staged else [part]
        shapes += [part] + [pltpu.SemaphoreType.DMA((Reduce.COPIES,))] * 2
        return shapes + [part] * 2 if near else shapes


class Plane:
    def __init__(self, head):
        self.core, self.me, self.size = head.core, head.chip(0, 0), 8

    def ahead(self, step):
        return (self.me + step) % self.size

    def away(self, step):
        return {"head": self.ahead(step) * 2 + self.core}


def greet_everyone(head, *groups):
    barrier = pltpu.get_barrier_semaphore()
    pl.semaphore_signal(barrier, 1, device_id=head.device(0, 0, 1), device_id_type=MESH)
    for group in groups:
        def signal(step, carry):
            pl.semaphore_signal(barrier, 1, device_id=group.away(step), device_id_type=MESH)
            return carry

        lax.fori_loop(1, group.size, signal, 0)
    pl.semaphore_wait(barrier, 1 + sum(group.size - 1 for group in groups))


class Spread:
    def __init__(self, group, send, recv):
        self.group, self.send, self.recv = group, send, recv

    def copy(self, step, src, dst):
        return pltpu.make_async_remote_copy(
            src_ref=src,
            dst_ref=dst,
            send_sem=self.send.at[step],
            recv_sem=self.recv.at[step],
            device_id=self.group.away(step),
            device_id_type=MESH,
        )

    def each(self, body):
        def run(step, carry):
            body(step)
            return carry

        lax.fori_loop(1, self.group.size, run, 0)

    def start(self, src_of, land):
        self.each(lambda step: self.copy(step, src_of(self.group.ahead(step)), land.at[self.group.me]).start())

    def wait(self, land):
        def one(step):
            slot = land.at[self.group.ahead(self.group.size - step)]
            self.copy(step, slot, slot).wait_recv()

        self.each(one)

    def drain(self, src_of, land):
        self.each(lambda step: self.copy(step, src_of(self.group.ahead(step)), land.at[self.group.me]).wait_send())


def normal_of(values):
    mean = jnp.mean(values, axis=-1, keepdims=True)
    centered = values - mean
    var = jnp.mean(centered * centered, axis=-1, keepdims=True)
    rstd = lax.rsqrt(var + EPSILON)
    return centered * rstd, rstd


def stack_heads(rows):
    lane = lax.broadcasted_iota(jnp.int32, rows.shape, 1)
    zero = jnp.zeros_like(rows)
    return jnp.concatenate(
        [jnp.where(lane < HDIM, rows, zero), jnp.where(lane < HDIM, zero, rows)], axis=0
    )


def causal_bias(chunk, block, tail_bias):
    key = block * KROWS + lax.broadcasted_iota(jnp.int32, (KROWS, 2 * QROWS), 0)
    lane = lax.broadcasted_iota(jnp.int32, (KROWS, 2 * QROWS), 1)
    query = chunk * QROWS + jnp.where(lane < QROWS, lane, lane - QROWS)
    own = jnp.where(block == 2048 // KROWS - 1, tail_bias, jnp.zeros_like(tail_bias))
    return jnp.where(key <= query, jnp.broadcast_to(own, key.shape), NEGATIVE)


def transpose_into(dst_ref, src_ref):
    rows = src_ref.shape[0]
    if rows <= 256:
        dst_ref[...] = src_ref[...].T
        return

    def body(i, carry):
        at = pl.multiple_of(i * 256, 256)
        dst_ref[:, pl.ds(at, 256)] = src_ref[pl.ds(at, 256), :].T
        return carry

    lax.fori_loop(0, rows // 256, body, 0)


def attend_chunk(chunk, q_ref, k_ref, vt_ref, mk_ref, mvt_ref, mem_bias, tail_bias):
    start = pl.multiple_of(chunk * QROWS, QROWS)
    q2 = stack_heads(q_ref[pl.ds(start, QROWS), :] * HDIM ** (-0.5))

    def values_times(values_t, probs):
        low = probs.astype(LOW)
        return (
            dot(values_t[:HDIM], low[:, :QROWS]),
            dot(values_t[HDIM:], low[:, QROWS:]),
        )

    scores = dot_nt(mk_ref[...], q2) + mem_bias
    peak = jnp.max(scores, axis=0, keepdims=True)
    raised = jnp.exp(scores - peak)
    total = jnp.sum(raised, axis=0, keepdims=True)
    first, second = values_times(mvt_ref[...], raised)

    def update(block, scores, carry):
        peak, total, first, second = carry
        at = pl.multiple_of(block * KROWS, KROWS)
        new_peak = jnp.maximum(peak, jnp.max(scores, axis=0, keepdims=True))
        scale = jnp.exp(peak - new_peak)
        raised = jnp.exp(scores - new_peak)
        total = total * scale + jnp.sum(raised, axis=0, keepdims=True)
        add_first, add_second = values_times(vt_ref[:, pl.ds(at, KROWS)], raised)
        return (
            new_peak,
            total,
            first * scale[:, :QROWS] + add_first,
            second * scale[:, QROWS:] + add_second,
        )

    def block_scores(block):
        at = pl.multiple_of(block * KROWS, KROWS)
        return dot_nt(k_ref[pl.ds(at, KROWS), :], q2)

    full = chunk * QROWS // KROWS
    carry = lax.fori_loop(
        0, full, lambda b, c: update(b, block_scores(b), c), (peak, total, first, second)
    )
    scores = block_scores(full) + causal_bias(chunk, full, tail_bias)
    peak, total, first, second = update(full, scores, carry)
    inverse = 1.0 / total
    attended = jnp.concatenate([first * inverse[:, :QROWS], second * inverse[:, QROWS:]], axis=0)
    return attended, peak + jnp.log(total)


def chip_at(group, order, step):
    return sum(jnp.where(step == j, group.chip(*place), 0) for j, place in enumerate(order))


def open_kernel(
    hidden_ref, cot_ref, memory_ref, counts_ref, gain_ref, shift_ref, w_ref, b_query_ref, b_value_ref,
    q_ref, k_ref, v_ref, mk_ref, mv_ref, mem_normed_ref, mem_bias_ref, tail_bias_ref, w_t_ref,
    normed_out, cot_out,
    rows_buf, cot_buf, flat_w, mem_wide, send, recv, cot_send, cot_recv, out_sem,
):
    head, seq = Group("head"), Group("seq")
    gather = Gather(head, rows_buf, send, recv, 112)
    cot_gather = Gather(seq, cot_buf, cot_send, cot_recv, 112)
    own, cot_own = head.block(0, 0), seq.block(0, 0)

    def norm_rows(rows):
        normal, _ = normal_of(hidden_ref[rows].astype(WIDE))
        rows_buf[own, rows] = (normal * gain_ref[...] + shift_ref[...]).astype(LOW)
        cot_buf[cot_own, rows] = cot_ref[rows]

    row_tiles(BLOCK, norm_rows, 32)
    greet_all(head, seq)
    gather.arrive(0, 0)
    cot_gather.arrive(0, 0)
    width = q_ref.shape[1]
    slots = memory_ref.shape[0]
    for i in range(3):
        flat_w[:, i * width : (i + 1) * width] = w_ref[i]
    copies = []

    def project(*place):
        gather.sibling(*place)
        chip = head.chip(*place)
        out = pltpu.make_async_copy(
            rows_buf.at[pl.ds(chip * 2, 2)], normed_out.at[pl.ds(chip * 2, 2)], out_sem.at[len(copies)]
        )
        out.start()
        copies.append(out)
        rows = rows_buf[pl.ds(chip * 2, 2)].reshape(2 * BLOCK, rows_buf.shape[2])
        at = pl.ds(pl.multiple_of(chip * 2 * BLOCK, 2 * BLOCK), 2 * BLOCK)
        all_parts = dot(rows, flat_w[...])
        q_ref[at, :] = (all_parts[:, :width] + b_query_ref[...]).astype(LOW)
        k_ref[at, :] = all_parts[:, width : 2 * width].astype(LOW)
        v_ref[at, :] = (all_parts[:, 2 * width :] + b_value_ref[...]).astype(LOW)

    def keep_cot(*place):
        block = seq.block(*place)
        out = pltpu.make_async_copy(cot_buf.at[block], cot_out.at[block], out_sem.at[len(copies)])
        out.start()
        copies.append(out)

    def side_work():
        mem_wide[...] = jnp.zeros_like(mem_wide)
        mem_wide[:slots, :] = memory_ref[...].astype(WIDE)

        def norm_memory(rows):
            normal, _ = normal_of(mem_wide[rows])
            mem_normed_ref[rows] = (normal * gain_ref[...] + shift_ref[...]).astype(LOW)

        row_tiles(MEMROWS, norm_memory, 32)
        mem = dot(mem_normed_ref[...], flat_w[:, width:])
        mk_ref[...] = mem[:, :width].astype(LOW)
        mv_ref[...] = (mem[:, width:] + b_value_ref[...]).astype(LOW)
        slot = lax.broadcasted_iota(jnp.int32, mem_bias_ref.shape, 0)
        mem_bias_ref[...] = jnp.where(slot < counts_ref[0, 0], 0.0, NEGATIVE)
        tail = slots - KROWS + lax.broadcasted_iota(jnp.int32, tail_bias_ref.shape, 0)
        tail_bias_ref[...] = jnp.where((tail < 0) | (tail < counts_ref[0, 1]), 0.0, NEGATIVE)
        for i in range(3):
            transpose_into(w_t_ref.at[pl.ds(i * width, width)], w_ref.at[i])

    side_work()
    project(0, 0)
    keep_cot(0, 0)
    gather.arrive(-1, 0)
    gather.arrive(1, 0)
    cot_gather.arrive(-1, 0)
    cot_gather.arrive(1, 0)
    gather.arrive(0, 1)
    cot_gather.arrive(0, 1)
    project(-1, 0)
    project(1, 0)
    gather.arrive(2, 0)
    cot_gather.arrive(2, 0)
    project(0, 1)
    gather.arrive(-1, 1)
    gather.arrive(1, 1)
    cot_gather.arrive(-1, 1)
    cot_gather.arrive(1, 1)
    project(2, 0)
    project(-1, 1)
    project(1, 1)
    gather.arrive(2, 1)
    cot_gather.arrive(2, 1)
    project(2, 1)
    for place in NEAR_FIRST[1:]:
        keep_cot(*place)
    gather.drain()
    cot_gather.drain()
    for out in copies:
        out.wait()


def open_layer(hidden, cot, memory, counts, gain, shift, w, b_query, b_value):
    rows, model = hidden.shape
    width = w.shape[2]
    part = jax.ShapeDtypeStruct((16 * rows, width), LOW)
    mem_part = jax.ShapeDtypeStruct((MEMROWS, width), LOW)
    sems = [pltpu.SemaphoreType.DMA((Gather.COPIES,))] * 4
    smem = pl.BlockSpec(memory_space=pltpu.SMEM)
    return pl.pallas_call(
        open_kernel,
        out_shape=(
            part, part, part, mem_part, mem_part,
            jax.ShapeDtypeStruct((MEMROWS, model), LOW),
            jax.ShapeDtypeStruct((MEMROWS, 1), WIDE),
            jax.ShapeDtypeStruct((KROWS, 1), WIDE),
            jax.ShapeDtypeStruct((3 * width, model), LOW),
            jax.ShapeDtypeStruct((16, rows, model), LOW),
            jax.ShapeDtypeStruct((8, rows, model), LOW),
        ),
        in_specs=[VMEM] * 3 + [smem] + [VMEM] * 5,
        out_specs=(VMEM,) * 9 + (ANY,) * 2,
        scratch_shapes=[
            pltpu.VMEM((16, rows, model), LOW),
            pltpu.VMEM((8, rows, model), LOW),
            pltpu.VMEM((model, 3 * width), LOW),
            pltpu.VMEM((MEMROWS, model), WIDE),
        ] + sems + [pltpu.SemaphoreType.DMA((16,))],
        compiler_params=pltpu.CompilerParams(
            collective_id=0, has_side_effects=True, vmem_limit_bytes=VMEM_LIMIT
        ),
        name="open_layer",
    )(hidden, cot, memory, counts, gain, shift, w, b_query, b_value)


def attend_kernel(
    q_ref, k_ref, v_ref, mk_ref, mv_ref, mem_bias_ref, tail_bias_ref, wo_ref,
    hidden_ref, b_out_ref, gain_ref, shift_ref, cot_hbm, w_down_hbm, w_up_hbm,
    attn_t_ref, lse_ref, resid_ref, second_ref, back_ref, w_up_t_ref,
    vt_ref, mvt_ref, attn_ref, cot_buf, wd_ref, wu_ref, load_sem,
    total, stage, land, send, recv, near_stage, near_land,
):
    head = Group("head")
    reduce = Reduce(head, total, stage, land, send, recv, 96, (near_stage, near_land), resid_ref)
    loads = [
        pltpu.make_async_copy(src, dst, load_sem.at[i])
        for i, (src, dst) in enumerate(
            ((cot_hbm, cot_buf), (w_down_hbm, wd_ref), (w_up_hbm, wu_ref))
        )
    ]
    for load in loads:
        load.start()
    transpose_into(vt_ref, v_ref)
    transpose_into(mvt_ref, mv_ref)
    greet_all(head)

    def step(k, carry):
        chip = chip_at(head, FAR_FIRST, k)
        start = pl.multiple_of(chip * QROWS, QROWS)
        attended, lse = attend_chunk(
            chip, q_ref, k_ref, vt_ref, mk_ref, mvt_ref, mem_bias_ref[...], tail_bias_ref[...]
        )
        attn_t_ref[:, pl.ds(start, QROWS)] = attended.astype(LOW)
        attn_ref[...] = attended.T.astype(LOW)
        lse_ref[chip] = lse
        mine = attn_ref[pl.ds(pl.multiple_of(head.core * BLOCK, BLOCK), BLOCK), :]
        other = attn_ref[pl.ds(pl.multiple_of((1 - head.core) * BLOCK, BLOCK), BLOCK), :]
        for at in range(0, total.shape[2], 512):
            near_stage[k, :, at : at + 512] = dot(other, wo_ref[:, at : at + 512]).astype(LOW)
        reduce.near_copy(k).start()
        for at in range(0, total.shape[2], 512):
            total[k, :, at : at + 512] = dot(mine, wo_ref[:, at : at + 512])
        for j, place in enumerate(FAR_FIRST[:-1]):
            @pl.when(k == j + 1)
            def _():
                reduce.settle(*place)
        return carry

    lax.fori_loop(0, 8, step, 0)
    units = wd_ref.shape[0]
    model = hidden_ref.shape[1]
    for load in loads:
        load.wait()

    def cot_times(i, carry):
        pairs = cot_buf[pl.ds(2 * i, 2)].reshape(2 * BLOCK, model)
        for at in range(0, units, 256):
            part = dot_nt(pairs, wd_ref[at : at + 256, :]).astype(LOW)
            back_ref[pl.ds(2 * i, 2), :, at : at + 256] = part.reshape(2, BLOCK, 256)
        return carry

    lax.fori_loop(0, 4, cot_times, 0)
    transpose_into(w_up_t_ref, wu_ref)
    reduce.settle(0, 0)

    def finish(rows):
        resid = hidden_ref[rows].astype(WIDE) + resid_ref[rows] + b_out_ref[...]
        resid_ref[rows] = resid
        normal, _ = normal_of(resid)
        second_ref[rows] = (normal * gain_ref[...] + shift_ref[...]).astype(LOW)

    row_tiles(BLOCK, finish, 32)
    reduce.drain()


def attend_layer(
    q, k, v, mk, mv, mem_bias, tail_bias, wo, hidden, b_out, gain, shift, cot_all, w_down, w_up
):
    length, width = q.shape
    rows, model = hidden.shape
    units = w_up.shape[1]
    return pl.pallas_call(
        attend_kernel,
        out_shape=(
            jax.ShapeDtypeStruct((width, length), LOW),
            jax.ShapeDtypeStruct((length // QROWS, 1, 2 * QROWS), WIDE),
            jax.ShapeDtypeStruct((rows, model), WIDE),
            jax.ShapeDtypeStruct((rows, model), LOW),
            jax.ShapeDtypeStruct((8, rows, units), LOW),
            jax.ShapeDtypeStruct((units, model), LOW),
        ),
        in_specs=[VMEM] * 12 + [ANY] * 3,
        out_specs=(VMEM,) * 6,
        scratch_shapes=[
            pltpu.VMEM((width, length), LOW),
            pltpu.VMEM((width, MEMROWS), LOW),
            pltpu.VMEM((QROWS, width), LOW),
            pltpu.VMEM((8, rows, model), LOW),
            pltpu.VMEM((units, model), LOW),
            pltpu.VMEM((model, units), LOW),
            pltpu.SemaphoreType.DMA((3,)),
        ] + Reduce.scratch(model, True, True),
        compiler_params=pltpu.CompilerParams(
            collective_id=1, has_side_effects=True, vmem_limit_bytes=VMEM_LIMIT
        ),
        name="attend_layer",
    )(
        q, k, v, mk, mv, mem_bias, tail_bias, wo, hidden, b_out, gain, shift,
        cot_all, w_down, w_up,
    )


def gelu_parts(u):
    square = u * u
    t = jnp.tanh(0.7978845608 * (u + 0.044715 * (square * u)))
    half = 0.5 * (1.0 + t)
    slope = half + 0.5 * u * (1.0 - t * t) * (0.7978845608 * (1.0 + 0.134145 * square))
    return u * half, slope


def fold_rows(values):
    return jnp.sum(values.reshape(values.shape[0] // 8, 8, values.shape[1]), axis=0)


def feed_kernel(
    second_ref, w_up_hbm, w_up_t_hbm, back_hbm, w_down_hbm, cot_hbm, up_bias_ref, resid_ref, gain_ref,
    cot_ref,
    grad_resid_ref, sums_ref, branch_hbm, grad_w_ref, grad_b_up_ref,
    rows_buf, wu_ref, wut_ref, wd_ref, cot_buf, act_ref, back_ref, pre_ref, fold_ref, sum_fold, branch_buf,
    load_sem, branch_sem, send, recv,
    total, land, rsend, rrecv,
    w_total, w_land, w_send, w_recv, w_near_stage, w_near_land,
):
    head, seq = Group("head"), Group("seq")
    gather = Gather(seq, rows_buf, send, recv, 64)
    reduce = Reduce(seq, total, None, land, rsend, rrecv, 112, None, grad_resid_ref)
    w_reduce = Reduce(head, w_total, None, w_land, w_send, w_recv, 96, (w_near_stage, w_near_land), grad_w_ref)
    loads = [
        pltpu.make_async_copy(src, dst, load_sem.at[i])
        for i, (src, dst) in enumerate(
            (
                (w_up_hbm, wu_ref), (back_hbm, back_ref), (w_up_t_hbm, wut_ref),
                (cot_hbm, cot_buf), (w_down_hbm, wd_ref),
            )
        )
    ]
    for load in loads:
        load.start()
    own = seq.block(0, 0)
    rows_buf[own] = second_ref[...]
    fold_ref[...] = jnp.zeros_like(fold_ref)
    greet_all(head, seq)
    gather.arrive(0, 0)
    for load in loads[:3]:
        load.wait()
    units = act_ref.shape[2]
    model = rows_buf.shape[2]
    bias_at = pl.ds(pl.multiple_of(own * units, units), units)

    def feed(*place):
        block = seq.block(*place)
        pre_ref[...] = dot(rows_buf[block], wu_ref[...]) + up_bias_ref[:, bias_at]

        def bend(rows):
            activated, slope = gelu_parts(pre_ref[rows])
            grad_pre = back_ref[block, rows].astype(WIDE) * slope
            act_ref[block, rows] = activated.astype(LOW)
            back_ref[block, rows] = grad_pre.astype(LOW)
            fold_ref[...] += fold_rows(grad_pre)

        row_tiles(BLOCK, bend)
        k = FAR_FIRST.index(place)
        for at in range(0, model, 512):
            total[k, :, at : at + 512] = dot(back_ref[block], wut_ref[:, at : at + 512]).astype(LOW)

    feed(0, 0)
    gather.arrive(-1, 0)
    gather.arrive(1, 0)
    gather.arrive(0, 1)
    feed(-1, 0)
    gather.arrive(2, 0)
    feed(1, 0)
    gather.arrive(-1, 1)
    gather.arrive(1, 1)
    feed(0, 1)
    feed(2, 0)
    feed(-1, 1)
    feed(1, 1)
    gather.arrive(2, 1)
    feed(2, 1)
    reduce.settle(2, 1)
    reduce.settle(2, 0)
    for load in loads[3:]:
        load.wait()
    grad_b_up_ref[...] = jnp.sum(fold_ref[...], axis=0, keepdims=True)

    def weights(k, carry):
        chip = chip_at(head, FAR_FIRST, k)

        def part(core):
            at = pl.ds(pl.multiple_of(chip * 2 * BLOCK + core * BLOCK, BLOCK), BLOCK)
            length = 8 * BLOCK
            up = dot_tn(
                rows_buf[:, :, at].reshape(length, BLOCK), back_ref[...].reshape(length, units)
            )
            down = dot_tn(
                cot_buf[:, :, at].reshape(length, BLOCK), act_ref[...].reshape(length, units)
            )
            return up.astype(LOW), down.astype(LOW)

        w_near_stage[k, :, :units], w_near_stage[k, :, units:] = part(1 - head.core)
        w_reduce.near_copy(k).start()
        w_total[k, :, :units], w_total[k, :, units:] = part(head.core)
        for j, place in enumerate(FAR_FIRST[:6]):
            @pl.when(k == j + 1)
            def _():
                w_reduce.settle(*place)

        @pl.when(k == 2)
        def _():
            reduce.settle(1, 1)
            reduce.settle(-1, 1)

        @pl.when(k == 5)
        def _():
            reduce.settle(1, 0)
            reduce.settle(-1, 0)

        return carry

    lax.fori_loop(0, 8, weights, 0)
    branch_copies = []

    def branch(i):
        slot = i % 2
        if i >= 2:
            branch_copies[i - 2].wait()
        for at in range(0, model, 512):
            branch_buf[slot, :, at : at + 512] = dot(act_ref[i], wd_ref[:, at : at + 512]).astype(LOW)
        copy = pltpu.make_async_copy(branch_buf.at[slot], branch_hbm.at[i], branch_sem.at[i])
        copy.start()
        branch_copies.append(copy)

    for i in range(4):
        branch(i)
    reduce.settle(0, 1)
    w_reduce.settle(0, 1)
    for i in range(4, 8):
        branch(i)
    reduce.settle(0, 0)
    sum_fold[...] = jnp.zeros_like(sum_fold)

    def back(rows):
        normal, rstd = normal_of(resid_ref[rows])
        incoming = grad_resid_ref[rows]
        scaled = incoming * gain_ref[...]
        inner = jnp.mean(scaled, axis=-1, keepdims=True)
        along = jnp.mean(scaled * normal, axis=-1, keepdims=True)
        cot = cot_ref[rows].astype(WIDE)
        grad = cot + rstd * (scaled - inner - normal * along)
        grad_resid_ref[rows] = grad
        for i, value in enumerate((grad, incoming * normal, incoming, cot)):
            sum_fold[i] += fold_rows(value)

    row_tiles(BLOCK, back)
    sums_ref[...] = jnp.sum(sum_fold[...], axis=1)
    w_reduce.settle(0, 0)
    for copy in branch_copies[-2:]:
        copy.wait()
    gather.drain()
    reduce.drain()
    w_reduce.drain()


def feed_layer(second, w_up, w_up_t, back, w_down, cot_all, up_bias, resid, gain, cot):
    rows, model = second.shape
    units = w_up.shape[1]
    gather_sems = [pltpu.SemaphoreType.DMA((Gather.COPIES,))] * 2
    return pl.pallas_call(
        feed_kernel,
        out_shape=(
            jax.ShapeDtypeStruct((rows, model), WIDE),
            jax.ShapeDtypeStruct((4, model), WIDE),
            jax.ShapeDtypeStruct((8, rows, model), LOW),
            jax.ShapeDtypeStruct((rows, 2 * units), WIDE),
            jax.ShapeDtypeStruct((1, units), WIDE),
        ),
        in_specs=[VMEM] + [ANY] * 5 + [VMEM] * 4,
        out_specs=(VMEM, VMEM, ANY, VMEM, VMEM),
        scratch_shapes=[
            pltpu.VMEM((8, rows, model), LOW),
            pltpu.VMEM((model, units), LOW),
            pltpu.VMEM((units, model), LOW),
            pltpu.VMEM((units, model), LOW),
            pltpu.VMEM((8, rows, model), LOW),
            pltpu.VMEM((8, rows, units), LOW),
            pltpu.VMEM((8, rows, units), LOW),
            pltpu.VMEM((rows, units), WIDE),
            pltpu.VMEM((8, units), WIDE),
            pltpu.VMEM((4, 8, model), WIDE),
            pltpu.VMEM((2, rows, model), LOW),
            pltpu.SemaphoreType.DMA((5,)),
            pltpu.SemaphoreType.DMA((8,)),
        ] + gather_sems + Reduce.scratch(model, False, False) + Reduce.scratch(2 * units, False, True),
        compiler_params=pltpu.CompilerParams(
            collective_id=2, has_side_effects=True, vmem_limit_bytes=VMEM_LIMIT
        ),
        name="feed_layer",
    )(second, w_up, w_up_t, back, w_down, cot_all, up_bias, resid, gain, cot)


def attend_back_chunk(
    chunk, q_ref, k_ref, kt_ref, v_ref, mk_ref, mkt_ref, mv_ref, mem_bias, tail_bias,
    attn_t_ref, lse_ref, grad_rows, dk_ref, dv_ref, dmk_ref, dmv_ref,
):
    start = pl.multiple_of(chunk * QROWS, QROWS)
    q2 = stack_heads(q_ref[pl.ds(start, QROWS), :] * HDIM ** (-0.5))
    g2 = stack_heads(grad_rows)
    product = grad_rows.astype(WIDE).T * attn_t_ref[:, pl.ds(start, QROWS)].astype(WIDE)
    inner = jnp.concatenate(
        [
            jnp.sum(product[:HDIM], axis=0, keepdims=True),
            jnp.sum(product[HDIM:], axis=0, keepdims=True),
        ],
        axis=1,
    )
    lse = lse_ref[chunk]

    def piece(scores, values, keys_t):
        probs = jnp.exp(scores - lse)
        grad_probs = dot_nt(values, g2)
        grad_scores = (probs * (grad_probs - inner)).astype(LOW)
        return (
            dot(probs.astype(LOW), g2),
            dot(grad_scores, q2),
            dot(keys_t[:HDIM], grad_scores[:, :QROWS]),
            dot(keys_t[HDIM:], grad_scores[:, QROWS:]),
        )

    dv, dk, first, second = piece(
        dot_nt(mk_ref[...], q2) + mem_bias, mv_ref[...], mkt_ref[...]
    )
    dmv_ref[...] += dv
    dmk_ref[...] += dk

    def block_step(block, bias, carry):
        first, second = carry
        at = pl.multiple_of(block * KROWS, KROWS)
        scores = dot_nt(k_ref[pl.ds(at, KROWS), :], q2)
        if bias is not None:
            scores = scores + bias
        dv, dk, add_first, add_second = piece(
            scores, v_ref[pl.ds(at, KROWS), :], kt_ref[:, pl.ds(at, KROWS)]
        )
        dv_ref[pl.ds(at, KROWS), :] += dv
        dk_ref[pl.ds(at, KROWS), :] += dk
        return first + add_first, second + add_second

    full = chunk * QROWS // KROWS
    carry = lax.fori_loop(0, full, lambda b, c: block_step(b, None, c), (first, second))
    first, second = block_step(full, causal_bias(chunk, full, tail_bias), carry)
    return jnp.concatenate([first, second], axis=0) * HDIM ** (-0.5)


def grad_kernel(
    grad_resid_ref, resid_ref, b_down_ref, branch_hbm, wo_ref,
    q_ref, k_ref, v_ref, mk_ref, mv_ref, mem_bias_ref, tail_bias_ref, attn_t_ref, lse_ref,
    out_ref, own_ref, own_t_ref, mem_ref, mem_t_ref, grad_wo_ref, sums_ref,
    rows_buf, kt_ref, mkt_ref, dk_ref, dv_ref, dmk_ref, dmv_ref, wo_sum, branch_sum, fold_ref,
    load_sem, send, recv, total, land, rsend, rrecv,
):
    head, seq = Group("head"), Group("seq")
    gather = Gather(head, rows_buf, send, recv, 112)
    reduce = Reduce(seq, total, None, land, rsend, rrecv, 128, None, branch_sum)
    loads = [
        pltpu.make_async_copy(branch_hbm.at[seq.block(*place)], total.at[k], load_sem.at[k])
        for k, place in enumerate(FAR_FIRST)
    ]
    for load in loads:
        load.start()
    own = head.block(0, 0)
    rows_buf[own] = grad_resid_ref[...].astype(LOW)
    greet_all(head, seq)
    gather.arrive(0, 0)
    loads[0].wait()
    reduce.settle(2, 1)
    loads[1].wait()
    reduce.settle(2, 0)
    transpose_into(kt_ref, k_ref)
    transpose_into(mkt_ref, mk_ref)
    for ref in (dk_ref, dv_ref, dmk_ref, dmv_ref, wo_sum, fold_ref):
        ref[...] = jnp.zeros_like(ref)
    width, model = wo_ref.shape
    for load in loads[2:]:
        load.wait()

    def step(k, carry):
        @pl.when(k == 0)
        def _():
            gather.sibling(0, 0)

        @pl.when(k == 1)
        def _():
            gather.arrive(-1, 0)
            gather.arrive(1, 0)
            reduce.settle(1, 1)
            reduce.settle(-1, 1)
            gather.arrive(0, 1)
            gather.sibling(-1, 0)

        @pl.when(k == 2)
        def _():
            reduce.settle(1, 0)
            reduce.settle(-1, 0)
            gather.sibling(1, 0)

        @pl.when(k == 3)
        def _():
            gather.arrive(2, 0)
            gather.sibling(0, 1)

        @pl.when(k == 4)
        def _():
            gather.arrive(-1, 1)
            gather.arrive(1, 1)
            gather.sibling(2, 0)

        @pl.when(k == 5)
        def _():
            reduce.settle(0, 1)
            gather.sibling(-1, 1)

        @pl.when(k == 6)
        def _():
            gather.arrive(2, 1)
            gather.sibling(1, 1)

        @pl.when(k == 7)
        def _():
            gather.sibling(2, 1)

        chip = chip_at(head, NEAR_FIRST, k)
        at = pl.ds(pl.multiple_of(chip * QROWS, QROWS), QROWS)
        rows = rows_buf[pl.ds(chip * 2, 2)].reshape(QROWS, model)
        grad_rows = dot_nt(rows, wo_ref[...]).astype(LOW)
        wo_sum[...] += dot(attn_t_ref[:, at], rows)
        dq = attend_back_chunk(
            chip, q_ref, k_ref, kt_ref, v_ref, mk_ref, mkt_ref, mv_ref,
            mem_bias_ref[...], tail_bias_ref[...], attn_t_ref, lse_ref,
            grad_rows, dk_ref, dv_ref, dmk_ref, dmv_ref,
        ).astype(LOW)
        own_t_ref[:width, at] = dq
        own_ref[at, :width] = dq.T
        return carry

    lax.fori_loop(0, 8, step, 0)

    def finish_keys(i, carry):
        at = pl.ds(pl.multiple_of(i * 256, 256), 256)
        dk = dk_ref[at, :].astype(LOW)
        dv = dv_ref[at, :].astype(LOW)
        own_ref[at, width : 2 * width] = dk
        own_ref[at, 2 * width :] = dv
        own_t_ref[width : 2 * width, at] = dk.T
        own_t_ref[2 * width :, at] = dv.T
        fold_ref[...] += fold_rows(own_ref[at, :].astype(WIDE))
        return carry

    lax.fori_loop(0, q_ref.shape[0] // 256, finish_keys, 0)
    for i, ref in enumerate((dmk_ref, dmv_ref)):
        low = ref[...].astype(LOW)
        mem_ref[:, i * width : (i + 1) * width] = low
        mem_t_ref[i * width : (i + 1) * width, :] = low.T
    fold_ref[:, width:] += fold_rows(mem_ref[...].astype(WIDE))
    sums_ref[...] = jnp.sum(fold_ref[...], axis=0, keepdims=True)
    grad_wo_ref[...] = wo_sum[...].astype(LOW)
    reduce.settle(0, 0)

    def finish(rows):
        out_ref[rows] = (resid_ref[rows] + branch_sum[rows] + b_down_ref[...]).astype(LOW)

    row_tiles(BLOCK, finish)
    gather.drain()
    reduce.drain()


def grad_layer(
    grad_resid, resid, b_down, branch, wo, q, k, v, mk, mv, mem_bias, tail_bias, attn_t, lse,
):
    rows, model = grad_resid.shape
    length, width = q.shape
    return pl.pallas_call(
        grad_kernel,
        out_shape=(
            jax.ShapeDtypeStruct((rows, model), LOW),
            jax.ShapeDtypeStruct((length, 3 * width), LOW),
            jax.ShapeDtypeStruct((3 * width, length), LOW),
            jax.ShapeDtypeStruct((MEMROWS, 2 * width), LOW),
            jax.ShapeDtypeStruct((2 * width, MEMROWS), LOW),
            jax.ShapeDtypeStruct((width, model), LOW),
            jax.ShapeDtypeStruct((1, 3 * width), WIDE),
        ),
        in_specs=[VMEM] * 3 + [ANY] + [VMEM] * 10,
        out_specs=(VMEM,) * 7,
        scratch_shapes=[
            pltpu.VMEM((16, rows, model), LOW),
            pltpu.VMEM((width, length), LOW),
            pltpu.VMEM((width, MEMROWS), LOW),
            pltpu.VMEM((length, width), WIDE),
            pltpu.VMEM((length, width), WIDE),
            pltpu.VMEM((MEMROWS, width), WIDE),
            pltpu.VMEM((MEMROWS, width), WIDE),
            pltpu.VMEM((width, model), WIDE),
            pltpu.VMEM((rows, model), WIDE),
            pltpu.VMEM((8, 3 * width), WIDE),
            pltpu.SemaphoreType.DMA((8,)),
        ] + [pltpu.SemaphoreType.DMA((Gather.COPIES,))] * 2 + Reduce.scratch(model, False, False),
        compiler_params=pltpu.CompilerParams(
            collective_id=3, has_side_effects=True, vmem_limit_bytes=VMEM_LIMIT
        ),
        name="grad_layer",
    )(
        grad_resid, resid, b_down, branch, wo, q, k, v, mk, mv, mem_bias, tail_bias, attn_t, lse,
    )


SUM_ROWS = 16


def close_kernel(
    own_ref, own_t_ref, mem_ref, mem_t_ref, grad_wo_ref, mem_normed_ref, normed_hbm, w_t_ref,
    gain_ref, shift_ref, bias_sums_ref, feed_sums_ref, b_up_ref,
    grad_normed_ref, grad_w_ref, small_ref,
    rows_buf, mem_pad, norm_sums, pay_ref, core_land, pay_half, pay_land, seq_land,
    core_send, core_recv, pay_send, pay_recv, seq_send, seq_recv, all_send, all_recv, load_sem,
    total, stage, land, send, recv, near_stage, near_land,
    w_total, w_stage, w_land, w_send, w_recv, g_send, g_recv,
):
    head, seq = Group("head"), Group("seq")
    reduce = Reduce(head, total, stage, land, send, recv, 112, (near_stage, near_land), grad_normed_ref)
    w_reduce = Reduce(seq, w_total, w_stage, w_land, w_send, w_recv, 128, None, w_total.at[7])
    gather = Gather(seq, grad_w_ref, g_send, g_recv, 128)
    plane = Plane(head)
    pay = Spread(plane, pay_send, pay_recv)
    across = Spread(seq, seq_send, seq_recv)
    back = Spread(plane, all_send, all_recv)
    load = pltpu.make_async_copy(normed_hbm, rows_buf, load_sem)
    load.start()
    width = grad_wo_ref.shape[0]
    model = rows_buf.shape[2]
    length = own_ref.shape[0]
    wide = model // 2
    share = model // head.size
    mem_pad[...] = jnp.zeros_like(mem_pad)
    mem_pad[pl.ds(width, 2 * width), :] = mem_t_ref[...]
    norm_sums[...] = jnp.zeros_like(norm_sums)
    greet_everyone(head, plane, seq)

    def chunk(k):
        chip = head.chip(*FAR_FIRST[k])

        def part(core):
            at = pl.ds(pl.multiple_of(chip * QROWS + core * BLOCK, BLOCK), BLOCK)
            return own_ref[at, :]

        mine, other = part(head.core), part(1 - head.core)
        for at in range(0, model, 512):
            near_stage[k, :, at : at + 512] = dot(other, w_t_ref[:, at : at + 512]).astype(LOW)
        reduce.near_copy(k).start()
        for at in range(0, model, 512):
            total[k, :, at : at + 512] = dot(mine, w_t_ref[:, at : at + 512])

    def weights(k, carry):
        target = chip_at(seq, FAR_FIRST, k)
        part, side = target // 2, target % 2
        columns = pl.ds(pl.multiple_of(side * wide, wide), wide)

        @pl.when(part < 3)
        def _():
            at = pl.ds(pl.multiple_of(part * width, width), width)
            term = dot(
                own_t_ref[at, :], rows_buf[:, :, columns].reshape(length, wide)
            ) + dot(mem_pad[at, :], mem_normed_ref[:, columns])
            w_total[k] = term
            flat = w_t_ref[at, columns].astype(WIDE)
            norm_sums[0:1, columns] += jnp.sum(flat * term, axis=0, keepdims=True)

        @pl.when(part == 3)
        def _():
            w_total[k] = grad_wo_ref[:, columns].astype(WIDE)

        return carry

    def shift_sums():
        sums = bias_sums_ref[...]
        high = sums.astype(LOW)
        rest = (sums - high.astype(WIDE)).astype(LOW)
        pair = jnp.concatenate([high, rest, jnp.zeros((14, sums.shape[1]), LOW)], axis=0)
        both = dot(pair, w_t_ref[...])
        norm_sums[1:2, :] = both[0:1] + both[1:2]

    def core_copy(i, src, dst):
        return pltpu.make_async_remote_copy(
            src_ref=src,
            dst_ref=dst,
            send_sem=core_send.at[i],
            recv_sem=core_recv.at[i],
            device_id=head.device(0, 0, 1),
            device_id_type=MESH,
        )

    def half_of(core):
        return pay_ref.at[:, pl.ds(pl.multiple_of(core * wide, wide), wide)]

    def pay_part(i):
        return pay_half.at[:, pl.ds(pl.multiple_of(i * share, share), share)]

    def pay_core():
        return core_copy(0, half_of(1 - head.core), core_land)

    def pay_whole():
        return core_copy(1, small_ref.at[head.core], small_ref.at[head.core])

    def pay_start():
        pay_ref[:MEMROWS, :] = dot(mem_ref[...], w_t_ref[width:, :]).astype(LOW)
        at_gain = norm_sums[0:1, :] - shift_ref[...] * norm_sums[1:2, :]
        rows = [at_gain / gain_ref[...], norm_sums[1:2, :], feed_sums_ref[...]]
        units = b_up_ref.shape[1]
        per_row = model // units
        for r in range(8 // per_row):
            row = [jnp.where(seq.me == r * per_row + c, b_up_ref[...], 0.0) for c in range(per_row)]
            rows.append(jnp.concatenate(row, axis=1))
        rows.append(jnp.zeros((SUM_ROWS - 6 - 8 // per_row, model), WIDE))
        pay_ref[MEMROWS:, :] = jnp.concatenate(rows, axis=0).astype(LOW)
        pay_core().start()

    def pay_send_parts():
        pay_core().wait_recv()
        pay_half[...] = (half_of(head.core)[...].astype(WIDE) + core_land[...].astype(WIDE)).astype(LOW)
        pay_land[plane.me] = pay_part(plane.me)[...]
        pay.start(pay_part, pay_land)

    def pay_sum():
        pay.wait(pay_land)
        sums = pay_land[0].astype(WIDE)
        for i in range(1, 8):
            sums += pay_land[i].astype(WIDE)
        small_ref[head.core, plane.me, :MEMROWS, :] = sums[:MEMROWS].astype(LOW)
        used = 6 + 8 * b_up_ref.shape[1] // model
        rows = [sums[MEMROWS : MEMROWS + used]]
        rows += [bias_sums_ref[:, i * width : (i + 1) * width] for i in range(3)]
        rows.append(jnp.zeros((SUM_ROWS - 3 - used, share), WIDE))
        seq_land[seq.me] = jnp.concatenate(rows, axis=0).astype(LOW)
        across.start(lambda i: seq_land.at[seq.me], seq_land)

    def pay_back():
        across.wait(seq_land)
        sums = seq_land[0].astype(WIDE)
        for i in range(1, 8):
            sums += seq_land[i].astype(WIDE)
        small_ref[head.core, plane.me, MEMROWS:, :] = sums.astype(LOW)
        back.start(lambda i: small_ref.at[head.core, plane.me], small_ref.at[head.core])

    def pay_end():
        back.wait(small_ref.at[head.core])
        pay_whole().start()

    chunk(0)
    chunk(1)
    load.wait()
    lax.fori_loop(0, 2, weights, 0)
    w_reduce.settle(2, 1)
    w_reduce.settle(2, 0)
    reduce.settle(2, 1)
    reduce.settle(2, 0)
    lax.fori_loop(2, 4, weights, 0)
    w_reduce.settle(1, 1)
    w_reduce.settle(-1, 1)
    chunk(2)
    chunk(3)
    lax.fori_loop(4, 6, weights, 0)
    w_reduce.settle(1, 0)
    w_reduce.settle(-1, 0)
    reduce.settle(1, 1)
    reduce.settle(-1, 1)
    lax.fori_loop(6, 7, weights, 0)
    w_reduce.settle(0, 1)
    lax.fori_loop(7, 8, weights, 0)
    shift_sums()
    pay_start()
    chunk(4)
    chunk(5)
    pay_send_parts()
    reduce.settle(1, 0)
    reduce.settle(-1, 0)
    w_reduce.settle(0, 0)
    grad_w_ref[seq.me] = w_total[7].astype(LOW)
    gather.arrive(0, 0)
    chunk(6)
    chunk(7)
    gather.arrive(-1, 0)
    gather.arrive(1, 0)
    gather.arrive(0, 1)
    pay_sum()
    reduce.settle(0, 1)
    gather.arrive(2, 0)
    gather.arrive(-1, 1)
    gather.arrive(1, 1)
    pay_back()
    reduce.settle(0, 0)
    pay_end()
    gather.arrive(2, 1)
    core_copy(1, small_ref.at[1 - head.core], small_ref.at[1 - head.core]).wait_recv()
    pay_core().wait_send()
    pay_whole().wait_send()
    pay.drain(pay_part, pay_land)
    across.drain(lambda i: seq_land.at[seq.me], seq_land)
    back.drain(lambda i: small_ref.at[head.core, plane.me], small_ref.at[head.core])
    gather.drain()
    w_reduce.drain()
    reduce.drain()


def close_layer(
    own, own_t, mem, mem_t, grad_wo, mem_normed, normed_all, w_t, gain, shift, bias_sums,
    feed_sums, b_up,
):
    rows, model = normed_all.shape[1:]
    width = grad_wo.shape[0]
    sems = [pltpu.SemaphoreType.DMA((Gather.COPIES,))] * 2
    pay_rows = MEMROWS + SUM_ROWS
    return pl.pallas_call(
        close_kernel,
        out_shape=(
            jax.ShapeDtypeStruct((rows, model), WIDE),
            jax.ShapeDtypeStruct((8, width, model // 2), LOW),
            jax.ShapeDtypeStruct((2, 8, pay_rows, model // 16), LOW),
        ),
        in_specs=[VMEM] * 6 + [ANY] + [VMEM] * 6,
        out_specs=(VMEM,) * 3,
        scratch_shapes=[
            pltpu.VMEM((16, rows, model), LOW),
            pltpu.VMEM((3 * width, MEMROWS), LOW),
            pltpu.VMEM((8, model), WIDE),
            pltpu.VMEM((pay_rows, model), LOW),
            pltpu.VMEM((pay_rows, model // 2), LOW),
            pltpu.VMEM((pay_rows, model // 2), LOW),
            pltpu.VMEM((8, pay_rows, model // 16), LOW),
            pltpu.VMEM((8, SUM_ROWS, model // 16), LOW),
            pltpu.SemaphoreType.DMA((2,)),
            pltpu.SemaphoreType.DMA((2,)),
            pltpu.SemaphoreType.DMA((8,)),
            pltpu.SemaphoreType.DMA((8,)),
            pltpu.SemaphoreType.DMA((8,)),
            pltpu.SemaphoreType.DMA((8,)),
            pltpu.SemaphoreType.DMA((8,)),
            pltpu.SemaphoreType.DMA((8,)),
            pltpu.SemaphoreType.DMA,
        ] + Reduce.scratch(model, True, True) + Reduce.scratch(model // 2, True, False) + sems,
        compiler_params=pltpu.CompilerParams(
            collective_id=4, has_side_effects=True, vmem_limit_bytes=VMEM_LIMIT
        ),
        name="close_layer",
    )(
        own, own_t, mem, mem_t, grad_wo, mem_normed, normed_all, w_t, gain, shift, bias_sums,
        feed_sums, b_up,
    )


def finish_kernel(
    grad_normed_ref, hidden_ref, grad_resid_ref, gain_ref, grad_w_ref, small_ref, memory_ref,
    feed_w_ref, output_ref,
    out_ref, grad_hidden_ref, grad_memory_ref, grad_qkv_ref, b_query_ref, b_value_ref, grad_wo_ref,
    b_out_ref, gain_one_ref, shift_one_ref, gain_two_ref, shift_two_ref,
    w_up_ref, b_up_ref, w_down_ref, b_down_ref,
    mem_wide, spread_ref,
):
    share = small_ref.shape[3]
    for i in range(16):
        spread_ref[:, i * share : (i + 1) * share] = small_ref[i // 8, i % 8].astype(WIDE)

    def norm_back(values, incoming):
        normal, rstd = normal_of(values)
        scaled = incoming * gain_ref[...]
        inner = jnp.mean(scaled, axis=-1, keepdims=True)
        along = jnp.mean(scaled * normal, axis=-1, keepdims=True)
        return rstd * (scaled - inner - normal * along)

    def back(rows):
        grad_hidden = grad_resid_ref[rows] + norm_back(
            hidden_ref[rows].astype(WIDE), grad_normed_ref[rows]
        )
        grad_hidden_ref[rows] = grad_hidden[:, None, :]

    row_tiles(hidden_ref.shape[0], back, 32)
    slots = memory_ref.shape[0]
    mem_wide[...] = jnp.zeros_like(mem_wide)
    mem_wide[:slots, :] = memory_ref[...].astype(WIDE)

    def back_memory(rows):
        mem_wide[rows] = norm_back(mem_wide[rows], spread_ref[rows])

    row_tiles(MEMROWS, back_memory, 32)
    grad_memory_ref[...] = mem_wide[:slots, :][:, None, :]
    out_ref[...] = output_ref[...]
    wide, units = grad_w_ref.shape[2], w_up_ref.shape[1]
    for i in range(3):
        for j in range(2):
            grad_qkv_ref[i, j * wide : (j + 1) * wide, :] = grad_w_ref[2 * i + j].astype(WIDE).T
    for j in range(2):
        grad_wo_ref[:, j * wide : (j + 1) * wide] = grad_w_ref[6 + j].astype(WIDE)
    w_up_ref[...] = feed_w_ref[:, :units]
    w_down_ref[...] = feed_w_ref[:, units:].T
    sums = [spread_ref[MEMROWS + i : MEMROWS + i + 1, :] for i in range(SUM_ROWS)]
    ordered = (gain_one_ref, shift_one_ref, b_out_ref, gain_two_ref, shift_two_ref, b_down_ref)
    for ref, row in zip(ordered, sums):
        ref[...] = row
    model = b_out_ref.shape[1]
    for i in range(4):
        b_up_ref[:, i * model : (i + 1) * model] = sums[6 + i]
    index = lax.axis_index("head")
    mine = small_ref[index % 2, index // 2].astype(WIDE)
    b_query_ref[...] = mine[MEMROWS + 10 : MEMROWS + 11, :]
    b_value_ref[...] = mine[MEMROWS + 12 : MEMROWS + 13, :]


def finish_layer(
    grad_normed, hidden, grad_resid, gain, grad_w, small, memory, feed_w, output
):
    rows, model = hidden.shape
    width, units = grad_w.shape[1], feed_w.shape[1] // 2
    wide = lambda *shape: jax.ShapeDtypeStruct(shape, WIDE)
    return pl.pallas_call(
        finish_kernel,
        out_shape=(
            jax.ShapeDtypeStruct((rows, model), LOW), wide(rows, 1, model), wide(memory.shape[0], 1, model),
            wide(3, model, width), wide(1, width), wide(1, width), wide(width, model),
            wide(1, model), wide(1, model), wide(1, model), wide(1, model), wide(1, model),
            wide(rows, units), wide(1, 8 * units), wide(units, rows), wide(1, model),
        ),
        in_specs=[VMEM] * 9,
        out_specs=(VMEM,) * 16,
        scratch_shapes=[
            pltpu.VMEM((MEMROWS, model), WIDE),
            pltpu.VMEM((MEMROWS + SUM_ROWS, model), WIDE),
        ],
        compiler_params=pltpu.CompilerParams(vmem_limit_bytes=VMEM_LIMIT),
        name="finish_layer",
    )(grad_normed, hidden, grad_resid, gain, grad_w, small, memory, feed_w, output)


def on_device(
    hidden, memory, counts, w_qkv, b_query, b_value, output_weight, b_out,
    gain_one, shift_one, gain_two, shift_two, w_up, up_bias, w_down, b_down, cotangent,
):
    hidden, memory, cot = hidden[:, 0], memory[:, 0], cotangent[:, 0]
    model = hidden.shape[1]
    width = w_qkv.shape[2]
    w_parts = jnp.transpose(w_qkv, (1, 0, 2))
    gain_one, shift_one, gain_two, shift_two, b_out, b_down, b_query, b_value, up_bias = (
        vector[None]
        for vector in (
            gain_one, shift_one, gain_two, shift_two, b_out, b_down, b_query, b_value, up_bias
        )
    )
    q, k, v, mk, mv, mem_normed, mem_bias, tail_bias, w_t, normed_all, cot_all = open_layer(
        hidden, cot, memory, counts, gain_one, shift_one, w_parts, b_query, b_value
    )
    attn_t, lse, resid, second, back, w_up_t = attend_layer(
        q, k, v, mk, mv, mem_bias, tail_bias, output_weight, hidden, b_out, gain_two, shift_two,
        cot_all, w_down, w_up,
    )
    grad_resid, feed_sums, branch, feed_w, grad_b_up = feed_layer(
        second, w_up, w_up_t, back, w_down, cot_all, up_bias, resid, gain_two, cot
    )
    output, own, own_t, mem, mem_t, grad_wo, bias_sums = grad_layer(
        grad_resid, resid, b_down, branch, output_weight,
        q, k, v, mk, mv, mem_bias, tail_bias, attn_t, lse,
    )
    grad_normed, grad_w, small = close_layer(
        own, own_t, mem, mem_t, grad_wo, mem_normed, normed_all, w_t, gain_one, shift_one,
        bias_sums, feed_sums, grad_b_up,
    )
    outs = finish_layer(
        grad_normed, hidden, grad_resid, gain_one, grad_w, small, memory, feed_w, output
    )
    output, grad_hidden, grad_memory, grad_w_qkv, *rest = outs
    rest = [part[0] if part.shape[0] == 1 else part for part in rest]
    return (
        output[:, None],
        grad_hidden,
        grad_memory,
        jnp.transpose(grad_w_qkv, (1, 0, 2)),
        *rest,
    )


def solution(mesh):
    return jax.shard_map(
        on_device,
        mesh=mesh,
        in_specs=(
            P("head", "seq", None),
            P(None, "seq", None),
            P("seq", None),
            P(None, None, "head"),
            P("head"),
            P("head"),
            P("head", None),
            P(),
            P(),
            P(),
            P(),
            P(),
            P(None, "seq"),
            P(),
            P("seq", None),
            P(),
            P("head", "seq", None),
        ),
        out_specs=(
            P("head", "seq", None),
            P("head", "seq", None),
            P(None, "seq", None),
            P(None, None, "head"),
            P("head"),
            P("head"),
            P("head", None),
            P(),
            P(),
            P(),
            P(),
            P(),
            P("head", "seq"),
            P(),
            P("seq", "head"),
            P(),
        ),
        check_vma=False,
    )
```

```python
import jax
import jax.numpy as jnp
from jax import lax
from jax.experimental import pallas as pl
from jax.experimental.pallas import tpu as pltpu
from jax.sharding import PartitionSpec as P

HDIM = 64
EPSILON = 1e-05
NEGATIVE = -1e30
LOW = jnp.bfloat16
WIDE = jnp.float32
QROWS = 256
KROWS = 512
MEMROWS = 64
BLOCK = 128
NEAR_FIRST = ((0, 0), (-1, 0), (1, 0), (0, 1), (2, 0), (-1, 1), (1, 1), (2, 1))
FAR_FIRST = ((2, 1), (2, 0), (1, 1), (-1, 1), (1, 0), (-1, 0), (0, 1), (0, 0))
MESH = pl.DeviceIdType.MESH
VMEM = pl.BlockSpec(memory_space=pltpu.VMEM)
ANY = pl.BlockSpec(memory_space=pl.ANY)
VMEM_LIMIT = 60 * 2**20


def dot(left, right):
    return jnp.dot(left, right, preferred_element_type=WIDE)


def dot_nt(left, right):
    return lax.dot_general(left, right, (((1,), (1,)), ((), ())), preferred_element_type=WIDE)


def dot_tn(left, right):
    return lax.dot_general(left, right, (((0,), (0,)), ((), ())), preferred_element_type=WIDE)


def row_tiles(rows, body, step=16):
    def run(i, carry):
        body(pl.ds(pl.multiple_of(i * step, step), step))
        return carry

    lax.fori_loop(0, rows // step, run, 0)


class Group:
    def __init__(self, axis):
        self.axis = axis
        index = lax.axis_index(axis)
        self.me = index
        self.cores = 2 if axis == "head" else 1
        self.size = 8 * self.cores
        self.core = index % self.cores
        self.pair = index // self.cores % 2
        self.ring = index // (2 * self.cores)

    def chip(self, dr, dp):
        pair = 1 - self.pair if dp else self.pair
        return (self.ring + (dr + 4)) % 4 * 2 + pair

    def block(self, dr, dp, dc=0):
        core = 1 - self.core if dc else self.core
        return self.chip(dr, dp) * self.cores + core

    def device(self, dr, dp, dc=0):
        return {self.axis: self.block(dr, dp, dc)}

    def ahead(self, step):
        return (self.me + step) % self.size

    def away(self, step):
        return {self.axis: self.ahead(step)}

    def greet(self, barrier):
        peers = [(1, 0, 0), (-1, 0, 0), (0, 1, 0)] + ([(0, 0, 1)] if self.cores == 2 else [])
        for peer in peers:
            pl.semaphore_signal(barrier, 1, device_id=self.device(*peer), device_id_type=MESH)
        return len(peers)


def greet_all(*groups):
    barrier = pltpu.get_barrier_semaphore()
    pl.semaphore_wait(barrier, sum(group.greet(barrier) for group in groups))


class Gather:
    COPIES = 21

    def __init__(self, group, buf, send, recv, cut=BLOCK):
        self.group, self.buf, self.send, self.recv = group, buf, send, recv
        half = BLOCK // 2
        low = (cut // 2 + 15) // 16 * 16
        every, upper = (0, BLOCK), (cut, BLOCK - cut)
        ops = {
            "v0": ((0, 0), (1, 0, 0), every, (-1, 0)),
            "n0": ((0, 0), (-1, 0, 0), every, (1, 0)),
            "pair": ((0, 0), (0, 1, 0), every, (0, 1)),
            "v0h": ((-1, 0), (1, 0, 0), (0, half), (2, 0)),
            "n0h": ((1, 0), (-1, 0, 0), (half, half), (2, 0)),
            "v1": ((0, 1), (1, 0, 0), (0, cut), (-1, 1)),
            "n1": ((0, 1), (-1, 0, 0), (0, cut), (1, 1)),
            "v1h": ((-1, 1), (1, 0, 0), (0, low), (2, 1)),
            "n1h": ((1, 1), (-1, 0, 0), (low, cut - low), (2, 1)),
            "bv": ((-1, 0), (0, 1, 0), upper, (-1, 1)),
            "bn": ((1, 0), (0, 1, 0), upper, (1, 1)),
            "b2": ((2, 0), (0, 1, 0), upper, (2, 1)),
        }
        if group.cores == 2:
            for place in NEAR_FIRST:
                ops["s%d%d" % place] = (place, (0, 0, 1), every, place)
        self.ops = {name: (i,) + op for i, (name, op) in enumerate(ops.items()) if op[2][1] > 0}
        self.started = []
        self.inward = {
            (0, 0): (),
            (-1, 0): ("v0",),
            (1, 0): ("n0",),
            (0, 1): ("pair",),
            (2, 0): ("v0h", "n0h"),
            (-1, 1): ("v1", "bv"),
            (1, 1): ("n1", "bn"),
            (2, 1): ("v1h", "n1h", "b2"),
        }
        self.outward = {
            (0, 0): ("v0", "n0", "pair"),
            (-1, 0): ("v0h", "bv"),
            (1, 0): ("n0h", "bn"),
            (0, 1): ("v1", "n1"),
            (2, 0): ("b2",),
            (-1, 1): ("v1h",),
            (1, 1): ("n1h",),
            (2, 1): (),
        }

    def copy(self, name, arriving):
        i, place, peer, (start, count), source = self.ops[name]
        sibling = 1 if arriving and name[0] == "s" else 0
        block = self.group.block(*(source if arriving else place), sibling)
        view = self.buf.at[block] if count == BLOCK else self.buf.at[block, pl.ds(start, count)]
        return pltpu.make_async_remote_copy(
            src_ref=view,
            dst_ref=view,
            send_sem=self.send.at[i],
            recv_sem=self.recv.at[i],
            device_id=self.group.device(*peer),
            device_id_type=MESH,
        )

    def arrive(self, *place):
        for name in self.inward[place]:
            if name in self.ops:
                self.copy(name, True).wait_recv()
        names = self.outward[place]
        if self.group.cores == 2:
            names += ("s%d%d" % place,)
        for name in names:
            if name in self.ops:
                self.copy(name, False).start()
                self.started.append(name)

    def sibling(self, *place):
        if self.group.cores == 2:
            self.copy("s%d%d" % place, True).wait_recv()

    def drain(self):
        for name in self.started:
            self.copy(name, False).wait_send()


class Reduce:
    COPIES = 21

    def __init__(self, group, total, stage, land, send, recv, cut=BLOCK, near=None, result=None):
        self.group, self.total, self.land = group, total, land
        self.stage = total if stage is None else stage
        self.staged = stage is not None
        self.send, self.recv, self.near, self.result = send, recv, near, result
        half = BLOCK // 2
        low = (cut // 2 + 15) // 16 * 16
        every, upper = (0, BLOCK), (cut, BLOCK - cut)
        ops = {
            "b2": ((2, 1), (0, 1, 0), upper, 0),
            "n1h": ((2, 1), (1, 0, 0), (0, low), 1),
            "v1h": ((2, 1), (-1, 0, 0), (low, cut - low), 1),
            "n0h": ((2, 0), (1, 0, 0), (0, half), 2),
            "v0h": ((2, 0), (-1, 0, 0), (half, half), 2),
            "bn": ((1, 1), (0, 1, 0), upper, 3),
            "bv": ((-1, 1), (0, 1, 0), upper, 4),
            "n1": ((1, 1), (1, 0, 0), (0, cut), 3),
            "v1": ((-1, 1), (-1, 0, 0), (0, cut), 4),
            "n0": ((1, 0), (1, 0, 0), every, 5),
            "v0": ((-1, 0), (-1, 0, 0), every, 6),
            "pu": ((0, 1), (0, 1, 0), upper, 7),
            "pl": ((0, 1), (0, 1, 0), (0, cut), 7),
        }
        self.ops = {name: (i,) + op for i, (name, op) in enumerate(ops.items()) if op[2][1] > 0}
        self.cut = cut
        self.started = []
        self.early = {(1, 1): "bn", (-1, 1): "bv", (0, 1): "pu"}
        self.inward = {
            (2, 1): (),
            (2, 0): ("b2",),
            (1, 1): ("n1h",),
            (-1, 1): ("v1h",),
            (1, 0): ("bn", "n0h"),
            (-1, 0): ("bv", "v0h"),
            (0, 1): ("n1", "v1"),
            (0, 0): ("pu", "n0", "v0", "pl"),
        }
        self.outward = {
            (2, 1): ("b2", "n1h", "v1h"),
            (2, 0): ("n0h", "v0h"),
            (1, 1): ("n1",),
            (-1, 1): ("v1",),
            (1, 0): ("n0",),
            (-1, 0): ("v0",),
            (0, 1): ("pl",),
            (0, 0): (),
        }

    def copy(self, name):
        i, place, peer, (start, count), slot = self.ops[name]
        return pltpu.make_async_remote_copy(
            src_ref=self.stage.at[FAR_FIRST.index(place), pl.ds(start, count)],
            dst_ref=self.land.at[slot, pl.ds(start, count)],
            send_sem=self.send.at[i],
            recv_sem=self.recv.at[i],
            device_id=self.group.device(*peer),
            device_id_type=MESH,
        )

    def near_copy(self, k):
        return pltpu.make_async_remote_copy(
            src_ref=self.near[0].at[k],
            dst_ref=self.near[1].at[k],
            send_sem=self.send.at[13 + k],
            recv_sem=self.recv.at[13 + k],
            device_id=self.group.device(0, 0, 1),
            device_id_type=MESH,
        )

    def begin(self, name):
        self.copy(name).start()
        self.started.append(name)

    def blend(self, place, start, count, names):
        k = FAR_FIRST.index(place)
        spans = [self.ops[name][3] + (self.ops[name][4],) for name in names]
        marks = {start, start + count}
        for first, size, _ in spans:
            marks |= {m for m in (first, first + size) if start < m < start + count}
        marks = sorted(marks)
        for low, high in zip(marks, marks[1:]):
            slots = [slot for first, size, slot in spans if first <= low and high <= first + size]
            if not (slots or self.near or self.staged or place == (0, 0)):
                continue

            def body(rows):
                at = pl.ds(pl.multiple_of(rows.start + low, 16), 16)
                value = self.total[k, at].astype(WIDE)
                if self.near is not None:
                    value += self.near[1][k, at].astype(WIDE)
                for slot in slots:
                    value += self.land[slot, at].astype(WIDE)
                if place == (0, 0):
                    self.result[at] = value
                else:
                    self.stage[k, at] = value.astype(LOW)

            row_tiles(high - low, body)

    def settle(self, *place):
        if self.near is not None:
            self.near_copy(FAR_FIRST.index(place)).wait_recv()
        rest = BLOCK
        early = self.early.get(place)
        if early in self.ops:
            rest = self.cut
            self.blend(place, self.cut, BLOCK - self.cut, ())
            self.begin(early)
        names = [name for name in self.inward[place] if name in self.ops]
        for name in names:
            self.copy(name).wait_recv()
        self.blend(place, 0, rest, names)
        for name in self.outward[place]:
            if name in self.ops:
                self.begin(name)

    def drain(self):
        for name in self.started:
            self.copy(name).wait_send()
        if self.near is not None:
            for k in range(8):
                self.near_copy(k).wait_send()

    @staticmethod
    def scratch(columns, staged, near):
        part = pltpu.VMEM((8, BLOCK, columns), LOW)
        shapes = [pltpu.VMEM((8, BLOCK, columns), WIDE), part] if staged else [part]
        shapes += [part] + [pltpu.SemaphoreType.DMA((Reduce.COPIES,))] * 2
        return shapes + [part] * 2 if near else shapes


class Plane:
    def __init__(self, head):
        self.core, self.me, self.size = head.core, head.chip(0, 0), 8

    def ahead(self, step):
        return (self.me + step) % self.size

    def away(self, step):
        return {"head": self.ahead(step) * 2 + self.core}


def greet_everyone(head, *groups):
    barrier = pltpu.get_barrier_semaphore()
    pl.semaphore_signal(barrier, 1, device_id=head.device(0, 0, 1), device_id_type=MESH)
    for group in groups:
        def signal(step, carry):
            pl.semaphore_signal(barrier, 1, device_id=group.away(step), device_id_type=MESH)
            return carry

        lax.fori_loop(1, group.size, signal, 0)
    pl.semaphore_wait(barrier, 1 + sum(group.size - 1 for group in groups))


class Spread:
    def __init__(self, group, send, recv):
        self.group, self.send, self.recv = group, send, recv

    def copy(self, step, src, dst):
        return pltpu.make_async_remote_copy(
            src_ref=src,
            dst_ref=dst,
            send_sem=self.send.at[step],
            recv_sem=self.recv.at[step],
            device_id=self.group.away(step),
            device_id_type=MESH,
        )

    def each(self, body):
        def run(step, carry):
            body(step)
            return carry

        lax.fori_loop(1, self.group.size, run, 0)

    def start(self, src_of, land):
        self.each(lambda step: self.copy(step, src_of(self.group.ahead(step)), land.at[self.group.me]).start())

    def wait(self, land):
        def one(step):
            slot = land.at[self.group.ahead(self.group.size - step)]
            self.copy(step, slot, slot).wait_recv()

        self.each(one)

    def drain(self, src_of, land):
        self.each(lambda step: self.copy(step, src_of(self.group.ahead(step)), land.at[self.group.me]).wait_send())


def normal_of(values):
    mean = jnp.mean(values, axis=-1, keepdims=True)
    centered = values - mean
    var = jnp.mean(centered * centered, axis=-1, keepdims=True)
    rstd = lax.rsqrt(var + EPSILON)
    return centered * rstd, rstd


def stack_heads(rows):
    lane = lax.broadcasted_iota(jnp.int32, rows.shape, 1)
    zero = jnp.zeros_like(rows)
    return jnp.concatenate(
        [jnp.where(lane < HDIM, rows, zero), jnp.where(lane < HDIM, zero, rows)], axis=0
    )


def causal_bias(chunk, block, tail_bias):
    key = block * KROWS + lax.broadcasted_iota(jnp.int32, (KROWS, 2 * QROWS), 0)
    lane = lax.broadcasted_iota(jnp.int32, (KROWS, 2 * QROWS), 1)
    query = chunk * QROWS + jnp.where(lane < QROWS, lane, lane - QROWS)
    own = jnp.where(block == 2048 // KROWS - 1, tail_bias, jnp.zeros_like(tail_bias))
    return jnp.where(key <= query, jnp.broadcast_to(own, key.shape), NEGATIVE)


def transpose_into(dst_ref, src_ref):
    rows = src_ref.shape[0]
    if rows <= 256:
        dst_ref[...] = src_ref[...].T
        return

    def body(i, carry):
        at = pl.multiple_of(i * 256, 256)
        dst_ref[:, pl.ds(at, 256)] = src_ref[pl.ds(at, 256), :].T
        return carry

    lax.fori_loop(0, rows // 256, body, 0)


def attend_chunk(chunk, q_ref, k_ref, vt_ref, mk_ref, mvt_ref, mem_bias, tail_bias):
    start = pl.multiple_of(chunk * QROWS, QROWS)
    q2 = stack_heads(q_ref[pl.ds(start, QROWS), :] * HDIM ** (-0.5))

    def values_times(values_t, probs):
        low = probs.astype(LOW)
        return (
            dot(values_t[:HDIM], low[:, :QROWS]),
            dot(values_t[HDIM:], low[:, QROWS:]),
        )

    scores = dot_nt(mk_ref[...], q2) + mem_bias
    peak = jnp.max(scores, axis=0, keepdims=True)
    raised = jnp.exp(scores - peak)
    total = jnp.sum(raised, axis=0, keepdims=True)
    first, second = values_times(mvt_ref[...], raised)

    def update(block, scores, carry):
        peak, total, first, second = carry
        at = pl.multiple_of(block * KROWS, KROWS)
        new_peak = jnp.maximum(peak, jnp.max(scores, axis=0, keepdims=True))
        scale = jnp.exp(peak - new_peak)
        raised = jnp.exp(scores - new_peak)
        total = total * scale + jnp.sum(raised, axis=0, keepdims=True)
        add_first, add_second = values_times(vt_ref[:, pl.ds(at, KROWS)], raised)
        return (
            new_peak,
            total,
            first * scale[:, :QROWS] + add_first,
            second * scale[:, QROWS:] + add_second,
        )

    def block_scores(block):
        at = pl.multiple_of(block * KROWS, KROWS)
        return dot_nt(k_ref[pl.ds(at, KROWS), :], q2)

    full = chunk * QROWS // KROWS
    carry = lax.fori_loop(
        0, full, lambda b, c: update(b, block_scores(b), c), (peak, total, first, second)
    )
    scores = block_scores(full) + causal_bias(chunk, full, tail_bias)
    peak, total, first, second = update(full, scores, carry)
    inverse = 1.0 / total
    attended = jnp.concatenate([first * inverse[:, :QROWS], second * inverse[:, QROWS:]], axis=0)
    return attended, peak + jnp.log(total)


def chip_at(group, order, step):
    return sum(jnp.where(step == j, group.chip(*place), 0) for j, place in enumerate(order))


def open_kernel(
    hidden_ref, memory_ref, counts_ref, gain_ref, shift_ref, w_ref, b_query_ref, b_value_ref,
    q_ref, k_ref, v_ref, mk_ref, mv_ref, mem_normed_ref, mem_bias_ref, tail_bias_ref, w_t_ref,
    normed_out,
    rows_buf, flat_w, mem_wide, send, recv, out_sem,
):
    head = Group("head")
    gather = Gather(head, rows_buf, send, recv, 64)
    own = head.block(0, 0)

    def norm_rows(rows):
        normal, _ = normal_of(hidden_ref[rows].astype(WIDE))
        rows_buf[own, rows] = (normal * gain_ref[...] + shift_ref[...]).astype(LOW)

    row_tiles(BLOCK, norm_rows, 32)
    greet_all(head)
    gather.arrive(0, 0)
    width = q_ref.shape[1]
    slots = memory_ref.shape[0]
    for i in range(3):
        flat_w[:, i * width : (i + 1) * width] = w_ref[i]
    copies = []

    def project(*place):
        gather.sibling(*place)
        chip = head.chip(*place)
        out = pltpu.make_async_copy(
            rows_buf.at[pl.ds(chip * 2, 2)], normed_out.at[pl.ds(chip * 2, 2)], out_sem.at[len(copies)]
        )
        out.start()
        copies.append(out)
        rows = rows_buf[pl.ds(chip * 2, 2)].reshape(2 * BLOCK, rows_buf.shape[2])
        at = pl.ds(pl.multiple_of(chip * 2 * BLOCK, 2 * BLOCK), 2 * BLOCK)
        all_parts = dot(rows, flat_w[...])
        q_ref[at, :] = (all_parts[:, :width] + b_query_ref[...]).astype(LOW)
        k_ref[at, :] = all_parts[:, width : 2 * width].astype(LOW)
        v_ref[at, :] = (all_parts[:, 2 * width :] + b_value_ref[...]).astype(LOW)

    def side_work():
        mem_wide[...] = jnp.zeros_like(mem_wide)
        mem_wide[:slots, :] = memory_ref[...].astype(WIDE)

        def norm_memory(rows):
            normal, _ = normal_of(mem_wide[rows])
            mem_normed_ref[rows] = (normal * gain_ref[...] + shift_ref[...]).astype(LOW)

        row_tiles(MEMROWS, norm_memory, 32)
        mem = dot(mem_normed_ref[...], flat_w[:, width:])
        mk_ref[...] = mem[:, :width].astype(LOW)
        mv_ref[...] = (mem[:, width:] + b_value_ref[...]).astype(LOW)
        slot = lax.broadcasted_iota(jnp.int32, mem_bias_ref.shape, 0)
        mem_bias_ref[...] = jnp.where(slot < counts_ref[0, 0], 0.0, NEGATIVE)
        tail = slots - KROWS + lax.broadcasted_iota(jnp.int32, tail_bias_ref.shape, 0)
        tail_bias_ref[...] = jnp.where((tail < 0) | (tail < counts_ref[0, 1]), 0.0, NEGATIVE)
        for i in range(3):
            transpose_into(w_t_ref.at[pl.ds(i * width, width)], w_ref.at[i])

    side_work()
    project(0, 0)
    gather.arrive(-1, 0)
    gather.arrive(1, 0)
    gather.arrive(0, 1)
    project(-1, 0)
    project(1, 0)
    gather.arrive(2, 0)
    project(0, 1)
    gather.arrive(-1, 1)
    gather.arrive(1, 1)
    project(2, 0)
    project(-1, 1)
    project(1, 1)
    gather.arrive(2, 1)
    project(2, 1)
    gather.drain()
    for out in copies:
        out.wait()


def open_layer(hidden, memory, counts, gain, shift, w, b_query, b_value):
    rows, model = hidden.shape
    width = w.shape[2]
    part = jax.ShapeDtypeStruct((16 * rows, width), LOW)
    mem_part = jax.ShapeDtypeStruct((MEMROWS, width), LOW)
    sems = [pltpu.SemaphoreType.DMA((Gather.COPIES,))] * 2
    smem = pl.BlockSpec(memory_space=pltpu.SMEM)
    return pl.pallas_call(
        open_kernel,
        out_shape=(
            part, part, part, mem_part, mem_part,
            jax.ShapeDtypeStruct((MEMROWS, model), LOW),
            jax.ShapeDtypeStruct((MEMROWS, 1), WIDE),
            jax.ShapeDtypeStruct((KROWS, 1), WIDE),
            jax.ShapeDtypeStruct((3 * width, model), LOW),
            jax.ShapeDtypeStruct((16, rows, model), LOW),
        ),
        in_specs=[VMEM] * 2 + [smem] + [VMEM] * 5,
        out_specs=(VMEM,) * 9 + (ANY,),
        scratch_shapes=[
            pltpu.VMEM((16, rows, model), LOW),
            pltpu.VMEM((model, 3 * width), LOW),
            pltpu.VMEM((MEMROWS, model), WIDE),
        ] + sems + [pltpu.SemaphoreType.DMA((8,))],
        compiler_params=pltpu.CompilerParams(
            collective_id=0, has_side_effects=True, vmem_limit_bytes=VMEM_LIMIT
        ),
        name="open_layer",
    )(hidden, memory, counts, gain, shift, w, b_query, b_value)


def attend_kernel(
    q_ref, k_ref, v_ref, mk_ref, mv_ref, mem_bias_ref, tail_bias_ref, wo_ref,
    hidden_ref, b_out_ref, gain_ref, shift_ref, cot_ref, w_up_hbm,
    attn_t_ref, lse_ref, resid_ref, second_ref, w_up_t_ref, cot_out,
    vt_ref, mvt_ref, attn_ref, cot_buf, wu_ref, load_sem, out_sem, cot_send, cot_recv,
    total, stage, land, send, recv, near_stage, near_land,
):
    head, seq = Group("head"), Group("seq")
    reduce = Reduce(head, total, stage, land, send, recv, 128, (near_stage, near_land), resid_ref)
    gather = Gather(seq, cot_buf, cot_send, cot_recv, 128)
    load = pltpu.make_async_copy(w_up_hbm, wu_ref, load_sem)
    load.start()
    cot_buf[seq.me] = cot_ref[...]
    transpose_into(vt_ref, v_ref)
    transpose_into(mvt_ref, mv_ref)
    greet_all(head, seq)
    gather.arrive(0, 0)

    def step(k, carry):
        chip = chip_at(head, FAR_FIRST, k)
        start = pl.multiple_of(chip * QROWS, QROWS)
        attended, lse = attend_chunk(
            chip, q_ref, k_ref, vt_ref, mk_ref, mvt_ref, mem_bias_ref[...], tail_bias_ref[...]
        )
        attn_t_ref[:, pl.ds(start, QROWS)] = attended.astype(LOW)
        attn_ref[...] = attended.T.astype(LOW)
        lse_ref[chip] = lse
        mine = attn_ref[pl.ds(pl.multiple_of(head.core * BLOCK, BLOCK), BLOCK), :]
        other = attn_ref[pl.ds(pl.multiple_of((1 - head.core) * BLOCK, BLOCK), BLOCK), :]
        for at in range(0, total.shape[2], 512):
            near_stage[k, :, at : at + 512] = dot(other, wo_ref[:, at : at + 512]).astype(LOW)
        reduce.near_copy(k).start()
        for at in range(0, total.shape[2], 512):
            total[k, :, at : at + 512] = dot(mine, wo_ref[:, at : at + 512])
        for j, place in enumerate(FAR_FIRST[:-1]):
            @pl.when(k == j + 1)
            def _():
                reduce.settle(*place)

        @pl.when(k == 4)
        def _():
            gather.arrive(-1, 0)
            gather.arrive(1, 0)
            gather.arrive(0, 1)

        @pl.when(k == 6)
        def _():
            gather.arrive(2, 0)

        return carry

    lax.fori_loop(0, 8, step, 0)
    gather.arrive(-1, 1)
    gather.arrive(1, 1)
    load.wait()
    transpose_into(w_up_t_ref, wu_ref)
    reduce.settle(0, 0)

    def finish(rows):
        resid = hidden_ref[rows].astype(WIDE) + resid_ref[rows] + b_out_ref[...]
        resid_ref[rows] = resid
        normal, _ = normal_of(resid)
        second_ref[rows] = (normal * gain_ref[...] + shift_ref[...]).astype(LOW)

    row_tiles(BLOCK, finish, 32)
    gather.arrive(2, 1)
    out = pltpu.make_async_copy(cot_buf, cot_out, out_sem)
    out.start()
    gather.drain()
    reduce.drain()
    out.wait()


def attend_layer(
    q, k, v, mk, mv, mem_bias, tail_bias, wo, hidden, b_out, gain, shift, cot, w_up
):
    length, width = q.shape
    rows, model = hidden.shape
    units = w_up.shape[1]
    return pl.pallas_call(
        attend_kernel,
        out_shape=(
            jax.ShapeDtypeStruct((width, length), LOW),
            jax.ShapeDtypeStruct((length // QROWS, 1, 2 * QROWS), WIDE),
            jax.ShapeDtypeStruct((rows, model), WIDE),
            jax.ShapeDtypeStruct((rows, model), LOW),
            jax.ShapeDtypeStruct((units, model), LOW),
            jax.ShapeDtypeStruct((8, rows, model), LOW),
        ),
        in_specs=[VMEM] * 13 + [ANY],
        out_specs=(VMEM,) * 5 + (ANY,),
        scratch_shapes=[
            pltpu.VMEM((width, length), LOW),
            pltpu.VMEM((width, MEMROWS), LOW),
            pltpu.VMEM((QROWS, width), LOW),
            pltpu.VMEM((8, rows, model), LOW),
            pltpu.VMEM((model, units), LOW),
            pltpu.SemaphoreType.DMA,
            pltpu.SemaphoreType.DMA,
        ] + [pltpu.SemaphoreType.DMA((Gather.COPIES,))] * 2 + Reduce.scratch(model, True, True),
        compiler_params=pltpu.CompilerParams(
            collective_id=1, has_side_effects=True, vmem_limit_bytes=VMEM_LIMIT
        ),
        name="attend_layer",
    )(
        q, k, v, mk, mv, mem_bias, tail_bias, wo, hidden, b_out, gain, shift,
        cot, w_up,
    )


def gelu_parts(u):
    square = u * u
    t = jnp.tanh(0.7978845608 * (u + 0.044715 * (square * u)))
    half = 0.5 * (1.0 + t)
    slope = half + 0.5 * u * (1.0 - t * t) * (0.7978845608 * (1.0 + 0.134145 * square))
    return u * half, slope


def fold_rows(values):
    return jnp.sum(values.reshape(values.shape[0] // 8, 8, values.shape[1]), axis=0)


def feed_kernel(
    second_ref, w_up_hbm, w_up_t_hbm, w_down_hbm, cot_hbm, up_bias_ref, resid_ref, gain_ref,
    cot_ref,
    grad_resid_ref, sums_ref, branch_hbm, grad_w_ref, grad_b_up_ref,
    rows_buf, wu_ref, wut_ref, wd_ref, cot_buf, act_ref, back_ref, pre_ref, fold_ref, sum_fold, branch_buf,
    load_sem, branch_sem, send, recv,
    total, land, rsend, rrecv,
    w_total, w_land, w_send, w_recv, w_near_stage, w_near_land,
):
    head, seq = Group("head"), Group("seq")
    gather = Gather(seq, rows_buf, send, recv, 64)
    reduce = Reduce(seq, total, None, land, rsend, rrecv, 128, None, grad_resid_ref)
    w_reduce = Reduce(head, w_total, None, w_land, w_send, w_recv, 112, (w_near_stage, w_near_land), grad_w_ref)
    loads = [
        pltpu.make_async_copy(src, dst, load_sem.at[i])
        for i, (src, dst) in enumerate(
            (
                (cot_hbm, cot_buf), (w_down_hbm, wd_ref), (w_up_hbm, wu_ref), (w_up_t_hbm, wut_ref),
            )
        )
    ]
    for load in loads:
        load.start()
    own = seq.block(0, 0)
    rows_buf[own] = second_ref[...]
    fold_ref[...] = jnp.zeros_like(fold_ref)
    greet_all(head, seq)
    gather.arrive(0, 0)
    loads[0].wait()
    loads[1].wait()
    units = act_ref.shape[2]
    model = rows_buf.shape[2]
    bias_at = pl.ds(pl.multiple_of(own * units, units), units)

    def cot_times(i, carry):
        pairs = cot_buf[pl.ds(2 * i, 2)].reshape(2 * BLOCK, model)
        for at in range(0, units, 256):
            part = dot_nt(pairs, wd_ref[at : at + 256, :]).astype(LOW)
            back_ref[pl.ds(2 * i, 2), :, at : at + 256] = part.reshape(2, BLOCK, 256)
        return carry

    def feed(*place):
        block = seq.block(*place)
        pre_ref[...] = dot(rows_buf[block], wu_ref[...]) + up_bias_ref[:, bias_at]

        def bend(rows):
            activated, slope = gelu_parts(pre_ref[rows])
            grad_pre = back_ref[block, rows].astype(WIDE) * slope
            act_ref[block, rows] = activated.astype(LOW)
            back_ref[block, rows] = grad_pre.astype(LOW)
            fold_ref[...] += fold_rows(grad_pre)

        row_tiles(BLOCK, bend)
        k = FAR_FIRST.index(place)
        for at in range(0, model, 512):
            total[k, :, at : at + 512] = dot(back_ref[block], wut_ref[:, at : at + 512]).astype(LOW)

    lax.fori_loop(0, 4, cot_times, 0)
    loads[2].wait()
    loads[3].wait()
    feed(0, 0)
    gather.arrive(-1, 0)
    gather.arrive(1, 0)
    gather.arrive(0, 1)
    feed(-1, 0)
    gather.arrive(2, 0)
    feed(1, 0)
    gather.arrive(-1, 1)
    gather.arrive(1, 1)
    feed(0, 1)
    feed(2, 0)
    feed(-1, 1)
    feed(1, 1)
    gather.arrive(2, 1)
    feed(2, 1)
    reduce.settle(2, 1)
    reduce.settle(2, 0)
    grad_b_up_ref[...] = jnp.sum(fold_ref[...], axis=0, keepdims=True)

    def weights(k, carry):
        chip = chip_at(head, FAR_FIRST, k)

        def part(core):
            at = pl.ds(pl.multiple_of(chip * 2 * BLOCK + core * BLOCK, BLOCK), BLOCK)
            length = 8 * BLOCK
            up = dot_tn(
                rows_buf[:, :, at].reshape(length, BLOCK), back_ref[...].reshape(length, units)
            )
            down = dot_tn(
                cot_buf[:, :, at].reshape(length, BLOCK), act_ref[...].reshape(length, units)
            )
            return up.astype(LOW), down.astype(LOW)

        w_near_stage[k, :, :units], w_near_stage[k, :, units:] = part(1 - head.core)
        w_reduce.near_copy(k).start()
        w_total[k, :, :units], w_total[k, :, units:] = part(head.core)
        for j, place in enumerate(FAR_FIRST[:6]):
            @pl.when(k == j + 1)
            def _():
                w_reduce.settle(*place)

        @pl.when(k == 2)
        def _():
            reduce.settle(1, 1)
            reduce.settle(-1, 1)

        @pl.when(k == 5)
        def _():
            reduce.settle(1, 0)
            reduce.settle(-1, 0)

        return carry

    lax.fori_loop(0, 8, weights, 0)
    branch_copies = []

    def branch(i):
        slot = i % 2
        if i >= 2:
            branch_copies[i - 2].wait()
        for at in range(0, model, 512):
            branch_buf[slot, :, at : at + 512] = dot(act_ref[i], wd_ref[:, at : at + 512]).astype(LOW)
        copy = pltpu.make_async_copy(branch_buf.at[slot], branch_hbm.at[i], branch_sem.at[i])
        copy.start()
        branch_copies.append(copy)

    for i in range(4):
        branch(i)
    reduce.settle(0, 1)
    w_reduce.settle(0, 1)
    for i in range(4, 8):
        branch(i)
    reduce.settle(0, 0)
    sum_fold[...] = jnp.zeros_like(sum_fold)

    def back(rows):
        normal, rstd = normal_of(resid_ref[rows])
        incoming = grad_resid_ref[rows]
        scaled = incoming * gain_ref[...]
        inner = jnp.mean(scaled, axis=-1, keepdims=True)
        along = jnp.mean(scaled * normal, axis=-1, keepdims=True)
        cot = cot_ref[rows].astype(WIDE)
        grad = cot + rstd * (scaled - inner - normal * along)
        grad_resid_ref[rows] = grad
        for i, value in enumerate((grad, incoming * normal, incoming, cot)):
            sum_fold[i] += fold_rows(value)

    row_tiles(BLOCK, back)
    sums_ref[...] = jnp.sum(sum_fold[...], axis=1)
    w_reduce.settle(0, 0)
    for copy in branch_copies[-2:]:
        copy.wait()
    gather.drain()
    reduce.drain()
    w_reduce.drain()


def feed_layer(second, w_up, w_up_t, w_down, cot_all, up_bias, resid, gain, cot):
    rows, model = second.shape
    units = w_up.shape[1]
    gather_sems = [pltpu.SemaphoreType.DMA((Gather.COPIES,))] * 2
    return pl.pallas_call(
        feed_kernel,
        out_shape=(
            jax.ShapeDtypeStruct((rows, model), WIDE),
            jax.ShapeDtypeStruct((4, model), WIDE),
            jax.ShapeDtypeStruct((8, rows, model), LOW),
            jax.ShapeDtypeStruct((rows, 2 * units), WIDE),
            jax.ShapeDtypeStruct((1, units), WIDE),
        ),
        in_specs=[VMEM] + [ANY] * 4 + [VMEM] * 4,
        out_specs=(VMEM, VMEM, ANY, VMEM, VMEM),
        scratch_shapes=[
            pltpu.VMEM((8, rows, model), LOW),
            pltpu.VMEM((model, units), LOW),
            pltpu.VMEM((units, model), LOW),
            pltpu.VMEM((units, model), LOW),
            pltpu.VMEM((8, rows, model), LOW),
            pltpu.VMEM((8, rows, units), LOW),
            pltpu.VMEM((8, rows, units), LOW),
            pltpu.VMEM((rows, units), WIDE),
            pltpu.VMEM((8, units), WIDE),
            pltpu.VMEM((4, 8, model), WIDE),
            pltpu.VMEM((2, rows, model), LOW),
            pltpu.SemaphoreType.DMA((4,)),
            pltpu.SemaphoreType.DMA((8,)),
        ] + gather_sems + Reduce.scratch(model, False, False) + Reduce.scratch(2 * units, False, True),
        compiler_params=pltpu.CompilerParams(
            collective_id=2, has_side_effects=True, vmem_limit_bytes=VMEM_LIMIT
        ),
        name="feed_layer",
    )(second, w_up, w_up_t, w_down, cot_all, up_bias, resid, gain, cot)


def attend_back_chunk(
    chunk, q_ref, k_ref, kt_ref, v_ref, mk_ref, mkt_ref, mv_ref, mem_bias, tail_bias,
    attn_t_ref, lse_ref, grad_rows, dk_ref, dv_ref, dmk_ref, dmv_ref,
):
    start = pl.multiple_of(chunk * QROWS, QROWS)
    q2 = stack_heads(q_ref[pl.ds(start, QROWS), :] * HDIM ** (-0.5))
    g2 = stack_heads(grad_rows)
    product = grad_rows.astype(WIDE).T * attn_t_ref[:, pl.ds(start, QROWS)].astype(WIDE)
    inner = jnp.concatenate(
        [
            jnp.sum(product[:HDIM], axis=0, keepdims=True),
            jnp.sum(product[HDIM:], axis=0, keepdims=True),
        ],
        axis=1,
    )
    lse = lse_ref[chunk]

    def piece(scores, values, keys_t):
        probs = jnp.exp(scores - lse)
        grad_probs = dot_nt(values, g2)
        grad_scores = (probs * (grad_probs - inner)).astype(LOW)
        return (
            dot(probs.astype(LOW), g2),
            dot(grad_scores, q2),
            dot(keys_t[:HDIM], grad_scores[:, :QROWS]),
            dot(keys_t[HDIM:], grad_scores[:, QROWS:]),
        )

    dv, dk, first, second = piece(
        dot_nt(mk_ref[...], q2) + mem_bias, mv_ref[...], mkt_ref[...]
    )
    dmv_ref[...] += dv
    dmk_ref[...] += dk

    def block_step(block, bias, carry):
        first, second = carry
        at = pl.multiple_of(block * KROWS, KROWS)
        scores = dot_nt(k_ref[pl.ds(at, KROWS), :], q2)
        if bias is not None:
            scores = scores + bias
        dv, dk, add_first, add_second = piece(
            scores, v_ref[pl.ds(at, KROWS), :], kt_ref[:, pl.ds(at, KROWS)]
        )
        dv_ref[pl.ds(at, KROWS), :] += dv
        dk_ref[pl.ds(at, KROWS), :] += dk
        return first + add_first, second + add_second

    full = chunk * QROWS // KROWS
    carry = lax.fori_loop(0, full, lambda b, c: block_step(b, None, c), (first, second))
    first, second = block_step(full, causal_bias(chunk, full, tail_bias), carry)
    return jnp.concatenate([first, second], axis=0) * HDIM ** (-0.5)


def grad_kernel(
    grad_resid_ref, resid_ref, b_down_ref, branch_hbm, wo_ref,
    q_ref, k_ref, v_ref, mk_ref, mv_ref, mem_bias_ref, tail_bias_ref, attn_t_ref, lse_ref,
    out_ref, own_ref, own_t_ref, mem_ref, mem_t_ref, grad_wo_ref, sums_ref,
    rows_buf, kt_ref, mkt_ref, dk_ref, dv_ref, dmk_ref, dmv_ref, wo_sum, branch_sum, fold_ref,
    load_sem, send, recv, total, land, rsend, rrecv,
):
    head, seq = Group("head"), Group("seq")
    gather = Gather(head, rows_buf, send, recv, 96)
    reduce = Reduce(seq, total, None, land, rsend, rrecv, 128, None, branch_sum)
    loads = [
        pltpu.make_async_copy(branch_hbm.at[seq.block(*place)], total.at[k], load_sem.at[k])
        for k, place in enumerate(FAR_FIRST)
    ]
    for load in loads:
        load.start()
    own = head.block(0, 0)
    rows_buf[own] = grad_resid_ref[...].astype(LOW)
    greet_all(head, seq)
    gather.arrive(0, 0)
    loads[0].wait()
    reduce.settle(2, 1)
    loads[1].wait()
    reduce.settle(2, 0)
    transpose_into(kt_ref, k_ref)
    transpose_into(mkt_ref, mk_ref)
    for ref in (dk_ref, dv_ref, dmk_ref, dmv_ref, wo_sum, fold_ref):
        ref[...] = jnp.zeros_like(ref)
    width, model = wo_ref.shape
    for load in loads[2:]:
        load.wait()

    def step(k, carry):
        @pl.when(k == 0)
        def _():
            gather.sibling(0, 0)

        @pl.when(k == 1)
        def _():
            gather.arrive(-1, 0)
            gather.arrive(1, 0)
            reduce.settle(1, 1)
            reduce.settle(-1, 1)
            gather.arrive(0, 1)
            gather.sibling(-1, 0)

        @pl.when(k == 2)
        def _():
            reduce.settle(1, 0)
            reduce.settle(-1, 0)
            gather.sibling(1, 0)

        @pl.when(k == 3)
        def _():
            gather.arrive(2, 0)
            gather.sibling(0, 1)

        @pl.when(k == 4)
        def _():
            gather.arrive(-1, 1)
            gather.arrive(1, 1)
            gather.sibling(2, 0)

        @pl.when(k == 5)
        def _():
            reduce.settle(0, 1)
            gather.sibling(-1, 1)

        @pl.when(k == 6)
        def _():
            gather.arrive(2, 1)
            gather.sibling(1, 1)

        @pl.when(k == 7)
        def _():
            gather.sibling(2, 1)

        chip = chip_at(head, NEAR_FIRST, k)
        at = pl.ds(pl.multiple_of(chip * QROWS, QROWS), QROWS)
        rows = rows_buf[pl.ds(chip * 2, 2)].reshape(QROWS, model)
        grad_rows = dot_nt(rows, wo_ref[...]).astype(LOW)
        wo_sum[...] += dot(attn_t_ref[:, at], rows)
        dq = attend_back_chunk(
            chip, q_ref, k_ref, kt_ref, v_ref, mk_ref, mkt_ref, mv_ref,
            mem_bias_ref[...], tail_bias_ref[...], attn_t_ref, lse_ref,
            grad_rows, dk_ref, dv_ref, dmk_ref, dmv_ref,
        ).astype(LOW)
        own_t_ref[:width, at] = dq
        own_ref[at, :width] = dq.T
        return carry

    lax.fori_loop(0, 8, step, 0)

    def finish_keys(i, carry):
        at = pl.ds(pl.multiple_of(i * 256, 256), 256)
        dk = dk_ref[at, :].astype(LOW)
        dv = dv_ref[at, :].astype(LOW)
        own_ref[at, width : 2 * width] = dk
        own_ref[at, 2 * width :] = dv
        own_t_ref[width : 2 * width, at] = dk.T
        own_t_ref[2 * width :, at] = dv.T
        fold_ref[...] += fold_rows(own_ref[at, :].astype(WIDE))
        return carry

    lax.fori_loop(0, q_ref.shape[0] // 256, finish_keys, 0)
    for i, ref in enumerate((dmk_ref, dmv_ref)):
        low = ref[...].astype(LOW)
        mem_ref[:, i * width : (i + 1) * width] = low
        mem_t_ref[i * width : (i + 1) * width, :] = low.T
    fold_ref[:, width:] += fold_rows(mem_ref[...].astype(WIDE))
    sums_ref[...] = jnp.sum(fold_ref[...], axis=0, keepdims=True)
    grad_wo_ref[...] = wo_sum[...].astype(LOW)
    reduce.settle(0, 0)

    def finish(rows):
        out_ref[rows] = (resid_ref[rows] + branch_sum[rows] + b_down_ref[...]).astype(LOW)

    row_tiles(BLOCK, finish)
    gather.drain()
    reduce.drain()


def grad_layer(
    grad_resid, resid, b_down, branch, wo, q, k, v, mk, mv, mem_bias, tail_bias, attn_t, lse,
):
    rows, model = grad_resid.shape
    length, width = q.shape
    return pl.pallas_call(
        grad_kernel,
        out_shape=(
            jax.ShapeDtypeStruct((rows, model), LOW),
            jax.ShapeDtypeStruct((length, 3 * width), LOW),
            jax.ShapeDtypeStruct((3 * width, length), LOW),
            jax.ShapeDtypeStruct((MEMROWS, 2 * width), LOW),
            jax.ShapeDtypeStruct((2 * width, MEMROWS), LOW),
            jax.ShapeDtypeStruct((width, model), LOW),
            jax.ShapeDtypeStruct((1, 3 * width), WIDE),
        ),
        in_specs=[VMEM] * 3 + [ANY] + [VMEM] * 10,
        out_specs=(VMEM,) * 7,
        scratch_shapes=[
            pltpu.VMEM((16, rows, model), LOW),
            pltpu.VMEM((width, length), LOW),
            pltpu.VMEM((width, MEMROWS), LOW),
            pltpu.VMEM((length, width), WIDE),
            pltpu.VMEM((length, width), WIDE),
            pltpu.VMEM((MEMROWS, width), WIDE),
            pltpu.VMEM((MEMROWS, width), WIDE),
            pltpu.VMEM((width, model), WIDE),
            pltpu.VMEM((rows, model), WIDE),
            pltpu.VMEM((8, 3 * width), WIDE),
            pltpu.SemaphoreType.DMA((8,)),
        ] + [pltpu.SemaphoreType.DMA((Gather.COPIES,))] * 2 + Reduce.scratch(model, False, False),
        compiler_params=pltpu.CompilerParams(
            collective_id=3, has_side_effects=True, vmem_limit_bytes=VMEM_LIMIT
        ),
        name="grad_layer",
    )(
        grad_resid, resid, b_down, branch, wo, q, k, v, mk, mv, mem_bias, tail_bias, attn_t, lse,
    )


SUM_ROWS = 16


def close_kernel(
    own_ref, own_t_ref, mem_ref, mem_t_ref, grad_wo_ref, mem_normed_ref, normed_hbm, w_t_ref,
    gain_ref, shift_ref, bias_sums_ref, feed_sums_ref, b_up_ref,
    grad_normed_ref, grad_w_ref, small_ref,
    rows_buf, mem_pad, norm_sums, pay_ref, core_land, pay_half, pay_land, seq_land,
    core_send, core_recv, pay_send, pay_recv, seq_send, seq_recv, all_send, all_recv, load_sem,
    total, stage, land, send, recv, near_stage, near_land,
    w_total, w_stage, w_land, w_send, w_recv, g_send, g_recv,
):
    head, seq = Group("head"), Group("seq")
    reduce = Reduce(head, total, stage, land, send, recv, 112, (near_stage, near_land), grad_normed_ref)
    w_reduce = Reduce(seq, w_total, w_stage, w_land, w_send, w_recv, 128, None, w_total.at[7])
    gather = Gather(seq, grad_w_ref, g_send, g_recv, 128)
    plane = Plane(head)
    pay = Spread(plane, pay_send, pay_recv)
    across = Spread(seq, seq_send, seq_recv)
    back = Spread(plane, all_send, all_recv)
    load = pltpu.make_async_copy(normed_hbm, rows_buf, load_sem)
    load.start()
    width = grad_wo_ref.shape[0]
    model = rows_buf.shape[2]
    length = own_ref.shape[0]
    wide = model // 2
    share = model // head.size
    mem_pad[...] = jnp.zeros_like(mem_pad)
    mem_pad[pl.ds(width, 2 * width), :] = mem_t_ref[...]
    norm_sums[...] = jnp.zeros_like(norm_sums)
    greet_everyone(head, plane, seq)

    def chunk(k):
        chip = head.chip(*FAR_FIRST[k])

        def part(core):
            at = pl.ds(pl.multiple_of(chip * QROWS + core * BLOCK, BLOCK), BLOCK)
            return own_ref[at, :]

        mine, other = part(head.core), part(1 - head.core)
        for at in range(0, model, 512):
            near_stage[k, :, at : at + 512] = dot(other, w_t_ref[:, at : at + 512]).astype(LOW)
        reduce.near_copy(k).start()
        for at in range(0, model, 512):
            total[k, :, at : at + 512] = dot(mine, w_t_ref[:, at : at + 512])

    def weights(k, carry):
        target = chip_at(seq, FAR_FIRST, k)
        part, side = target // 2, target % 2
        columns = pl.ds(pl.multiple_of(side * wide, wide), wide)

        @pl.when(part < 3)
        def _():
            at = pl.ds(pl.multiple_of(part * width, width), width)
            term = dot(
                own_t_ref[at, :], rows_buf[:, :, columns].reshape(length, wide)
            ) + dot(mem_pad[at, :], mem_normed_ref[:, columns])
            w_total[k] = term
            flat = w_t_ref[at, columns].astype(WIDE)
            norm_sums[0:1, columns] += jnp.sum(flat * term, axis=0, keepdims=True)

        @pl.when(part == 3)
        def _():
            w_total[k] = grad_wo_ref[:, columns].astype(WIDE)

        return carry

    def shift_sums():
        sums = bias_sums_ref[...]
        high = sums.astype(LOW)
        rest = (sums - high.astype(WIDE)).astype(LOW)
        pair = jnp.concatenate([high, rest, jnp.zeros((14, sums.shape[1]), LOW)], axis=0)
        both = dot(pair, w_t_ref[...])
        norm_sums[1:2, :] = both[0:1] + both[1:2]

    def core_copy(i, src, dst):
        return pltpu.make_async_remote_copy(
            src_ref=src,
            dst_ref=dst,
            send_sem=core_send.at[i],
            recv_sem=core_recv.at[i],
            device_id=head.device(0, 0, 1),
            device_id_type=MESH,
        )

    def half_of(core):
        return pay_ref.at[:, pl.ds(pl.multiple_of(core * wide, wide), wide)]

    def pay_part(i):
        return pay_half.at[:, pl.ds(pl.multiple_of(i * share, share), share)]

    def pay_core():
        return core_copy(0, half_of(1 - head.core), core_land)

    def pay_whole():
        return core_copy(1, small_ref.at[head.core], small_ref.at[head.core])

    def pay_start():
        pay_ref[:MEMROWS, :] = dot(mem_ref[...], w_t_ref[width:, :]).astype(LOW)
        at_gain = norm_sums[0:1, :] - shift_ref[...] * norm_sums[1:2, :]
        rows = [at_gain / gain_ref[...], norm_sums[1:2, :], feed_sums_ref[...]]
        units = b_up_ref.shape[1]
        per_row = model // units
        for r in range(8 // per_row):
            row = [jnp.where(seq.me == r * per_row + c, b_up_ref[...], 0.0) for c in range(per_row)]
            rows.append(jnp.concatenate(row, axis=1))
        rows.append(jnp.zeros((SUM_ROWS - 6 - 8 // per_row, model), WIDE))
        pay_ref[MEMROWS:, :] = jnp.concatenate(rows, axis=0).astype(LOW)
        pay_core().start()

    def pay_send_parts():
        pay_core().wait_recv()
        pay_half[...] = (half_of(head.core)[...].astype(WIDE) + core_land[...].astype(WIDE)).astype(LOW)
        pay_land[plane.me] = pay_part(plane.me)[...]
        pay.start(pay_part, pay_land)

    def pay_sum():
        pay.wait(pay_land)
        sums = pay_land[0].astype(WIDE)
        for i in range(1, 8):
            sums += pay_land[i].astype(WIDE)
        small_ref[head.core, plane.me, :MEMROWS, :] = sums[:MEMROWS].astype(LOW)
        used = 6 + 8 * b_up_ref.shape[1] // model
        rows = [sums[MEMROWS : MEMROWS + used]]
        rows += [bias_sums_ref[:, i * width : (i + 1) * width] for i in range(3)]
        rows.append(jnp.zeros((SUM_ROWS - 3 - used, share), WIDE))
        seq_land[seq.me] = jnp.concatenate(rows, axis=0).astype(LOW)
        across.start(lambda i: seq_land.at[seq.me], seq_land)

    def pay_back():
        across.wait(seq_land)
        sums = seq_land[0].astype(WIDE)
        for i in range(1, 8):
            sums += seq_land[i].astype(WIDE)
        small_ref[head.core, plane.me, MEMROWS:, :] = sums.astype(LOW)
        back.start(lambda i: small_ref.at[head.core, plane.me], small_ref.at[head.core])

    def pay_end():
        back.wait(small_ref.at[head.core])
        pay_whole().start()

    chunk(0)
    chunk(1)
    load.wait()
    lax.fori_loop(0, 2, weights, 0)
    w_reduce.settle(2, 1)
    w_reduce.settle(2, 0)
    reduce.settle(2, 1)
    reduce.settle(2, 0)
    lax.fori_loop(2, 4, weights, 0)
    w_reduce.settle(1, 1)
    w_reduce.settle(-1, 1)
    chunk(2)
    chunk(3)
    lax.fori_loop(4, 6, weights, 0)
    w_reduce.settle(1, 0)
    w_reduce.settle(-1, 0)
    reduce.settle(1, 1)
    reduce.settle(-1, 1)
    lax.fori_loop(6, 7, weights, 0)
    w_reduce.settle(0, 1)
    lax.fori_loop(7, 8, weights, 0)
    shift_sums()
    pay_start()
    chunk(4)
    chunk(5)
    pay_send_parts()
    reduce.settle(1, 0)
    reduce.settle(-1, 0)
    w_reduce.settle(0, 0)
    grad_w_ref[seq.me] = w_total[7].astype(LOW)
    gather.arrive(0, 0)
    chunk(6)
    chunk(7)
    gather.arrive(-1, 0)
    gather.arrive(1, 0)
    gather.arrive(0, 1)
    pay_sum()
    reduce.settle(0, 1)
    gather.arrive(2, 0)
    gather.arrive(-1, 1)
    gather.arrive(1, 1)
    pay_back()
    reduce.settle(0, 0)
    pay_end()
    gather.arrive(2, 1)
    core_copy(1, small_ref.at[1 - head.core], small_ref.at[1 - head.core]).wait_recv()
    pay_core().wait_send()
    pay_whole().wait_send()
    pay.drain(pay_part, pay_land)
    across.drain(lambda i: seq_land.at[seq.me], seq_land)
    back.drain(lambda i: small_ref.at[head.core, plane.me], small_ref.at[head.core])
    gather.drain()
    w_reduce.drain()
    reduce.drain()


def close_layer(
    own, own_t, mem, mem_t, grad_wo, mem_normed, normed_all, w_t, gain, shift, bias_sums,
    feed_sums, b_up,
):
    rows, model = normed_all.shape[1:]
    width = grad_wo.shape[0]
    sems = [pltpu.SemaphoreType.DMA((Gather.COPIES,))] * 2
    pay_rows = MEMROWS + SUM_ROWS
    return pl.pallas_call(
        close_kernel,
        out_shape=(
            jax.ShapeDtypeStruct((rows, model), WIDE),
            jax.ShapeDtypeStruct((8, width, model // 2), LOW),
            jax.ShapeDtypeStruct((2, 8, pay_rows, model // 16), LOW),
        ),
        in_specs=[VMEM] * 6 + [ANY] + [VMEM] * 6,
        out_specs=(VMEM,) * 3,
        scratch_shapes=[
            pltpu.VMEM((16, rows, model), LOW),
            pltpu.VMEM((3 * width, MEMROWS), LOW),
            pltpu.VMEM((8, model), WIDE),
            pltpu.VMEM((pay_rows, model), LOW),
            pltpu.VMEM((pay_rows, model // 2), LOW),
            pltpu.VMEM((pay_rows, model // 2), LOW),
            pltpu.VMEM((8, pay_rows, model // 16), LOW),
            pltpu.VMEM((8, SUM_ROWS, model // 16), LOW),
            pltpu.SemaphoreType.DMA((2,)),
            pltpu.SemaphoreType.DMA((2,)),
            pltpu.SemaphoreType.DMA((8,)),
            pltpu.SemaphoreType.DMA((8,)),
            pltpu.SemaphoreType.DMA((8,)),
            pltpu.SemaphoreType.DMA((8,)),
            pltpu.SemaphoreType.DMA((8,)),
            pltpu.SemaphoreType.DMA((8,)),
            pltpu.SemaphoreType.DMA,
        ] + Reduce.scratch(model, True, True) + Reduce.scratch(model // 2, True, False) + sems,
        compiler_params=pltpu.CompilerParams(
            collective_id=4, has_side_effects=True, vmem_limit_bytes=VMEM_LIMIT
        ),
        name="close_layer",
    )(
        own, own_t, mem, mem_t, grad_wo, mem_normed, normed_all, w_t, gain, shift, bias_sums,
        feed_sums, b_up,
    )


def finish_kernel(
    grad_normed_ref, hidden_ref, grad_resid_ref, gain_ref, grad_w_ref, small_ref, memory_ref,
    feed_w_ref, output_ref,
    out_ref, grad_hidden_ref, grad_memory_ref, grad_qkv_ref, b_query_ref, b_value_ref, grad_wo_ref,
    b_out_ref, gain_one_ref, shift_one_ref, gain_two_ref, shift_two_ref,
    w_up_ref, b_up_ref, w_down_ref, b_down_ref,
    mem_wide, spread_ref,
):
    share = small_ref.shape[3]
    for i in range(16):
        spread_ref[:, i * share : (i + 1) * share] = small_ref[i // 8, i % 8].astype(WIDE)

    def norm_back(values, incoming):
        normal, rstd = normal_of(values)
        scaled = incoming * gain_ref[...]
        inner = jnp.mean(scaled, axis=-1, keepdims=True)
        along = jnp.mean(scaled * normal, axis=-1, keepdims=True)
        return rstd * (scaled - inner - normal * along)

    def back(rows):
        grad_hidden = grad_resid_ref[rows] + norm_back(
            hidden_ref[rows].astype(WIDE), grad_normed_ref[rows]
        )
        grad_hidden_ref[rows] = grad_hidden[:, None, :]

    row_tiles(hidden_ref.shape[0], back, 32)
    slots = memory_ref.shape[0]
    mem_wide[...] = jnp.zeros_like(mem_wide)
    mem_wide[:slots, :] = memory_ref[...].astype(WIDE)

    def back_memory(rows):
        mem_wide[rows] = norm_back(mem_wide[rows], spread_ref[rows])

    row_tiles(MEMROWS, back_memory, 32)
    grad_memory_ref[...] = mem_wide[:slots, :][:, None, :]
    out_ref[...] = output_ref[...]
    wide, units = grad_w_ref.shape[2], w_up_ref.shape[1]
    for i in range(3):
        for j in range(2):
            grad_qkv_ref[i, j * wide : (j + 1) * wide, :] = grad_w_ref[2 * i + j].astype(WIDE).T
    for j in range(2):
        grad_wo_ref[:, j * wide : (j + 1) * wide] = grad_w_ref[6 + j].astype(WIDE)
    w_up_ref[...] = feed_w_ref[:, :units]
    w_down_ref[...] = feed_w_ref[:, units:].T
    sums = [spread_ref[MEMROWS + i : MEMROWS + i + 1, :] for i in range(SUM_ROWS)]
    ordered = (gain_one_ref, shift_one_ref, b_out_ref, gain_two_ref, shift_two_ref, b_down_ref)
    for ref, row in zip(ordered, sums):
        ref[...] = row
    model = b_out_ref.shape[1]
    for i in range(4):
        b_up_ref[:, i * model : (i + 1) * model] = sums[6 + i]
    index = lax.axis_index("head")
    mine = small_ref[index % 2, index // 2].astype(WIDE)
    b_query_ref[...] = mine[MEMROWS + 10 : MEMROWS + 11, :]
    b_value_ref[...] = mine[MEMROWS + 12 : MEMROWS + 13, :]


def finish_layer(
    grad_normed, hidden, grad_resid, gain, grad_w, small, memory, feed_w, output
):
    rows, model = hidden.shape
    width, units = grad_w.shape[1], feed_w.shape[1] // 2
    wide = lambda *shape: jax.ShapeDtypeStruct(shape, WIDE)
    return pl.pallas_call(
        finish_kernel,
        out_shape=(
            jax.ShapeDtypeStruct((rows, model), LOW), wide(rows, 1, model), wide(memory.shape[0], 1, model),
            wide(3, model, width), wide(1, width), wide(1, width), wide(width, model),
            wide(1, model), wide(1, model), wide(1, model), wide(1, model), wide(1, model),
            wide(rows, units), wide(1, 8 * units), wide(units, rows), wide(1, model),
        ),
        in_specs=[VMEM] * 9,
        out_specs=(VMEM,) * 16,
        scratch_shapes=[
            pltpu.VMEM((MEMROWS, model), WIDE),
            pltpu.VMEM((MEMROWS + SUM_ROWS, model), WIDE),
        ],
        compiler_params=pltpu.CompilerParams(vmem_limit_bytes=VMEM_LIMIT),
        name="finish_layer",
    )(grad_normed, hidden, grad_resid, gain, grad_w, small, memory, feed_w, output)


def on_device(
    hidden, memory, counts, w_qkv, b_query, b_value, output_weight, b_out,
    gain_one, shift_one, gain_two, shift_two, w_up, up_bias, w_down, b_down, cotangent,
):
    hidden, memory, cot = hidden[:, 0], memory[:, 0], cotangent[:, 0]
    model = hidden.shape[1]
    width = w_qkv.shape[2]
    w_parts = jnp.transpose(w_qkv, (1, 0, 2))
    gain_one, shift_one, gain_two, shift_two, b_out, b_down, b_query, b_value, up_bias = (
        vector[None]
        for vector in (
            gain_one, shift_one, gain_two, shift_two, b_out, b_down, b_query, b_value, up_bias
        )
    )
    q, k, v, mk, mv, mem_normed, mem_bias, tail_bias, w_t, normed_all = open_layer(
        hidden, memory, counts, gain_one, shift_one, w_parts, b_query, b_value
    )
    attn_t, lse, resid, second, w_up_t, cot_all = attend_layer(
        q, k, v, mk, mv, mem_bias, tail_bias, output_weight, hidden, b_out, gain_two, shift_two,
        cot, w_up,
    )
    grad_resid, feed_sums, branch, feed_w, grad_b_up = feed_layer(
        second, w_up, w_up_t, w_down, cot_all, up_bias, resid, gain_two, cot
    )
    output, own, own_t, mem, mem_t, grad_wo, bias_sums = grad_layer(
        grad_resid, resid, b_down, branch, output_weight,
        q, k, v, mk, mv, mem_bias, tail_bias, attn_t, lse,
    )
    grad_normed, grad_w, small = close_layer(
        own, own_t, mem, mem_t, grad_wo, mem_normed, normed_all, w_t, gain_one, shift_one,
        bias_sums, feed_sums, grad_b_up,
    )
    outs = finish_layer(
        grad_normed, hidden, grad_resid, gain_one, grad_w, small, memory, feed_w, output
    )
    output, grad_hidden, grad_memory, grad_w_qkv, *rest = outs
    rest = [part[0] if part.shape[0] == 1 else part for part in rest]
    return (
        output[:, None],
        grad_hidden,
        grad_memory,
        jnp.transpose(grad_w_qkv, (1, 0, 2)),
        *rest,
    )


def solution(mesh):
    return jax.shard_map(
        on_device,
        mesh=mesh,
        in_specs=(
            P("head", "seq", None),
            P(None, "seq", None),
            P("seq", None),
            P(None, None, "head"),
            P("head"),
            P("head"),
            P("head", None),
            P(),
            P(),
            P(),
            P(),
            P(),
            P(None, "seq"),
            P(),
            P("seq", None),
            P(),
            P("head", "seq", None),
        ),
        out_specs=(
            P("head", "seq", None),
            P("head", "seq", None),
            P(None, "seq", None),
            P(None, None, "head"),
            P("head"),
            P("head"),
            P("head", None),
            P(),
            P(),
            P(),
            P(),
            P(),
            P("head", "seq"),
            P(),
            P("seq", "head"),
            P(),
        ),
        check_vma=False,
    )
```

```python
import jax
import jax.numpy as jnp
from jax import lax
from jax.experimental import pallas as pl
from jax.experimental.pallas import tpu as pltpu
from jax.sharding import PartitionSpec as P

HDIM = 64
EPSILON = 1e-05
NEGATIVE = -1e30
LOW = jnp.bfloat16
WIDE = jnp.float32
QROWS = 256
KROWS = 512
MEMROWS = 64
BLOCK = 128
NEAR_FIRST = ((0, 0), (-1, 0), (1, 0), (0, 1), (2, 0), (-1, 1), (1, 1), (2, 1))
FAR_FIRST = ((2, 1), (2, 0), (1, 1), (-1, 1), (1, 0), (-1, 0), (0, 1), (0, 0))
MESH = pl.DeviceIdType.MESH
VMEM = pl.BlockSpec(memory_space=pltpu.VMEM)
ANY = pl.BlockSpec(memory_space=pl.ANY)
VMEM_LIMIT = 60 * 2**20


def dot(left, right):
    return jnp.dot(left, right, preferred_element_type=WIDE)


def dot_nt(left, right):
    return lax.dot_general(left, right, (((1,), (1,)), ((), ())), preferred_element_type=WIDE)


def dot_tn(left, right):
    return lax.dot_general(left, right, (((0,), (0,)), ((), ())), preferred_element_type=WIDE)


def row_tiles(rows, body, step=16):
    def run(i, carry):
        body(pl.ds(pl.multiple_of(i * step, step), step))
        return carry

    lax.fori_loop(0, rows // step, run, 0)


class Group:
    def __init__(self, axis):
        self.axis = axis
        index = lax.axis_index(axis)
        self.me = index
        self.cores = 2 if axis == "head" else 1
        self.size = 8 * self.cores
        self.core = index % self.cores
        self.pair = index // self.cores % 2
        self.ring = index // (2 * self.cores)

    def chip(self, dr, dp):
        pair = 1 - self.pair if dp else self.pair
        return (self.ring + (dr + 4)) % 4 * 2 + pair

    def block(self, dr, dp, dc=0):
        core = 1 - self.core if dc else self.core
        return self.chip(dr, dp) * self.cores + core

    def device(self, dr, dp, dc=0):
        return {self.axis: self.block(dr, dp, dc)}

    def ahead(self, step):
        return (self.me + step) % self.size

    def away(self, step):
        return {self.axis: self.ahead(step)}

    def greet(self, barrier):
        peers = [(1, 0, 0), (-1, 0, 0), (0, 1, 0)] + ([(0, 0, 1)] if self.cores == 2 else [])
        for peer in peers:
            pl.semaphore_signal(barrier, 1, device_id=self.device(*peer), device_id_type=MESH)
        return len(peers)


def greet_all(*groups):
    barrier = pltpu.get_barrier_semaphore()
    pl.semaphore_wait(barrier, sum(group.greet(barrier) for group in groups))


class Gather:
    COPIES = 21

    def __init__(self, group, buf, send, recv, cut=BLOCK):
        self.group, self.buf, self.send, self.recv = group, buf, send, recv
        half = BLOCK // 2
        low = (cut // 2 + 15) // 16 * 16
        every, upper = (0, BLOCK), (cut, BLOCK - cut)
        ops = {
            "v0": ((0, 0), (1, 0, 0), every, (-1, 0)),
            "n0": ((0, 0), (-1, 0, 0), every, (1, 0)),
            "pair": ((0, 0), (0, 1, 0), every, (0, 1)),
            "v0h": ((-1, 0), (1, 0, 0), (0, half), (2, 0)),
            "n0h": ((1, 0), (-1, 0, 0), (half, half), (2, 0)),
            "v1": ((0, 1), (1, 0, 0), (0, cut), (-1, 1)),
            "n1": ((0, 1), (-1, 0, 0), (0, cut), (1, 1)),
            "v1h": ((-1, 1), (1, 0, 0), (0, low), (2, 1)),
            "n1h": ((1, 1), (-1, 0, 0), (low, cut - low), (2, 1)),
            "bv": ((-1, 0), (0, 1, 0), upper, (-1, 1)),
            "bn": ((1, 0), (0, 1, 0), upper, (1, 1)),
            "b2": ((2, 0), (0, 1, 0), upper, (2, 1)),
        }
        if group.cores == 2:
            for place in NEAR_FIRST:
                ops["s%d%d" % place] = (place, (0, 0, 1), every, place)
        self.ops = {name: (i,) + op for i, (name, op) in enumerate(ops.items()) if op[2][1] > 0}
        self.started = []
        self.inward = {
            (0, 0): (),
            (-1, 0): ("v0",),
            (1, 0): ("n0",),
            (0, 1): ("pair",),
            (2, 0): ("v0h", "n0h"),
            (-1, 1): ("v1", "bv"),
            (1, 1): ("n1", "bn"),
            (2, 1): ("v1h", "n1h", "b2"),
        }
        self.outward = {
            (0, 0): ("v0", "n0", "pair"),
            (-1, 0): ("v0h", "bv"),
            (1, 0): ("n0h", "bn"),
            (0, 1): ("v1", "n1"),
            (2, 0): ("b2",),
            (-1, 1): ("v1h",),
            (1, 1): ("n1h",),
            (2, 1): (),
        }

    def copy(self, name, arriving):
        i, place, peer, (start, count), source = self.ops[name]
        sibling = 1 if arriving and name[0] == "s" else 0
        block = self.group.block(*(source if arriving else place), sibling)
        view = self.buf.at[block] if count == BLOCK else self.buf.at[block, pl.ds(start, count)]
        return pltpu.make_async_remote_copy(
            src_ref=view,
            dst_ref=view,
            send_sem=self.send.at[i],
            recv_sem=self.recv.at[i],
            device_id=self.group.device(*peer),
            device_id_type=MESH,
        )

    def arrive(self, *place):
        for name in self.inward[place]:
            if name in self.ops:
                self.copy(name, True).wait_recv()
        names = self.outward[place]
        if self.group.cores == 2:
            names += ("s%d%d" % place,)
        for name in names:
            if name in self.ops:
                self.copy(name, False).start()
                self.started.append(name)

    def sibling(self, *place):
        if self.group.cores == 2:
            self.copy("s%d%d" % place, True).wait_recv()

    def drain(self):
        for name in self.started:
            self.copy(name, False).wait_send()


class Reduce:
    COPIES = 21

    def __init__(self, group, total, stage, land, send, recv, cut=BLOCK, near=None, result=None):
        self.group, self.total, self.land = group, total, land
        self.stage = total if stage is None else stage
        self.staged = stage is not None
        self.send, self.recv, self.near, self.result = send, recv, near, result
        half = BLOCK // 2
        low = (cut // 2 + 15) // 16 * 16
        every, upper = (0, BLOCK), (cut, BLOCK - cut)
        ops = {
            "b2": ((2, 1), (0, 1, 0), upper, 0),
            "n1h": ((2, 1), (1, 0, 0), (0, low), 1),
            "v1h": ((2, 1), (-1, 0, 0), (low, cut - low), 1),
            "n0h": ((2, 0), (1, 0, 0), (0, half), 2),
            "v0h": ((2, 0), (-1, 0, 0), (half, half), 2),
            "bn": ((1, 1), (0, 1, 0), upper, 3),
            "bv": ((-1, 1), (0, 1, 0), upper, 4),
            "n1": ((1, 1), (1, 0, 0), (0, cut), 3),
            "v1": ((-1, 1), (-1, 0, 0), (0, cut), 4),
            "n0": ((1, 0), (1, 0, 0), every, 5),
            "v0": ((-1, 0), (-1, 0, 0), every, 6),
            "pu": ((0, 1), (0, 1, 0), upper, 7),
            "pl": ((0, 1), (0, 1, 0), (0, cut), 7),
        }
        self.ops = {name: (i,) + op for i, (name, op) in enumerate(ops.items()) if op[2][1] > 0}
        self.cut = cut
        self.started = []
        self.early = {(1, 1): "bn", (-1, 1): "bv", (0, 1): "pu"}
        self.inward = {
            (2, 1): (),
            (2, 0): ("b2",),
            (1, 1): ("n1h",),
            (-1, 1): ("v1h",),
            (1, 0): ("bn", "n0h"),
            (-1, 0): ("bv", "v0h"),
            (0, 1): ("n1", "v1"),
            (0, 0): ("pu", "n0", "v0", "pl"),
        }
        self.outward = {
            (2, 1): ("b2", "n1h", "v1h"),
            (2, 0): ("n0h", "v0h"),
            (1, 1): ("n1",),
            (-1, 1): ("v1",),
            (1, 0): ("n0",),
            (-1, 0): ("v0",),
            (0, 1): ("pl",),
            (0, 0): (),
        }

    def copy(self, name):
        i, place, peer, (start, count), slot = self.ops[name]
        return pltpu.make_async_remote_copy(
            src_ref=self.stage.at[FAR_FIRST.index(place), pl.ds(start, count)],
            dst_ref=self.land.at[slot, pl.ds(start, count)],
            send_sem=self.send.at[i],
            recv_sem=self.recv.at[i],
            device_id=self.group.device(*peer),
            device_id_type=MESH,
        )

    def near_copy(self, k):
        return pltpu.make_async_remote_copy(
            src_ref=self.near[0].at[k],
            dst_ref=self.near[1].at[k],
            send_sem=self.send.at[13 + k],
            recv_sem=self.recv.at[13 + k],
            device_id=self.group.device(0, 0, 1),
            device_id_type=MESH,
        )

    def begin(self, name):
        self.copy(name).start()
        self.started.append(name)

    def blend(self, place, start, count, names):
        k = FAR_FIRST.index(place)
        spans = [self.ops[name][3] + (self.ops[name][4],) for name in names]
        marks = {start, start + count}
        for first, size, _ in spans:
            marks |= {m for m in (first, first + size) if start < m < start + count}
        marks = sorted(marks)
        for low, high in zip(marks, marks[1:]):
            slots = [slot for first, size, slot in spans if first <= low and high <= first + size]
            if not (slots or self.near or self.staged or place == (0, 0)):
                continue

            def body(rows):
                at = pl.ds(pl.multiple_of(rows.start + low, 16), 16)
                value = self.total[k, at].astype(WIDE)
                if self.near is not None:
                    value += self.near[1][k, at].astype(WIDE)
                for slot in slots:
                    value += self.land[slot, at].astype(WIDE)
                if place == (0, 0):
                    self.result[at] = value
                else:
                    self.stage[k, at] = value.astype(LOW)

            row_tiles(high - low, body)

    def settle(self, *place):
        if self.near is not None:
            self.near_copy(FAR_FIRST.index(place)).wait_recv()
        rest = BLOCK
        early = self.early.get(place)
        if early in self.ops:
            rest = self.cut
            self.blend(place, self.cut, BLOCK - self.cut, ())
            self.begin(early)
        names = [name for name in self.inward[place] if name in self.ops]
        for name in names:
            self.copy(name).wait_recv()
        self.blend(place, 0, rest, names)
        for name in self.outward[place]:
            if name in self.ops:
                self.begin(name)

    def drain(self):
        for name in self.started:
            self.copy(name).wait_send()
        if self.near is not None:
            for k in range(8):
                self.near_copy(k).wait_send()

    @staticmethod
    def scratch(columns, staged, near):
        part = pltpu.VMEM((8, BLOCK, columns), LOW)
        shapes = [pltpu.VMEM((8, BLOCK, columns), WIDE), part] if staged else [part]
        shapes += [part] + [pltpu.SemaphoreType.DMA((Reduce.COPIES,))] * 2
        return shapes + [part] * 2 if near else shapes


class Plane:
    def __init__(self, head):
        self.core, self.me, self.size = head.core, head.chip(0, 0), 8

    def ahead(self, step):
        return (self.me + step) % self.size

    def away(self, step):
        return {"head": self.ahead(step) * 2 + self.core}


def greet_everyone(head, *groups):
    barrier = pltpu.get_barrier_semaphore()
    pl.semaphore_signal(barrier, 1, device_id=head.device(0, 0, 1), device_id_type=MESH)
    for group in groups:
        def signal(step, carry):
            pl.semaphore_signal(barrier, 1, device_id=group.away(step), device_id_type=MESH)
            return carry

        lax.fori_loop(1, group.size, signal, 0)
    pl.semaphore_wait(barrier, 1 + sum(group.size - 1 for group in groups))


class Spread:
    def __init__(self, group, send, recv):
        self.group, self.send, self.recv = group, send, recv

    def copy(self, step, src, dst):
        return pltpu.make_async_remote_copy(
            src_ref=src,
            dst_ref=dst,
            send_sem=self.send.at[step],
            recv_sem=self.recv.at[step],
            device_id=self.group.away(step),
            device_id_type=MESH,
        )

    def each(self, body):
        def run(step, carry):
            body(step)
            return carry

        lax.fori_loop(1, self.group.size, run, 0)

    def start(self, src_of, land):
        self.each(lambda step: self.copy(step, src_of(self.group.ahead(step)), land.at[self.group.me]).start())

    def wait(self, land):
        def one(step):
            slot = land.at[self.group.ahead(self.group.size - step)]
            self.copy(step, slot, slot).wait_recv()

        self.each(one)

    def drain(self, src_of, land):
        self.each(lambda step: self.copy(step, src_of(self.group.ahead(step)), land.at[self.group.me]).wait_send())


def normal_of(values):
    mean = jnp.mean(values, axis=-1, keepdims=True)
    centered = values - mean
    var = jnp.mean(centered * centered, axis=-1, keepdims=True)
    rstd = lax.rsqrt(var + EPSILON)
    return centered * rstd, rstd


def stack_heads(rows):
    lane = lax.broadcasted_iota(jnp.int32, rows.shape, 1)
    zero = jnp.zeros_like(rows)
    return jnp.concatenate(
        [jnp.where(lane < HDIM, rows, zero), jnp.where(lane < HDIM, zero, rows)], axis=0
    )


def causal_bias(chunk, block, tail_bias):
    key = block * KROWS + lax.broadcasted_iota(jnp.int32, (KROWS, 2 * QROWS), 0)
    lane = lax.broadcasted_iota(jnp.int32, (KROWS, 2 * QROWS), 1)
    query = chunk * QROWS + jnp.where(lane < QROWS, lane, lane - QROWS)
    own = jnp.where(block == 2048 // KROWS - 1, tail_bias, jnp.zeros_like(tail_bias))
    return jnp.where(key <= query, jnp.broadcast_to(own, key.shape), NEGATIVE)


def transpose_into(dst_ref, src_ref):
    rows = src_ref.shape[0]
    if rows <= 256:
        dst_ref[...] = src_ref[...].T
        return

    def body(i, carry):
        at = pl.multiple_of(i * 256, 256)
        dst_ref[:, pl.ds(at, 256)] = src_ref[pl.ds(at, 256), :].T
        return carry

    lax.fori_loop(0, rows // 256, body, 0)


def attend_chunk(chunk, q_ref, k_ref, vt_ref, mk_ref, mvt_ref, mem_bias, tail_bias):
    start = pl.multiple_of(chunk * QROWS, QROWS)
    q2 = stack_heads(q_ref[pl.ds(start, QROWS), :] * HDIM ** (-0.5))

    def values_times(values_t, probs):
        low = probs.astype(LOW)
        return (
            dot(values_t[:HDIM], low[:, :QROWS]),
            dot(values_t[HDIM:], low[:, QROWS:]),
        )

    scores = dot_nt(mk_ref[...], q2) + mem_bias
    peak = jnp.max(scores, axis=0, keepdims=True)
    raised = jnp.exp(scores - peak)
    total = jnp.sum(raised, axis=0, keepdims=True)
    first, second = values_times(mvt_ref[...], raised)

    def update(block, scores, carry):
        peak, total, first, second = carry
        at = pl.multiple_of(block * KROWS, KROWS)
        new_peak = jnp.maximum(peak, jnp.max(scores, axis=0, keepdims=True))
        scale = jnp.exp(peak - new_peak)
        raised = jnp.exp(scores - new_peak)
        total = total * scale + jnp.sum(raised, axis=0, keepdims=True)
        add_first, add_second = values_times(vt_ref[:, pl.ds(at, KROWS)], raised)
        return (
            new_peak,
            total,
            first * scale[:, :QROWS] + add_first,
            second * scale[:, QROWS:] + add_second,
        )

    def block_scores(block):
        at = pl.multiple_of(block * KROWS, KROWS)
        return dot_nt(k_ref[pl.ds(at, KROWS), :], q2)

    full = chunk * QROWS // KROWS
    carry = lax.fori_loop(
        0, full, lambda b, c: update(b, block_scores(b), c), (peak, total, first, second)
    )
    scores = block_scores(full) + causal_bias(chunk, full, tail_bias)
    peak, total, first, second = update(full, scores, carry)
    inverse = 1.0 / total
    attended = jnp.concatenate([first * inverse[:, :QROWS], second * inverse[:, QROWS:]], axis=0)
    return attended, peak + jnp.log(total)


def chip_at(group, order, step):
    return sum(jnp.where(step == j, group.chip(*place), 0) for j, place in enumerate(order))


def open_kernel(
    hidden_ref, memory_ref, counts_ref, gain_ref, shift_ref, w_ref, b_query_ref, b_value_ref,
    q_ref, k_ref, v_ref, mk_ref, mv_ref, mem_normed_ref, mem_bias_ref, tail_bias_ref, w_t_ref,
    normed_out,
    rows_buf, flat_w, mem_wide, send, recv, out_sem,
):
    head = Group("head")
    gather = Gather(head, rows_buf, send, recv, 64)
    own = head.block(0, 0)

    def norm_rows(rows):
        normal, _ = normal_of(hidden_ref[rows].astype(WIDE))
        rows_buf[own, rows] = (normal * gain_ref[...] + shift_ref[...]).astype(LOW)

    row_tiles(BLOCK, norm_rows, 32)
    greet_all(head)
    gather.arrive(0, 0)
    width = q_ref.shape[1]
    slots = memory_ref.shape[0]
    for i in range(3):
        flat_w[:, i * width : (i + 1) * width] = w_ref[i]
    copies = []

    def project(*place):
        gather.sibling(*place)
        chip = head.chip(*place)
        out = pltpu.make_async_copy(
            rows_buf.at[pl.ds(chip * 2, 2)], normed_out.at[pl.ds(chip * 2, 2)], out_sem.at[len(copies)]
        )
        out.start()
        copies.append(out)
        rows = rows_buf[pl.ds(chip * 2, 2)].reshape(2 * BLOCK, rows_buf.shape[2])
        at = pl.ds(pl.multiple_of(chip * 2 * BLOCK, 2 * BLOCK), 2 * BLOCK)
        all_parts = dot(rows, flat_w[...])
        q_ref[at, :] = (all_parts[:, :width] + b_query_ref[...]).astype(LOW)
        k_ref[at, :] = all_parts[:, width : 2 * width].astype(LOW)
        v_ref[at, :] = (all_parts[:, 2 * width :] + b_value_ref[...]).astype(LOW)

    def side_work():
        mem_wide[...] = jnp.zeros_like(mem_wide)
        mem_wide[:slots, :] = memory_ref[...].astype(WIDE)

        def norm_memory(rows):
            normal, _ = normal_of(mem_wide[rows])
            mem_normed_ref[rows] = (normal * gain_ref[...] + shift_ref[...]).astype(LOW)

        row_tiles(MEMROWS, norm_memory, 32)
        mem = dot(mem_normed_ref[...], flat_w[:, width:])
        mk_ref[...] = mem[:, :width].astype(LOW)
        mv_ref[...] = (mem[:, width:] + b_value_ref[...]).astype(LOW)
        slot = lax.broadcasted_iota(jnp.int32, mem_bias_ref.shape, 0)
        mem_bias_ref[...] = jnp.where(slot < counts_ref[0, 0], 0.0, NEGATIVE)
        tail = slots - KROWS + lax.broadcasted_iota(jnp.int32, tail_bias_ref.shape, 0)
        tail_bias_ref[...] = jnp.where((tail < 0) | (tail < counts_ref[0, 1]), 0.0, NEGATIVE)
        for i in range(3):
            transpose_into(w_t_ref.at[pl.ds(i * width, width)], w_ref.at[i])

    side_work()
    project(0, 0)
    gather.arrive(-1, 0)
    gather.arrive(1, 0)
    gather.arrive(0, 1)
    project(-1, 0)
    project(1, 0)
    gather.arrive(2, 0)
    project(0, 1)
    gather.arrive(-1, 1)
    gather.arrive(1, 1)
    project(2, 0)
    project(-1, 1)
    project(1, 1)
    gather.arrive(2, 1)
    project(2, 1)
    gather.drain()
    for out in copies:
        out.wait()


def open_layer(hidden, memory, counts, gain, shift, w, b_query, b_value):
    rows, model = hidden.shape
    width = w.shape[2]
    part = jax.ShapeDtypeStruct((16 * rows, width), LOW)
    mem_part = jax.ShapeDtypeStruct((MEMROWS, width), LOW)
    sems = [pltpu.SemaphoreType.DMA((Gather.COPIES,))] * 2
    smem = pl.BlockSpec(memory_space=pltpu.SMEM)
    return pl.pallas_call(
        open_kernel,
        out_shape=(
            part, part, part, mem_part, mem_part,
            jax.ShapeDtypeStruct((MEMROWS, model), LOW),
            jax.ShapeDtypeStruct((MEMROWS, 1), WIDE),
            jax.ShapeDtypeStruct((KROWS, 1), WIDE),
            jax.ShapeDtypeStruct((3 * width, model), LOW),
            jax.ShapeDtypeStruct((16, rows, model), LOW),
        ),
        in_specs=[VMEM] * 2 + [smem] + [VMEM] * 5,
        out_specs=(VMEM,) * 9 + (ANY,),
        scratch_shapes=[
            pltpu.VMEM((16, rows, model), LOW),
            pltpu.VMEM((model, 3 * width), LOW),
            pltpu.VMEM((MEMROWS, model), WIDE),
        ] + sems + [pltpu.SemaphoreType.DMA((8,))],
        compiler_params=pltpu.CompilerParams(
            collective_id=0, has_side_effects=True, vmem_limit_bytes=VMEM_LIMIT
        ),
        name="open_layer",
    )(hidden, memory, counts, gain, shift, w, b_query, b_value)


def attend_kernel(
    q_ref, k_ref, v_ref, mk_ref, mv_ref, mem_bias_ref, tail_bias_ref, wo_ref,
    hidden_ref, b_out_ref, gain_ref, shift_ref, cot_ref, w_up_hbm,
    attn_t_ref, lse_ref, resid_ref, second_ref, w_up_t_ref, cot_out,
    vt_ref, mvt_ref, attn_ref, cot_buf, wu_ref, load_sem, out_sem, cot_send, cot_recv,
    total, stage, land, send, recv, near_stage, near_land,
):
    head, seq = Group("head"), Group("seq")
    reduce = Reduce(head, total, stage, land, send, recv, 128, (near_stage, near_land), resid_ref)
    gather = Gather(seq, cot_buf, cot_send, cot_recv, 128)

    def keep_cot(*place):
        block = seq.block(*place)
        return pltpu.make_async_copy(
            cot_buf.at[block], cot_out.at[block], out_sem.at[NEAR_FIRST.index(place)]
        )

    load = pltpu.make_async_copy(w_up_hbm, wu_ref, load_sem)
    load.start()
    cot_buf[seq.me] = cot_ref[...]
    transpose_into(vt_ref, v_ref)
    transpose_into(mvt_ref, mv_ref)
    greet_all(head, seq)
    gather.arrive(0, 0)

    def step(k, carry):
        chip = chip_at(head, FAR_FIRST, k)
        start = pl.multiple_of(chip * QROWS, QROWS)
        attended, lse = attend_chunk(
            chip, q_ref, k_ref, vt_ref, mk_ref, mvt_ref, mem_bias_ref[...], tail_bias_ref[...]
        )
        attn_t_ref[:, pl.ds(start, QROWS)] = attended.astype(LOW)
        attn_ref[...] = attended.T.astype(LOW)
        lse_ref[chip] = lse
        mine = attn_ref[pl.ds(pl.multiple_of(head.core * BLOCK, BLOCK), BLOCK), :]
        other = attn_ref[pl.ds(pl.multiple_of((1 - head.core) * BLOCK, BLOCK), BLOCK), :]
        for at in range(0, total.shape[2], 512):
            near_stage[k, :, at : at + 512] = dot(other, wo_ref[:, at : at + 512]).astype(LOW)
        reduce.near_copy(k).start()
        for at in range(0, total.shape[2], 512):
            total[k, :, at : at + 512] = dot(mine, wo_ref[:, at : at + 512])
        for j, place in enumerate(FAR_FIRST[:-1]):
            @pl.when(k == j + 1)
            def _():
                reduce.settle(*place)

        @pl.when(k == 4)
        def _():
            gather.arrive(-1, 0)
            gather.arrive(1, 0)
            gather.arrive(0, 1)

        @pl.when(k == 6)
        def _():
            gather.arrive(2, 0)

        return carry

    lax.fori_loop(0, 8, step, 0)
    gather.arrive(-1, 1)
    gather.arrive(1, 1)
    for place in NEAR_FIRST[:-1]:
        keep_cot(*place).start()
    load.wait()
    transpose_into(w_up_t_ref, wu_ref)
    reduce.settle(0, 0)

    def finish(rows):
        resid = hidden_ref[rows].astype(WIDE) + resid_ref[rows] + b_out_ref[...]
        resid_ref[rows] = resid
        normal, _ = normal_of(resid)
        second_ref[rows] = (normal * gain_ref[...] + shift_ref[...]).astype(LOW)

    row_tiles(BLOCK, finish, 32)
    gather.arrive(2, 1)
    keep_cot(2, 1).start()
    gather.drain()
    reduce.drain()
    for place in NEAR_FIRST:
        keep_cot(*place).wait()


def attend_layer(
    q, k, v, mk, mv, mem_bias, tail_bias, wo, hidden, b_out, gain, shift, cot, w_up
):
    length, width = q.shape
    rows, model = hidden.shape
    units = w_up.shape[1]
    return pl.pallas_call(
        attend_kernel,
        out_shape=(
            jax.ShapeDtypeStruct((width, length), LOW),
            jax.ShapeDtypeStruct((length // QROWS, 1, 2 * QROWS), WIDE),
            jax.ShapeDtypeStruct((rows, model), WIDE),
            jax.ShapeDtypeStruct((rows, model), LOW),
            jax.ShapeDtypeStruct((units, model), LOW),
            jax.ShapeDtypeStruct((8, rows, model), LOW),
        ),
        in_specs=[VMEM] * 13 + [ANY],
        out_specs=(VMEM,) * 5 + (ANY,),
        scratch_shapes=[
            pltpu.VMEM((width, length), LOW),
            pltpu.VMEM((width, MEMROWS), LOW),
            pltpu.VMEM((QROWS, width), LOW),
            pltpu.VMEM((8, rows, model), LOW),
            pltpu.VMEM((model, units), LOW),
            pltpu.SemaphoreType.DMA,
            pltpu.SemaphoreType.DMA((8,)),
        ] + [pltpu.SemaphoreType.DMA((Gather.COPIES,))] * 2 + Reduce.scratch(model, True, True),
        compiler_params=pltpu.CompilerParams(
            collective_id=1, has_side_effects=True, vmem_limit_bytes=VMEM_LIMIT
        ),
        name="attend_layer",
    )(
        q, k, v, mk, mv, mem_bias, tail_bias, wo, hidden, b_out, gain, shift,
        cot, w_up,
    )


def gelu_parts(u):
    square = u * u
    t = jnp.tanh(0.7978845608 * (u + 0.044715 * (square * u)))
    half = 0.5 * (1.0 + t)
    slope = half + 0.5 * u * (1.0 - t * t) * (0.7978845608 * (1.0 + 0.134145 * square))
    return u * half, slope


def fold_rows(values):
    return jnp.sum(values.reshape(values.shape[0] // 8, 8, values.shape[1]), axis=0)


def feed_kernel(
    second_ref, w_up_hbm, w_up_t_hbm, w_down_hbm, cot_hbm, up_bias_ref, resid_ref, gain_ref,
    cot_ref,
    grad_resid_ref, sums_ref, branch_hbm, grad_w_ref, grad_b_up_ref,
    rows_buf, wu_ref, wut_ref, wd_ref, cot_buf, act_ref, back_ref, pre_ref, fold_ref, sum_fold, branch_buf,
    load_sem, branch_sem, send, recv,
    total, land, rsend, rrecv,
    w_total, w_land, w_send, w_recv, w_near_stage, w_near_land,
):
    head, seq = Group("head"), Group("seq")
    gather = Gather(seq, rows_buf, send, recv, 64)
    reduce = Reduce(seq, total, None, land, rsend, rrecv, 128, None, grad_resid_ref)
    w_reduce = Reduce(head, w_total, None, w_land, w_send, w_recv, 112, (w_near_stage, w_near_land), grad_w_ref)
    loads = [
        pltpu.make_async_copy(src, dst, load_sem.at[i])
        for i, (src, dst) in enumerate(
            (
                (cot_hbm, cot_buf), (w_down_hbm, wd_ref), (w_up_hbm, wu_ref), (w_up_t_hbm, wut_ref),
            )
        )
    ]
    for load in loads:
        load.start()
    own = seq.block(0, 0)
    rows_buf[own] = second_ref[...]
    fold_ref[...] = jnp.zeros_like(fold_ref)
    greet_all(head, seq)
    gather.arrive(0, 0)
    loads[0].wait()
    loads[1].wait()
    units = act_ref.shape[2]
    model = rows_buf.shape[2]
    bias_at = pl.ds(pl.multiple_of(own * units, units), units)

    def cot_times(i, carry):
        pairs = cot_buf[pl.ds(2 * i, 2)].reshape(2 * BLOCK, model)
        for at in range(0, units, 256):
            part = dot_nt(pairs, wd_ref[at : at + 256, :]).astype(LOW)
            back_ref[pl.ds(2 * i, 2), :, at : at + 256] = part.reshape(2, BLOCK, 256)
        return carry

    def feed(*place):
        block = seq.block(*place)
        pre_ref[...] = dot(rows_buf[block], wu_ref[...]) + up_bias_ref[:, bias_at]

        def bend(rows):
            activated, slope = gelu_parts(pre_ref[rows])
            grad_pre = back_ref[block, rows].astype(WIDE) * slope
            act_ref[block, rows] = activated.astype(LOW)
            back_ref[block, rows] = grad_pre.astype(LOW)
            fold_ref[...] += fold_rows(grad_pre)

        row_tiles(BLOCK, bend)
        k = FAR_FIRST.index(place)
        for at in range(0, model, 512):
            total[k, :, at : at + 512] = dot(back_ref[block], wut_ref[:, at : at + 512]).astype(LOW)

    lax.fori_loop(0, 4, cot_times, 0)
    loads[2].wait()
    loads[3].wait()
    feed(0, 0)
    gather.arrive(-1, 0)
    gather.arrive(1, 0)
    gather.arrive(0, 1)
    feed(-1, 0)
    gather.arrive(2, 0)
    feed(1, 0)
    gather.arrive(-1, 1)
    gather.arrive(1, 1)
    feed(0, 1)
    feed(2, 0)
    feed(-1, 1)
    feed(1, 1)
    gather.arrive(2, 1)
    feed(2, 1)
    reduce.settle(2, 1)
    reduce.settle(2, 0)
    grad_b_up_ref[...] = jnp.sum(fold_ref[...], axis=0, keepdims=True)

    def weights(k, carry):
        chip = chip_at(head, FAR_FIRST, k)

        def part(core):
            at = pl.ds(pl.multiple_of(chip * 2 * BLOCK + core * BLOCK, BLOCK), BLOCK)
            length = 8 * BLOCK
            up = dot_tn(
                rows_buf[:, :, at].reshape(length, BLOCK), back_ref[...].reshape(length, units)
            )
            down = dot_tn(
                cot_buf[:, :, at].reshape(length, BLOCK), act_ref[...].reshape(length, units)
            )
            return up.astype(LOW), down.astype(LOW)

        w_near_stage[k, :, :units], w_near_stage[k, :, units:] = part(1 - head.core)
        w_reduce.near_copy(k).start()
        w_total[k, :, :units], w_total[k, :, units:] = part(head.core)
        for j, place in enumerate(FAR_FIRST[:6]):
            @pl.when(k == j + 1)
            def _():
                w_reduce.settle(*place)

        @pl.when(k == 2)
        def _():
            reduce.settle(1, 1)
            reduce.settle(-1, 1)

        @pl.when(k == 5)
        def _():
            reduce.settle(1, 0)
            reduce.settle(-1, 0)

        return carry

    lax.fori_loop(0, 8, weights, 0)
    branch_copies = []

    def branch(i):
        slot = i % 2
        if i >= 2:
            branch_copies[i - 2].wait()
        for at in range(0, model, 512):
            branch_buf[slot, :, at : at + 512] = dot(act_ref[i], wd_ref[:, at : at + 512]).astype(LOW)
        copy = pltpu.make_async_copy(branch_buf.at[slot], branch_hbm.at[i], branch_sem.at[i])
        copy.start()
        branch_copies.append(copy)

    for i in range(4):
        branch(i)
    reduce.settle(0, 1)
    w_reduce.settle(0, 1)
    for i in range(4, 8):
        branch(i)
    reduce.settle(0, 0)
    sum_fold[...] = jnp.zeros_like(sum_fold)

    def back(rows):
        normal, rstd = normal_of(resid_ref[rows])
        incoming = grad_resid_ref[rows]
        scaled = incoming * gain_ref[...]
        inner = jnp.mean(scaled, axis=-1, keepdims=True)
        along = jnp.mean(scaled * normal, axis=-1, keepdims=True)
        cot = cot_ref[rows].astype(WIDE)
        grad = cot + rstd * (scaled - inner - normal * along)
        grad_resid_ref[rows] = grad
        for i, value in enumerate((grad, incoming * normal, incoming, cot)):
            sum_fold[i] += fold_rows(value)

    row_tiles(BLOCK, back)
    sums_ref[...] = jnp.sum(sum_fold[...], axis=1)
    w_reduce.settle(0, 0)
    for copy in branch_copies[-2:]:
        copy.wait()
    gather.drain()
    reduce.drain()
    w_reduce.drain()


def feed_layer(second, w_up, w_up_t, w_down, cot_all, up_bias, resid, gain, cot):
    rows, model = second.shape
    units = w_up.shape[1]
    gather_sems = [pltpu.SemaphoreType.DMA((Gather.COPIES,))] * 2
    return pl.pallas_call(
        feed_kernel,
        out_shape=(
            jax.ShapeDtypeStruct((rows, model), WIDE),
            jax.ShapeDtypeStruct((4, model), WIDE),
            jax.ShapeDtypeStruct((8, rows, model), LOW),
            jax.ShapeDtypeStruct((rows, 2 * units), WIDE),
            jax.ShapeDtypeStruct((1, units), WIDE),
        ),
        in_specs=[VMEM] + [ANY] * 4 + [VMEM] * 4,
        out_specs=(VMEM, VMEM, ANY, VMEM, VMEM),
        scratch_shapes=[
            pltpu.VMEM((8, rows, model), LOW),
            pltpu.VMEM((model, units), LOW),
            pltpu.VMEM((units, model), LOW),
            pltpu.VMEM((units, model), LOW),
            pltpu.VMEM((8, rows, model), LOW),
            pltpu.VMEM((8, rows, units), LOW),
            pltpu.VMEM((8, rows, units), LOW),
            pltpu.VMEM((rows, units), WIDE),
            pltpu.VMEM((8, units), WIDE),
            pltpu.VMEM((4, 8, model), WIDE),
            pltpu.VMEM((2, rows, model), LOW),
            pltpu.SemaphoreType.DMA((4,)),
            pltpu.SemaphoreType.DMA((8,)),
        ] + gather_sems + Reduce.scratch(model, False, False) + Reduce.scratch(2 * units, False, True),
        compiler_params=pltpu.CompilerParams(
            collective_id=2, has_side_effects=True, vmem_limit_bytes=VMEM_LIMIT
        ),
        name="feed_layer",
    )(second, w_up, w_up_t, w_down, cot_all, up_bias, resid, gain, cot)


def attend_back_chunk(
    chunk, q_ref, k_ref, kt_ref, v_ref, mk_ref, mkt_ref, mv_ref, mem_bias, tail_bias,
    attn_t_ref, lse_ref, grad_rows, dk_ref, dv_ref, dmk_ref, dmv_ref,
):
    start = pl.multiple_of(chunk * QROWS, QROWS)
    q2 = stack_heads(q_ref[pl.ds(start, QROWS), :] * HDIM ** (-0.5))
    g2 = stack_heads(grad_rows)
    product = grad_rows.astype(WIDE).T * attn_t_ref[:, pl.ds(start, QROWS)].astype(WIDE)
    inner = jnp.concatenate(
        [
            jnp.sum(product[:HDIM], axis=0, keepdims=True),
            jnp.sum(product[HDIM:], axis=0, keepdims=True),
        ],
        axis=1,
    )
    lse = lse_ref[chunk]

    def piece(scores, values, keys_t):
        probs = jnp.exp(scores - lse)
        grad_probs = dot_nt(values, g2)
        grad_scores = (probs * (grad_probs - inner)).astype(LOW)
        return (
            dot(probs.astype(LOW), g2),
            dot(grad_scores, q2),
            dot(keys_t[:HDIM], grad_scores[:, :QROWS]),
            dot(keys_t[HDIM:], grad_scores[:, QROWS:]),
        )

    dv, dk, first, second = piece(
        dot_nt(mk_ref[...], q2) + mem_bias, mv_ref[...], mkt_ref[...]
    )
    dmv_ref[...] += dv
    dmk_ref[...] += dk

    def block_step(block, bias, carry):
        first, second = carry
        at = pl.multiple_of(block * KROWS, KROWS)
        scores = dot_nt(k_ref[pl.ds(at, KROWS), :], q2)
        if bias is not None:
            scores = scores + bias
        dv, dk, add_first, add_second = piece(
            scores, v_ref[pl.ds(at, KROWS), :], kt_ref[:, pl.ds(at, KROWS)]
        )
        dv_ref[pl.ds(at, KROWS), :] += dv
        dk_ref[pl.ds(at, KROWS), :] += dk
        return first + add_first, second + add_second

    full = chunk * QROWS // KROWS
    carry = lax.fori_loop(0, full, lambda b, c: block_step(b, None, c), (first, second))
    first, second = block_step(full, causal_bias(chunk, full, tail_bias), carry)
    return jnp.concatenate([first, second], axis=0) * HDIM ** (-0.5)


def grad_kernel(
    grad_resid_ref, resid_ref, b_down_ref, branch_hbm, wo_ref,
    q_ref, k_ref, v_ref, mk_ref, mv_ref, mem_bias_ref, tail_bias_ref, attn_t_ref, lse_ref,
    out_ref, own_ref, own_t_ref, mem_ref, mem_t_ref, grad_wo_ref, sums_ref,
    rows_buf, kt_ref, mkt_ref, dk_ref, dv_ref, dmk_ref, dmv_ref, wo_sum, branch_sum, fold_ref,
    load_sem, send, recv, total, land, rsend, rrecv,
):
    head, seq = Group("head"), Group("seq")
    gather = Gather(head, rows_buf, send, recv, 64)
    reduce = Reduce(seq, total, None, land, rsend, rrecv, 128, None, branch_sum)
    loads = [
        pltpu.make_async_copy(branch_hbm.at[seq.block(*place)], total.at[k], load_sem.at[k])
        for k, place in enumerate(FAR_FIRST)
    ]
    for load in loads:
        load.start()
    own = head.block(0, 0)
    rows_buf[own] = grad_resid_ref[...].astype(LOW)
    greet_all(head, seq)
    gather.arrive(0, 0)
    loads[0].wait()
    reduce.settle(2, 1)
    loads[1].wait()
    reduce.settle(2, 0)
    transpose_into(kt_ref, k_ref)
    transpose_into(mkt_ref, mk_ref)
    for ref in (dk_ref, dv_ref, dmk_ref, dmv_ref, wo_sum, fold_ref):
        ref[...] = jnp.zeros_like(ref)
    width, model = wo_ref.shape
    for load in loads[2:]:
        load.wait()

    def step(k, carry):
        @pl.when(k == 0)
        def _():
            gather.sibling(0, 0)

        @pl.when(k == 1)
        def _():
            gather.arrive(-1, 0)
            gather.arrive(1, 0)
            reduce.settle(1, 1)
            reduce.settle(-1, 1)
            gather.arrive(0, 1)
            gather.sibling(-1, 0)

        @pl.when(k == 2)
        def _():
            reduce.settle(1, 0)
            reduce.settle(-1, 0)
            gather.sibling(1, 0)

        @pl.when(k == 3)
        def _():
            gather.arrive(2, 0)
            gather.sibling(0, 1)

        @pl.when(k == 4)
        def _():
            gather.arrive(-1, 1)
            gather.arrive(1, 1)
            gather.sibling(2, 0)

        @pl.when(k == 5)
        def _():
            reduce.settle(0, 1)
            gather.sibling(-1, 1)

        @pl.when(k == 6)
        def _():
            gather.arrive(2, 1)
            gather.sibling(1, 1)

        @pl.when(k == 7)
        def _():
            gather.sibling(2, 1)

        chip = chip_at(head, NEAR_FIRST, k)
        at = pl.ds(pl.multiple_of(chip * QROWS, QROWS), QROWS)
        rows = rows_buf[pl.ds(chip * 2, 2)].reshape(QROWS, model)
        grad_rows = dot_nt(rows, wo_ref[...]).astype(LOW)
        wo_sum[...] += dot(attn_t_ref[:, at], rows)
        dq = attend_back_chunk(
            chip, q_ref, k_ref, kt_ref, v_ref, mk_ref, mkt_ref, mv_ref,
            mem_bias_ref[...], tail_bias_ref[...], attn_t_ref, lse_ref,
            grad_rows, dk_ref, dv_ref, dmk_ref, dmv_ref,
        ).astype(LOW)
        own_t_ref[:width, at] = dq
        own_ref[at, :width] = dq.T
        return carry

    lax.fori_loop(0, 8, step, 0)

    def finish_keys(i, carry):
        at = pl.ds(pl.multiple_of(i * 256, 256), 256)
        dk = dk_ref[at, :].astype(LOW)
        dv = dv_ref[at, :].astype(LOW)
        own_ref[at, width : 2 * width] = dk
        own_ref[at, 2 * width :] = dv
        own_t_ref[width : 2 * width, at] = dk.T
        own_t_ref[2 * width :, at] = dv.T
        fold_ref[...] += fold_rows(own_ref[at, :].astype(WIDE))
        return carry

    lax.fori_loop(0, q_ref.shape[0] // 256, finish_keys, 0)
    for i, ref in enumerate((dmk_ref, dmv_ref)):
        low = ref[...].astype(LOW)
        mem_ref[:, i * width : (i + 1) * width] = low
        mem_t_ref[i * width : (i + 1) * width, :] = low.T
    fold_ref[:, width:] += fold_rows(mem_ref[...].astype(WIDE))
    sums_ref[...] = jnp.sum(fold_ref[...], axis=0, keepdims=True)
    grad_wo_ref[...] = wo_sum[...].astype(LOW)
    reduce.settle(0, 0)

    def finish(rows):
        out_ref[rows] = (resid_ref[rows] + branch_sum[rows] + b_down_ref[...]).astype(LOW)

    row_tiles(BLOCK, finish)
    gather.drain()
    reduce.drain()


def grad_layer(
    grad_resid, resid, b_down, branch, wo, q, k, v, mk, mv, mem_bias, tail_bias, attn_t, lse,
):
    rows, model = grad_resid.shape
    length, width = q.shape
    return pl.pallas_call(
        grad_kernel,
        out_shape=(
            jax.ShapeDtypeStruct((rows, model), LOW),
            jax.ShapeDtypeStruct((length, 3 * width), LOW),
            jax.ShapeDtypeStruct((3 * width, length), LOW),
            jax.ShapeDtypeStruct((MEMROWS, 2 * width), LOW),
            jax.ShapeDtypeStruct((2 * width, MEMROWS), LOW),
            jax.ShapeDtypeStruct((width, model), LOW),
            jax.ShapeDtypeStruct((1, 3 * width), WIDE),
        ),
        in_specs=[VMEM] * 3 + [ANY] + [VMEM] * 10,
        out_specs=(VMEM,) * 7,
        scratch_shapes=[
            pltpu.VMEM((16, rows, model), LOW),
            pltpu.VMEM((width, length), LOW),
            pltpu.VMEM((width, MEMROWS), LOW),
            pltpu.VMEM((length, width), WIDE),
            pltpu.VMEM((length, width), WIDE),
            pltpu.VMEM((MEMROWS, width), WIDE),
            pltpu.VMEM((MEMROWS, width), WIDE),
            pltpu.VMEM((width, model), WIDE),
            pltpu.VMEM((rows, model), WIDE),
            pltpu.VMEM((8, 3 * width), WIDE),
            pltpu.SemaphoreType.DMA((8,)),
        ] + [pltpu.SemaphoreType.DMA((Gather.COPIES,))] * 2 + Reduce.scratch(model, False, False),
        compiler_params=pltpu.CompilerParams(
            collective_id=3, has_side_effects=True, vmem_limit_bytes=VMEM_LIMIT
        ),
        name="grad_layer",
    )(
        grad_resid, resid, b_down, branch, wo, q, k, v, mk, mv, mem_bias, tail_bias, attn_t, lse,
    )


SUM_ROWS = 16


def close_kernel(
    own_ref, own_t_ref, mem_ref, mem_t_ref, grad_wo_ref, mem_normed_ref, normed_hbm, w_t_ref,
    gain_ref, shift_ref, bias_sums_ref, feed_sums_ref, b_up_ref,
    grad_normed_ref, grad_w_ref, small_ref,
    rows_buf, mem_pad, norm_sums, pay_ref, core_land, pay_half, pay_land, seq_land,
    core_send, core_recv, pay_send, pay_recv, seq_send, seq_recv, all_send, all_recv, load_sem,
    total, stage, land, send, recv, near_stage, near_land,
    w_total, w_stage, w_land, w_send, w_recv, g_send, g_recv,
):
    head, seq = Group("head"), Group("seq")
    reduce = Reduce(head, total, stage, land, send, recv, 112, (near_stage, near_land), grad_normed_ref)
    w_reduce = Reduce(seq, w_total, w_stage, w_land, w_send, w_recv, 128, None, w_total.at[7])
    gather = Gather(seq, grad_w_ref, g_send, g_recv, 128)
    plane = Plane(head)
    pay = Spread(plane, pay_send, pay_recv)
    across = Spread(seq, seq_send, seq_recv)
    back = Spread(plane, all_send, all_recv)
    load = pltpu.make_async_copy(normed_hbm, rows_buf, load_sem)
    load.start()
    width = grad_wo_ref.shape[0]
    model = rows_buf.shape[2]
    length = own_ref.shape[0]
    wide = model // 2
    share = model // head.size
    mem_pad[...] = jnp.zeros_like(mem_pad)
    mem_pad[pl.ds(width, 2 * width), :] = mem_t_ref[...]
    norm_sums[...] = jnp.zeros_like(norm_sums)
    greet_everyone(head, plane, seq)

    def chunk(k):
        chip = head.chip(*FAR_FIRST[k])

        def part(core):
            at = pl.ds(pl.multiple_of(chip * QROWS + core * BLOCK, BLOCK), BLOCK)
            return own_ref[at, :]

        mine, other = part(head.core), part(1 - head.core)
        for at in range(0, model, 512):
            near_stage[k, :, at : at + 512] = dot(other, w_t_ref[:, at : at + 512]).astype(LOW)
        reduce.near_copy(k).start()
        for at in range(0, model, 512):
            total[k, :, at : at + 512] = dot(mine, w_t_ref[:, at : at + 512])

    def weights(k, carry):
        target = chip_at(seq, FAR_FIRST, k)
        part, side = target // 2, target % 2
        columns = pl.ds(pl.multiple_of(side * wide, wide), wide)

        @pl.when(part < 3)
        def _():
            at = pl.ds(pl.multiple_of(part * width, width), width)
            term = dot(
                own_t_ref[at, :], rows_buf[:, :, columns].reshape(length, wide)
            ) + dot(mem_pad[at, :], mem_normed_ref[:, columns])
            w_total[k] = term
            flat = w_t_ref[at, columns].astype(WIDE)
            norm_sums[0:1, columns] += jnp.sum(flat * term, axis=0, keepdims=True)

        @pl.when(part == 3)
        def _():
            w_total[k] = grad_wo_ref[:, columns].astype(WIDE)

        return carry

    def shift_sums():
        sums = bias_sums_ref[...]
        high = sums.astype(LOW)
        rest = (sums - high.astype(WIDE)).astype(LOW)
        pair = jnp.concatenate([high, rest, jnp.zeros((14, sums.shape[1]), LOW)], axis=0)
        both = dot(pair, w_t_ref[...])
        norm_sums[1:2, :] = both[0:1] + both[1:2]

    def core_copy(i, src, dst):
        return pltpu.make_async_remote_copy(
            src_ref=src,
            dst_ref=dst,
            send_sem=core_send.at[i],
            recv_sem=core_recv.at[i],
            device_id=head.device(0, 0, 1),
            device_id_type=MESH,
        )

    def half_of(core):
        return pay_ref.at[:, pl.ds(pl.multiple_of(core * wide, wide), wide)]

    def pay_part(i):
        return pay_half.at[:, pl.ds(pl.multiple_of(i * share, share), share)]

    def pay_core():
        return core_copy(0, half_of(1 - head.core), core_land)

    def pay_whole():
        return core_copy(1, small_ref.at[head.core], small_ref.at[head.core])

    def pay_start():
        pay_ref[:MEMROWS, :] = dot(mem_ref[...], w_t_ref[width:, :]).astype(LOW)
        at_gain = norm_sums[0:1, :] - shift_ref[...] * norm_sums[1:2, :]
        rows = [at_gain / gain_ref[...], norm_sums[1:2, :], feed_sums_ref[...]]
        units = b_up_ref.shape[1]
        per_row = model // units
        for r in range(8 // per_row):
            row = [jnp.where(seq.me == r * per_row + c, b_up_ref[...], 0.0) for c in range(per_row)]
            rows.append(jnp.concatenate(row, axis=1))
        rows.append(jnp.zeros((SUM_ROWS - 6 - 8 // per_row, model), WIDE))
        pay_ref[MEMROWS:, :] = jnp.concatenate(rows, axis=0).astype(LOW)
        pay_core().start()

    def pay_send_parts():
        pay_core().wait_recv()
        pay_half[...] = (half_of(head.core)[...].astype(WIDE) + core_land[...].astype(WIDE)).astype(LOW)
        pay_land[plane.me] = pay_part(plane.me)[...]
        pay.start(pay_part, pay_land)

    def pay_sum():
        pay.wait(pay_land)
        sums = pay_land[0].astype(WIDE)
        for i in range(1, 8):
            sums += pay_land[i].astype(WIDE)
        small_ref[head.core, plane.me, :MEMROWS, :] = sums[:MEMROWS].astype(LOW)
        used = 6 + 8 * b_up_ref.shape[1] // model
        rows = [sums[MEMROWS : MEMROWS + used]]
        rows += [bias_sums_ref[:, i * width : (i + 1) * width] for i in range(3)]
        rows.append(jnp.zeros((SUM_ROWS - 3 - used, share), WIDE))
        seq_land[seq.me] = jnp.concatenate(rows, axis=0).astype(LOW)
        across.start(lambda i: seq_land.at[seq.me], seq_land)

    def pay_back():
        across.wait(seq_land)
        sums = seq_land[0].astype(WIDE)
        for i in range(1, 8):
            sums += seq_land[i].astype(WIDE)
        small_ref[head.core, plane.me, MEMROWS:, :] = sums.astype(LOW)
        back.start(lambda i: small_ref.at[head.core, plane.me], small_ref.at[head.core])

    def pay_end():
        back.wait(small_ref.at[head.core])
        pay_whole().start()

    chunk(0)
    chunk(1)
    load.wait()
    lax.fori_loop(0, 2, weights, 0)
    w_reduce.settle(2, 1)
    w_reduce.settle(2, 0)
    reduce.settle(2, 1)
    reduce.settle(2, 0)
    lax.fori_loop(2, 4, weights, 0)
    w_reduce.settle(1, 1)
    w_reduce.settle(-1, 1)
    chunk(2)
    chunk(3)
    lax.fori_loop(4, 6, weights, 0)
    w_reduce.settle(1, 0)
    w_reduce.settle(-1, 0)
    reduce.settle(1, 1)
    reduce.settle(-1, 1)
    lax.fori_loop(6, 7, weights, 0)
    w_reduce.settle(0, 1)
    lax.fori_loop(7, 8, weights, 0)
    shift_sums()
    pay_start()
    chunk(4)
    chunk(5)
    pay_send_parts()
    reduce.settle(1, 0)
    reduce.settle(-1, 0)
    w_reduce.settle(0, 0)
    grad_w_ref[seq.me] = w_total[7].astype(LOW)
    gather.arrive(0, 0)
    chunk(6)
    chunk(7)
    gather.arrive(-1, 0)
    gather.arrive(1, 0)
    gather.arrive(0, 1)
    pay_sum()
    reduce.settle(0, 1)
    gather.arrive(2, 0)
    gather.arrive(-1, 1)
    gather.arrive(1, 1)
    pay_back()
    reduce.settle(0, 0)
    pay_end()
    gather.arrive(2, 1)
    core_copy(1, small_ref.at[1 - head.core], small_ref.at[1 - head.core]).wait_recv()
    pay_core().wait_send()
    pay_whole().wait_send()
    pay.drain(pay_part, pay_land)
    across.drain(lambda i: seq_land.at[seq.me], seq_land)
    back.drain(lambda i: small_ref.at[head.core, plane.me], small_ref.at[head.core])
    gather.drain()
    w_reduce.drain()
    reduce.drain()


def close_layer(
    own, own_t, mem, mem_t, grad_wo, mem_normed, normed_all, w_t, gain, shift, bias_sums,
    feed_sums, b_up,
):
    rows, model = normed_all.shape[1:]
    width = grad_wo.shape[0]
    sems = [pltpu.SemaphoreType.DMA((Gather.COPIES,))] * 2
    pay_rows = MEMROWS + SUM_ROWS
    return pl.pallas_call(
        close_kernel,
        out_shape=(
            jax.ShapeDtypeStruct((rows, model), WIDE),
            jax.ShapeDtypeStruct((8, width, model // 2), LOW),
            jax.ShapeDtypeStruct((2, 8, pay_rows, model // 16), LOW),
        ),
        in_specs=[VMEM] * 6 + [ANY] + [VMEM] * 6,
        out_specs=(VMEM,) * 3,
        scratch_shapes=[
            pltpu.VMEM((16, rows, model), LOW),
            pltpu.VMEM((3 * width, MEMROWS), LOW),
            pltpu.VMEM((8, model), WIDE),
            pltpu.VMEM((pay_rows, model), LOW),
            pltpu.VMEM((pay_rows, model // 2), LOW),
            pltpu.VMEM((pay_rows, model // 2), LOW),
            pltpu.VMEM((8, pay_rows, model // 16), LOW),
            pltpu.VMEM((8, SUM_ROWS, model // 16), LOW),
            pltpu.SemaphoreType.DMA((2,)),
            pltpu.SemaphoreType.DMA((2,)),
            pltpu.SemaphoreType.DMA((8,)),
            pltpu.SemaphoreType.DMA((8,)),
            pltpu.SemaphoreType.DMA((8,)),
            pltpu.SemaphoreType.DMA((8,)),
            pltpu.SemaphoreType.DMA((8,)),
            pltpu.SemaphoreType.DMA((8,)),
            pltpu.SemaphoreType.DMA,
        ] + Reduce.scratch(model, True, True) + Reduce.scratch(model // 2, True, False) + sems,
        compiler_params=pltpu.CompilerParams(
            collective_id=4, has_side_effects=True, vmem_limit_bytes=VMEM_LIMIT
        ),
        name="close_layer",
    )(
        own, own_t, mem, mem_t, grad_wo, mem_normed, normed_all, w_t, gain, shift, bias_sums,
        feed_sums, b_up,
    )


def finish_kernel(
    grad_normed_hbm, hidden_hbm, grad_resid_hbm, gain_ref, grad_w_hbm, small_ref, memory_ref,
    feed_w_hbm, output_hbm,
    out_hbm, grad_hidden_hbm, grad_memory_ref, grad_qkv_hbm, b_query_ref, b_value_ref, grad_wo_hbm,
    b_out_ref, gain_one_ref, shift_one_ref, gain_two_ref, shift_two_ref,
    w_up_hbm, b_up_ref, w_down_hbm, b_down_ref,
    grad_w_ref, grad_normed_ref, hidden_ref, grad_resid_ref, feed_w_ref, output_ref,
    grad_qkv_ref, grad_wo_ref, w_down_ref, grad_hidden_ref, mem_wide, spread_ref, load_sem, out_sem,
):
    wide, units = grad_w_ref.shape[2], w_up_hbm.shape[1]
    loads = [
        pltpu.make_async_copy(src, dst, load_sem.at[i])
        for i, (src, dst) in enumerate(
            (
                (grad_w_hbm, grad_w_ref), (grad_normed_hbm, grad_normed_ref), (hidden_hbm, hidden_ref),
                (grad_resid_hbm, grad_resid_ref), (feed_w_hbm, feed_w_ref), (output_hbm, output_ref),
            )
        )
    ]
    for load in loads:
        load.start()
    outs = []

    def leave(src, dst):
        out = pltpu.make_async_copy(src, dst, out_sem.at[len(outs)])
        out.start()
        outs.append(out)

    share = small_ref.shape[3]
    for i in range(16):
        spread_ref[:, i * share : (i + 1) * share] = small_ref[i // 8, i % 8].astype(WIDE)

    def norm_back(values, incoming):
        normal, rstd = normal_of(values)
        scaled = incoming * gain_ref[...]
        inner = jnp.mean(scaled, axis=-1, keepdims=True)
        along = jnp.mean(scaled * normal, axis=-1, keepdims=True)
        return rstd * (scaled - inner - normal * along)

    def back(rows):
        grad_hidden = grad_resid_ref[rows] + norm_back(
            hidden_ref[rows].astype(WIDE), grad_normed_ref[rows]
        )
        grad_hidden_ref[rows] = grad_hidden[:, None, :]

    loads[0].wait()
    for i in range(3):
        for j in range(2):
            grad_qkv_ref[i, j * wide : (j + 1) * wide, :] = grad_w_ref[2 * i + j].astype(WIDE).T
        leave(grad_qkv_ref.at[i], grad_qkv_hbm.at[i])
    for j in range(2):
        grad_wo_ref[:, j * wide : (j + 1) * wide] = grad_w_ref[6 + j].astype(WIDE)
    leave(grad_wo_ref, grad_wo_hbm)
    for load in loads[1:]:
        load.wait()
    leave(output_ref, out_hbm)
    leave(feed_w_ref.at[:, pl.ds(0, units)], w_up_hbm)
    w_down_ref[...] = feed_w_ref[:, units:].T
    leave(w_down_ref, w_down_hbm)
    row_tiles(hidden_ref.shape[0], back, 32)
    leave(grad_hidden_ref, grad_hidden_hbm)
    slots = memory_ref.shape[0]
    mem_wide[...] = jnp.zeros_like(mem_wide)
    mem_wide[:slots, :] = memory_ref[...].astype(WIDE)

    def back_memory(rows):
        mem_wide[rows] = norm_back(mem_wide[rows], spread_ref[rows])

    row_tiles(MEMROWS, back_memory, 32)
    grad_memory_ref[...] = mem_wide[:slots, :][:, None, :]
    sums = [spread_ref[MEMROWS + i : MEMROWS + i + 1, :] for i in range(SUM_ROWS)]
    ordered = (gain_one_ref, shift_one_ref, b_out_ref, gain_two_ref, shift_two_ref, b_down_ref)
    for ref, row in zip(ordered, sums):
        ref[...] = row
    model = b_out_ref.shape[1]
    for i in range(4):
        b_up_ref[:, i * model : (i + 1) * model] = sums[6 + i]
    index = lax.axis_index("head")
    mine = small_ref[index % 2, index // 2].astype(WIDE)
    b_query_ref[...] = mine[MEMROWS + 10 : MEMROWS + 11, :]
    b_value_ref[...] = mine[MEMROWS + 12 : MEMROWS + 13, :]
    for out in outs:
        out.wait()


def finish_layer(
    grad_normed, hidden, grad_resid, gain, grad_w, small, memory, feed_w, output
):
    rows, model = hidden.shape
    width, units = grad_w.shape[1], feed_w.shape[1] // 2
    wide = lambda *shape: jax.ShapeDtypeStruct(shape, WIDE)
    return pl.pallas_call(
        finish_kernel,
        out_shape=(
            jax.ShapeDtypeStruct((rows, model), LOW), wide(rows, 1, model), wide(memory.shape[0], 1, model),
            wide(3, model, width), wide(1, width), wide(1, width), wide(width, model),
            wide(1, model), wide(1, model), wide(1, model), wide(1, model), wide(1, model),
            wide(rows, units), wide(1, 8 * units), wide(units, rows), wide(1, model),
        ),
        in_specs=[ANY] * 3 + [VMEM, ANY, VMEM, VMEM, ANY, ANY],
        out_specs=(ANY, ANY, VMEM, ANY, VMEM, VMEM, ANY) + (VMEM,) * 5 + (ANY, VMEM, ANY, VMEM),
        scratch_shapes=[
            pltpu.VMEM(grad_w.shape, LOW),
            pltpu.VMEM((rows, model), WIDE),
            pltpu.VMEM((rows, model), LOW),
            pltpu.VMEM((rows, model), WIDE),
            pltpu.VMEM(feed_w.shape, WIDE),
            pltpu.VMEM((rows, model), LOW),
            pltpu.VMEM((3, model, width), WIDE),
            pltpu.VMEM((width, model), WIDE),
            pltpu.VMEM((units, rows), WIDE),
            pltpu.VMEM((rows, 1, model), WIDE),
            pltpu.VMEM((MEMROWS, model), WIDE),
            pltpu.VMEM((MEMROWS + SUM_ROWS, model), WIDE),
            pltpu.SemaphoreType.DMA((6,)),
            pltpu.SemaphoreType.DMA((8,)),
        ],
        compiler_params=pltpu.CompilerParams(vmem_limit_bytes=VMEM_LIMIT),
        name="finish_layer",
    )(grad_normed, hidden, grad_resid, gain, grad_w, small, memory, feed_w, output)


def on_device(
    hidden, memory, counts, w_qkv, b_query, b_value, output_weight, b_out,
    gain_one, shift_one, gain_two, shift_two, w_up, up_bias, w_down, b_down, cotangent,
):
    hidden, memory, cot = hidden[:, 0], memory[:, 0], cotangent[:, 0]
    model = hidden.shape[1]
    width = w_qkv.shape[2]
    w_parts = jnp.transpose(w_qkv, (1, 0, 2))
    gain_one, shift_one, gain_two, shift_two, b_out, b_down, b_query, b_value, up_bias = (
        vector[None]
        for vector in (
            gain_one, shift_one, gain_two, shift_two, b_out, b_down, b_query, b_value, up_bias
        )
    )
    q, k, v, mk, mv, mem_normed, mem_bias, tail_bias, w_t, normed_all = open_layer(
        hidden, memory, counts, gain_one, shift_one, w_parts, b_query, b_value
    )
    attn_t, lse, resid, second, w_up_t, cot_all = attend_layer(
        q, k, v, mk, mv, mem_bias, tail_bias, output_weight, hidden, b_out, gain_two, shift_two,
        cot, w_up,
    )
    grad_resid, feed_sums, branch, feed_w, grad_b_up = feed_layer(
        second, w_up, w_up_t, w_down, cot_all, up_bias, resid, gain_two, cot
    )
    output, own, own_t, mem, mem_t, grad_wo, bias_sums = grad_layer(
        grad_resid, resid, b_down, branch, output_weight,
        q, k, v, mk, mv, mem_bias, tail_bias, attn_t, lse,
    )
    grad_normed, grad_w, small = close_layer(
        own, own_t, mem, mem_t, grad_wo, mem_normed, normed_all, w_t, gain_one, shift_one,
        bias_sums, feed_sums, grad_b_up,
    )
    outs = finish_layer(
        grad_normed, hidden, grad_resid, gain_one, grad_w, small, memory, feed_w, output
    )
    output, grad_hidden, grad_memory, grad_w_qkv, *rest = outs
    rest = [part[0] if part.shape[0] == 1 else part for part in rest]
    return (
        output[:, None],
        grad_hidden,
        grad_memory,
        jnp.transpose(grad_w_qkv, (1, 0, 2)),
        *rest,
    )


def solution(mesh):
    return jax.shard_map(
        on_device,
        mesh=mesh,
        in_specs=(
            P("head", "seq", None),
            P(None, "seq", None),
            P("seq", None),
            P(None, None, "head"),
            P("head"),
            P("head"),
            P("head", None),
            P(),
            P(),
            P(),
            P(),
            P(),
            P(None, "seq"),
            P(),
            P("seq", None),
            P(),
            P("head", "seq", None),
        ),
        out_specs=(
            P("head", "seq", None),
            P("head", "seq", None),
            P(None, "seq", None),
            P(None, None, "head"),
            P("head"),
            P("head"),
            P("head", None),
            P(),
            P(),
            P(),
            P(),
            P(),
            P("head", "seq"),
            P(),
            P("seq", "head"),
            P(),
        ),
        check_vma=False,
    )
```

```python
import jax
import jax.numpy as jnp
from jax import lax
from jax.experimental import pallas as pl
from jax.experimental.pallas import tpu as pltpu
from jax.sharding import PartitionSpec as P

HDIM = 64
EPSILON = 1e-05
NEGATIVE = -1e30
LOW = jnp.bfloat16
WIDE = jnp.float32
QROWS = 256
KROWS = 512
MEMROWS = 64
BLOCK = 128
NEAR_FIRST = ((0, 0), (-1, 0), (1, 0), (0, 1), (2, 0), (-1, 1), (1, 1), (2, 1))
FAR_FIRST = ((2, 1), (2, 0), (1, 1), (-1, 1), (1, 0), (-1, 0), (0, 1), (0, 0))
MESH = pl.DeviceIdType.MESH
VMEM = pl.BlockSpec(memory_space=pltpu.VMEM)
ANY = pl.BlockSpec(memory_space=pl.ANY)
VMEM_LIMIT = 60 * 2**20


def dot(left, right):
    return jnp.dot(left, right, preferred_element_type=WIDE)


def dot_nt(left, right):
    return lax.dot_general(left, right, (((1,), (1,)), ((), ())), preferred_element_type=WIDE)


def dot_tn(left, right):
    return lax.dot_general(left, right, (((0,), (0,)), ((), ())), preferred_element_type=WIDE)


def row_tiles(rows, body, step=16):
    def run(i, carry):
        body(pl.ds(pl.multiple_of(i * step, step), step))
        return carry

    lax.fori_loop(0, rows // step, run, 0)


class Group:
    def __init__(self, axis):
        self.axis = axis
        index = lax.axis_index(axis)
        self.me = index
        self.cores = 2 if axis == "head" else 1
        self.size = 8 * self.cores
        self.core = index % self.cores
        self.pair = index // self.cores % 2
        self.ring = index // (2 * self.cores)

    def chip(self, dr, dp):
        pair = 1 - self.pair if dp else self.pair
        return (self.ring + (dr + 4)) % 4 * 2 + pair

    def block(self, dr, dp, dc=0):
        core = 1 - self.core if dc else self.core
        return self.chip(dr, dp) * self.cores + core

    def device(self, dr, dp, dc=0):
        return {self.axis: self.block(dr, dp, dc)}

    def ahead(self, step):
        return (self.me + step) % self.size

    def away(self, step):
        return {self.axis: self.ahead(step)}

    def greet(self, barrier):
        peers = [(1, 0, 0), (-1, 0, 0), (0, 1, 0)] + ([(0, 0, 1)] if self.cores == 2 else [])
        for peer in peers:
            pl.semaphore_signal(barrier, 1, device_id=self.device(*peer), device_id_type=MESH)
        return len(peers)


def greet_all(*groups):
    barrier = pltpu.get_barrier_semaphore()
    pl.semaphore_wait(barrier, sum(group.greet(barrier) for group in groups))


class Gather:
    COPIES = 21

    def __init__(self, group, buf, send, recv, cut=BLOCK):
        self.group, self.buf, self.send, self.recv = group, buf, send, recv
        half = BLOCK // 2
        low = (cut // 2 + 15) // 16 * 16
        every, upper = (0, BLOCK), (cut, BLOCK - cut)
        ops = {
            "v0": ((0, 0), (1, 0, 0), every, (-1, 0)),
            "n0": ((0, 0), (-1, 0, 0), every, (1, 0)),
            "pair": ((0, 0), (0, 1, 0), every, (0, 1)),
            "v0h": ((-1, 0), (1, 0, 0), (0, half), (2, 0)),
            "n0h": ((1, 0), (-1, 0, 0), (half, half), (2, 0)),
            "v1": ((0, 1), (1, 0, 0), (0, cut), (-1, 1)),
            "n1": ((0, 1), (-1, 0, 0), (0, cut), (1, 1)),
            "v1h": ((-1, 1), (1, 0, 0), (0, low), (2, 1)),
            "n1h": ((1, 1), (-1, 0, 0), (low, cut - low), (2, 1)),
            "bv": ((-1, 0), (0, 1, 0), upper, (-1, 1)),
            "bn": ((1, 0), (0, 1, 0), upper, (1, 1)),
            "b2": ((2, 0), (0, 1, 0), upper, (2, 1)),
        }
        if group.cores == 2:
            for place in NEAR_FIRST:
                ops["s%d%d" % place] = (place, (0, 0, 1), every, place)
        self.ops = {name: (i,) + op for i, (name, op) in enumerate(ops.items()) if op[2][1] > 0}
        self.started = []
        self.inward = {
            (0, 0): (),
            (-1, 0): ("v0",),
            (1, 0): ("n0",),
            (0, 1): ("pair",),
            (2, 0): ("v0h", "n0h"),
            (-1, 1): ("v1", "bv"),
            (1, 1): ("n1", "bn"),
            (2, 1): ("v1h", "n1h", "b2"),
        }
        self.outward = {
            (0, 0): ("v0", "n0", "pair"),
            (-1, 0): ("v0h", "bv"),
            (1, 0): ("n0h", "bn"),
            (0, 1): ("v1", "n1"),
            (2, 0): ("b2",),
            (-1, 1): ("v1h",),
            (1, 1): ("n1h",),
            (2, 1): (),
        }

    def copy(self, name, arriving):
        i, place, peer, (start, count), source = self.ops[name]
        sibling = 1 if arriving and name[0] == "s" else 0
        block = self.group.block(*(source if arriving else place), sibling)
        view = self.buf.at[block] if count == BLOCK else self.buf.at[block, pl.ds(start, count)]
        return pltpu.make_async_remote_copy(
            src_ref=view,
            dst_ref=view,
            send_sem=self.send.at[i],
            recv_sem=self.recv.at[i],
            device_id=self.group.device(*peer),
            device_id_type=MESH,
        )

    def arrive(self, *place):
        for name in self.inward[place]:
            if name in self.ops:
                self.copy(name, True).wait_recv()
        names = self.outward[place]
        if self.group.cores == 2:
            names += ("s%d%d" % place,)
        for name in names:
            if name in self.ops:
                self.copy(name, False).start()
                self.started.append(name)

    def sibling(self, *place):
        if self.group.cores == 2:
            self.copy("s%d%d" % place, True).wait_recv()

    def drain(self):
        for name in self.started:
            self.copy(name, False).wait_send()


class Reduce:
    COPIES = 21

    def __init__(self, group, total, stage, land, send, recv, cut=BLOCK, near=None, result=None):
        self.group, self.total, self.land = group, total, land
        self.stage = total if stage is None else stage
        self.staged = stage is not None
        self.send, self.recv, self.near, self.result = send, recv, near, result
        half = BLOCK // 2
        low = (cut // 2 + 15) // 16 * 16
        every, upper = (0, BLOCK), (cut, BLOCK - cut)
        ops = {
            "b2": ((2, 1), (0, 1, 0), upper, 0),
            "n1h": ((2, 1), (1, 0, 0), (0, low), 1),
            "v1h": ((2, 1), (-1, 0, 0), (low, cut - low), 1),
            "n0h": ((2, 0), (1, 0, 0), (0, half), 2),
            "v0h": ((2, 0), (-1, 0, 0), (half, half), 2),
            "bn": ((1, 1), (0, 1, 0), upper, 3),
            "bv": ((-1, 1), (0, 1, 0), upper, 4),
            "n1": ((1, 1), (1, 0, 0), (0, cut), 3),
            "v1": ((-1, 1), (-1, 0, 0), (0, cut), 4),
            "n0": ((1, 0), (1, 0, 0), every, 5),
            "v0": ((-1, 0), (-1, 0, 0), every, 6),
            "pu": ((0, 1), (0, 1, 0), upper, 7),
            "pl": ((0, 1), (0, 1, 0), (0, cut), 7),
        }
        self.ops = {name: (i,) + op for i, (name, op) in enumerate(ops.items()) if op[2][1] > 0}
        self.cut = cut
        self.started = []
        self.early = {(1, 1): "bn", (-1, 1): "bv", (0, 1): "pu"}
        self.inward = {
            (2, 1): (),
            (2, 0): ("b2",),
            (1, 1): ("n1h",),
            (-1, 1): ("v1h",),
            (1, 0): ("bn", "n0h"),
            (-1, 0): ("bv", "v0h"),
            (0, 1): ("n1", "v1"),
            (0, 0): ("pu", "n0", "v0", "pl"),
        }
        self.outward = {
            (2, 1): ("b2", "n1h", "v1h"),
            (2, 0): ("n0h", "v0h"),
            (1, 1): ("n1",),
            (-1, 1): ("v1",),
            (1, 0): ("n0",),
            (-1, 0): ("v0",),
            (0, 1): ("pl",),
            (0, 0): (),
        }

    def copy(self, name):
        i, place, peer, (start, count), slot = self.ops[name]
        return pltpu.make_async_remote_copy(
            src_ref=self.stage.at[FAR_FIRST.index(place), pl.ds(start, count)],
            dst_ref=self.land.at[slot, pl.ds(start, count)],
            send_sem=self.send.at[i],
            recv_sem=self.recv.at[i],
            device_id=self.group.device(*peer),
            device_id_type=MESH,
        )

    def near_copy(self, k):
        return pltpu.make_async_remote_copy(
            src_ref=self.near[0].at[k],
            dst_ref=self.near[1].at[k],
            send_sem=self.send.at[13 + k],
            recv_sem=self.recv.at[13 + k],
            device_id=self.group.device(0, 0, 1),
            device_id_type=MESH,
        )

    def begin(self, name):
        self.copy(name).start()
        self.started.append(name)

    def blend(self, place, start, count, names):
        k = FAR_FIRST.index(place)
        spans = [self.ops[name][3] + (self.ops[name][4],) for name in names]
        marks = {start, start + count}
        for first, size, _ in spans:
            marks |= {m for m in (first, first + size) if start < m < start + count}
        marks = sorted(marks)
        for low, high in zip(marks, marks[1:]):
            slots = [slot for first, size, slot in spans if first <= low and high <= first + size]
            if not (slots or self.near or self.staged or place == (0, 0)):
                continue

            step = 32 if (high - low) % 32 == 0 else 16

            def body(rows):
                at = pl.ds(pl.multiple_of(rows.start + low, 16), step)
                value = self.total[k, at].astype(WIDE)
                if self.near is not None:
                    value += self.near[1][k, at].astype(WIDE)
                for slot in slots:
                    value += self.land[slot, at].astype(WIDE)
                if place == (0, 0):
                    self.result[at] = value
                else:
                    self.stage[k, at] = value.astype(LOW)

            row_tiles(high - low, body, step)

    def settle(self, *place):
        if self.near is not None:
            self.near_copy(FAR_FIRST.index(place)).wait_recv()
        rest = BLOCK
        early = self.early.get(place)
        if early in self.ops:
            rest = self.cut
            self.blend(place, self.cut, BLOCK - self.cut, ())
            self.begin(early)
        names = [name for name in self.inward[place] if name in self.ops]
        for name in names:
            self.copy(name).wait_recv()
        self.blend(place, 0, rest, names)
        for name in self.outward[place]:
            if name in self.ops:
                self.begin(name)

    def drain(self):
        for name in self.started:
            self.copy(name).wait_send()
        if self.near is not None:
            for k in range(8):
                self.near_copy(k).wait_send()

    @staticmethod
    def scratch(columns, staged, near):
        part = pltpu.VMEM((8, BLOCK, columns), LOW)
        shapes = [pltpu.VMEM((8, BLOCK, columns), WIDE), part] if staged else [part]
        shapes += [part] + [pltpu.SemaphoreType.DMA((Reduce.COPIES,))] * 2
        return shapes + [part] * 2 if near else shapes


class Plane:
    def __init__(self, head):
        self.core, self.me, self.size = head.core, head.chip(0, 0), 8

    def ahead(self, step):
        return (self.me + step) % self.size

    def away(self, step):
        return {"head": self.ahead(step) * 2 + self.core}


def greet_everyone(head, *groups):
    barrier = pltpu.get_barrier_semaphore()
    pl.semaphore_signal(barrier, 1, device_id=head.device(0, 0, 1), device_id_type=MESH)
    for group in groups:
        def signal(step, carry):
            pl.semaphore_signal(barrier, 1, device_id=group.away(step), device_id_type=MESH)
            return carry

        lax.fori_loop(1, group.size, signal, 0)
    pl.semaphore_wait(barrier, 1 + sum(group.size - 1 for group in groups))


class Spread:
    def __init__(self, group, send, recv):
        self.group, self.send, self.recv = group, send, recv

    def copy(self, step, src, dst):
        return pltpu.make_async_remote_copy(
            src_ref=src,
            dst_ref=dst,
            send_sem=self.send.at[step],
            recv_sem=self.recv.at[step],
            device_id=self.group.away(step),
            device_id_type=MESH,
        )

    def each(self, body):
        def run(step, carry):
            body(step)
            return carry

        lax.fori_loop(1, self.group.size, run, 0)

    def start(self, src_of, land):
        self.each(lambda step: self.copy(step, src_of(self.group.ahead(step)), land.at[self.group.me]).start())

    def wait(self, land):
        def one(step):
            slot = land.at[self.group.ahead(self.group.size - step)]
            self.copy(step, slot, slot).wait_recv()

        self.each(one)

    def drain(self, src_of, land):
        self.each(lambda step: self.copy(step, src_of(self.group.ahead(step)), land.at[self.group.me]).wait_send())


def normal_of(values):
    mean = jnp.mean(values, axis=-1, keepdims=True)
    centered = values - mean
    var = jnp.mean(centered * centered, axis=-1, keepdims=True)
    rstd = lax.rsqrt(var + EPSILON)
    return centered * rstd, rstd


def stack_heads(rows):
    lane = lax.broadcasted_iota(jnp.int32, rows.shape, 1)
    zero = jnp.zeros_like(rows)
    return jnp.concatenate(
        [jnp.where(lane < HDIM, rows, zero), jnp.where(lane < HDIM, zero, rows)], axis=0
    )


def causal_bias(chunk, block, tail_bias):
    key = block * KROWS + lax.broadcasted_iota(jnp.int32, (KROWS, 2 * QROWS), 0)
    lane = lax.broadcasted_iota(jnp.int32, (KROWS, 2 * QROWS), 1)
    query = chunk * QROWS + jnp.where(lane < QROWS, lane, lane - QROWS)
    own = jnp.where(block == 2048 // KROWS - 1, tail_bias, jnp.zeros_like(tail_bias))
    return jnp.where(key <= query, jnp.broadcast_to(own, key.shape), NEGATIVE)


def transpose_into(dst_ref, src_ref):
    rows = src_ref.shape[0]
    if rows <= 256:
        dst_ref[...] = src_ref[...].T
        return

    def body(i, carry):
        at = pl.multiple_of(i * 256, 256)
        dst_ref[:, pl.ds(at, 256)] = src_ref[pl.ds(at, 256), :].T
        return carry

    lax.fori_loop(0, rows // 256, body, 0)


def attend_chunk(chunk, q_ref, k_ref, vt_ref, mk_ref, mvt_ref, mem_bias, tail_bias):
    start = pl.multiple_of(chunk * QROWS, QROWS)
    q2 = stack_heads(q_ref[pl.ds(start, QROWS), :] * HDIM ** (-0.5))

    def values_times(values_t, probs):
        low = probs.astype(LOW)
        return (
            dot(values_t[:HDIM], low[:, :QROWS]),
            dot(values_t[HDIM:], low[:, QROWS:]),
        )

    scores = dot_nt(mk_ref[...], q2) + mem_bias
    peak = jnp.max(scores, axis=0, keepdims=True)
    raised = jnp.exp(scores - peak)
    total = jnp.sum(raised, axis=0, keepdims=True)
    first, second = values_times(mvt_ref[...], raised)

    def update(block, scores, carry):
        peak, total, first, second = carry
        at = pl.multiple_of(block * KROWS, KROWS)
        new_peak = jnp.maximum(peak, jnp.max(scores, axis=0, keepdims=True))
        scale = jnp.exp(peak - new_peak)
        raised = jnp.exp(scores - new_peak)
        total = total * scale + jnp.sum(raised, axis=0, keepdims=True)
        add_first, add_second = values_times(vt_ref[:, pl.ds(at, KROWS)], raised)
        return (
            new_peak,
            total,
            first * scale[:, :QROWS] + add_first,
            second * scale[:, QROWS:] + add_second,
        )

    def block_scores(block):
        at = pl.multiple_of(block * KROWS, KROWS)
        return dot_nt(k_ref[pl.ds(at, KROWS), :], q2)

    full = chunk * QROWS // KROWS
    carry = lax.fori_loop(
        0, full, lambda b, c: update(b, block_scores(b), c), (peak, total, first, second)
    )
    scores = block_scores(full) + causal_bias(chunk, full, tail_bias)
    peak, total, first, second = update(full, scores, carry)
    inverse = 1.0 / total
    attended = jnp.concatenate([first * inverse[:, :QROWS], second * inverse[:, QROWS:]], axis=0)
    return attended, peak + jnp.log(total)


def chip_at(group, order, step):
    return sum(jnp.where(step == j, group.chip(*place), 0) for j, place in enumerate(order))


def open_kernel(
    hidden_ref, memory_ref, counts_ref, gain_ref, shift_ref, w_ref, b_query_ref, b_value_ref,
    q_ref, k_ref, v_ref, mk_ref, mv_ref, mem_normed_ref, mem_bias_ref, tail_bias_ref, w_t_ref,
    normed_out,
    rows_buf, flat_w, mem_wide, send, recv, out_sem,
):
    head = Group("head")
    gather = Gather(head, rows_buf, send, recv, 64)
    own = head.block(0, 0)

    def norm_rows(rows):
        normal, _ = normal_of(hidden_ref[rows].astype(WIDE))
        rows_buf[own, rows] = (normal * gain_ref[...] + shift_ref[...]).astype(LOW)

    row_tiles(BLOCK, norm_rows, 32)
    greet_all(head)
    gather.arrive(0, 0)
    width = q_ref.shape[1]
    slots = memory_ref.shape[0]
    for i in range(3):
        flat_w[:, i * width : (i + 1) * width] = w_ref[i]
    copies = []

    def project(*place):
        gather.sibling(*place)
        chip = head.chip(*place)
        out = pltpu.make_async_copy(
            rows_buf.at[pl.ds(chip * 2, 2)], normed_out.at[pl.ds(chip * 2, 2)], out_sem.at[len(copies)]
        )
        out.start()
        copies.append(out)
        rows = rows_buf[pl.ds(chip * 2, 2)].reshape(2 * BLOCK, rows_buf.shape[2])
        at = pl.ds(pl.multiple_of(chip * 2 * BLOCK, 2 * BLOCK), 2 * BLOCK)
        all_parts = dot(rows, flat_w[...])
        q_ref[at, :] = (all_parts[:, :width] + b_query_ref[...]).astype(LOW)
        k_ref[at, :] = all_parts[:, width : 2 * width].astype(LOW)
        v_ref[at, :] = (all_parts[:, 2 * width :] + b_value_ref[...]).astype(LOW)

    def side_work():
        mem_wide[...] = jnp.zeros_like(mem_wide)
        mem_wide[:slots, :] = memory_ref[...].astype(WIDE)

        def norm_memory(rows):
            normal, _ = normal_of(mem_wide[rows])
            mem_normed_ref[rows] = (normal * gain_ref[...] + shift_ref[...]).astype(LOW)

        row_tiles(MEMROWS, norm_memory, 32)
        mem = dot(mem_normed_ref[...], flat_w[:, width:])
        mk_ref[...] = mem[:, :width].astype(LOW)
        mv_ref[...] = (mem[:, width:] + b_value_ref[...]).astype(LOW)
        slot = lax.broadcasted_iota(jnp.int32, mem_bias_ref.shape, 0)
        mem_bias_ref[...] = jnp.where(slot < counts_ref[0, 0], 0.0, NEGATIVE)
        tail = slots - KROWS + lax.broadcasted_iota(jnp.int32, tail_bias_ref.shape, 0)
        tail_bias_ref[...] = jnp.where((tail < 0) | (tail < counts_ref[0, 1]), 0.0, NEGATIVE)
        for i in range(3):
            transpose_into(w_t_ref.at[pl.ds(i * width, width)], w_ref.at[i])

    side_work()
    project(0, 0)
    gather.arrive(-1, 0)
    gather.arrive(1, 0)
    gather.arrive(0, 1)
    project(-1, 0)
    project(1, 0)
    gather.arrive(2, 0)
    project(0, 1)
    gather.arrive(-1, 1)
    gather.arrive(1, 1)
    project(2, 0)
    project(-1, 1)
    project(1, 1)
    gather.arrive(2, 1)
    project(2, 1)
    gather.drain()
    for out in copies:
        out.wait()


def open_layer(hidden, memory, counts, gain, shift, w, b_query, b_value):
    rows, model = hidden.shape
    width = w.shape[2]
    part = jax.ShapeDtypeStruct((16 * rows, width), LOW)
    mem_part = jax.ShapeDtypeStruct((MEMROWS, width), LOW)
    sems = [pltpu.SemaphoreType.DMA((Gather.COPIES,))] * 2
    smem = pl.BlockSpec(memory_space=pltpu.SMEM)
    return pl.pallas_call(
        open_kernel,
        out_shape=(
            part, part, part, mem_part, mem_part,
            jax.ShapeDtypeStruct((MEMROWS, model), LOW),
            jax.ShapeDtypeStruct((MEMROWS, 1), WIDE),
            jax.ShapeDtypeStruct((KROWS, 1), WIDE),
            jax.ShapeDtypeStruct((3 * width, model), LOW),
            jax.ShapeDtypeStruct((16, rows, model), LOW),
        ),
        in_specs=[VMEM] * 2 + [smem] + [VMEM] * 5,
        out_specs=(VMEM,) * 9 + (ANY,),
        scratch_shapes=[
            pltpu.VMEM((16, rows, model), LOW),
            pltpu.VMEM((model, 3 * width), LOW),
            pltpu.VMEM((MEMROWS, model), WIDE),
        ] + sems + [pltpu.SemaphoreType.DMA((8,))],
        compiler_params=pltpu.CompilerParams(
            collective_id=0, has_side_effects=True, vmem_limit_bytes=VMEM_LIMIT
        ),
        name="open_layer",
    )(hidden, memory, counts, gain, shift, w, b_query, b_value)


def attend_kernel(
    q_ref, k_ref, v_ref, mk_ref, mv_ref, mem_bias_ref, tail_bias_ref, wo_ref,
    hidden_ref, b_out_ref, gain_ref, shift_ref, cot_ref, w_up_hbm,
    attn_t_ref, lse_ref, resid_ref, second_ref, w_up_t_ref, cot_out,
    vt_ref, mvt_ref, attn_ref, cot_buf, wu_ref, load_sem, out_sem, cot_send, cot_recv,
    total, stage, land, send, recv, near_stage, near_land,
):
    head, seq = Group("head"), Group("seq")
    reduce = Reduce(head, total, stage, land, send, recv, 128, (near_stage, near_land), resid_ref)
    gather = Gather(seq, cot_buf, cot_send, cot_recv, 128)

    def keep_cot(*place):
        block = seq.block(*place)
        return pltpu.make_async_copy(
            cot_buf.at[block], cot_out.at[block], out_sem.at[NEAR_FIRST.index(place)]
        )

    load = pltpu.make_async_copy(w_up_hbm, wu_ref, load_sem)
    load.start()
    cot_buf[seq.me] = cot_ref[...]
    transpose_into(vt_ref, v_ref)
    transpose_into(mvt_ref, mv_ref)
    greet_all(head, seq)
    gather.arrive(0, 0)

    def step(k, carry):
        chip = chip_at(head, FAR_FIRST, k)
        start = pl.multiple_of(chip * QROWS, QROWS)
        attended, lse = attend_chunk(
            chip, q_ref, k_ref, vt_ref, mk_ref, mvt_ref, mem_bias_ref[...], tail_bias_ref[...]
        )
        attn_t_ref[:, pl.ds(start, QROWS)] = attended.astype(LOW)
        attn_ref[...] = attended.T.astype(LOW)
        lse_ref[chip] = lse
        mine = attn_ref[pl.ds(pl.multiple_of(head.core * BLOCK, BLOCK), BLOCK), :]
        other = attn_ref[pl.ds(pl.multiple_of((1 - head.core) * BLOCK, BLOCK), BLOCK), :]
        for at in range(0, total.shape[2], 512):
            near_stage[k, :, at : at + 512] = dot(other, wo_ref[:, at : at + 512]).astype(LOW)
        reduce.near_copy(k).start()
        for at in range(0, total.shape[2], 512):
            total[k, :, at : at + 512] = dot(mine, wo_ref[:, at : at + 512])
        for j, place in enumerate(FAR_FIRST[:-1]):
            @pl.when(k == j + 1)
            def _():
                reduce.settle(*place)

        @pl.when(k == 4)
        def _():
            gather.arrive(-1, 0)
            gather.arrive(1, 0)
            gather.arrive(0, 1)

        @pl.when(k == 6)
        def _():
            gather.arrive(2, 0)

        return carry

    lax.fori_loop(0, 8, step, 0)
    gather.arrive(-1, 1)
    gather.arrive(1, 1)
    for place in NEAR_FIRST[:-1]:
        keep_cot(*place).start()
    load.wait()
    transpose_into(w_up_t_ref, wu_ref)
    reduce.settle(0, 0)

    def finish(rows):
        resid = hidden_ref[rows].astype(WIDE) + resid_ref[rows] + b_out_ref[...]
        resid_ref[rows] = resid
        normal, _ = normal_of(resid)
        second_ref[rows] = (normal * gain_ref[...] + shift_ref[...]).astype(LOW)

    row_tiles(BLOCK, finish, 32)
    gather.arrive(2, 1)
    keep_cot(2, 1).start()
    gather.drain()
    reduce.drain()
    for place in NEAR_FIRST:
        keep_cot(*place).wait()


def attend_layer(
    q, k, v, mk, mv, mem_bias, tail_bias, wo, hidden, b_out, gain, shift, cot, w_up
):
    length, width = q.shape
    rows, model = hidden.shape
    units = w_up.shape[1]
    return pl.pallas_call(
        attend_kernel,
        out_shape=(
            jax.ShapeDtypeStruct((width, length), LOW),
            jax.ShapeDtypeStruct((length // QROWS, 1, 2 * QROWS), WIDE),
            jax.ShapeDtypeStruct((rows, model), WIDE),
            jax.ShapeDtypeStruct((rows, model), LOW),
            jax.ShapeDtypeStruct((units, model), LOW),
            jax.ShapeDtypeStruct((8, rows, model), LOW),
        ),
        in_specs=[VMEM] * 13 + [ANY],
        out_specs=(VMEM,) * 5 + (ANY,),
        scratch_shapes=[
            pltpu.VMEM((width, length), LOW),
            pltpu.VMEM((width, MEMROWS), LOW),
            pltpu.VMEM((QROWS, width), LOW),
            pltpu.VMEM((8, rows, model), LOW),
            pltpu.VMEM((model, units), LOW),
            pltpu.SemaphoreType.DMA,
            pltpu.SemaphoreType.DMA((8,)),
        ] + [pltpu.SemaphoreType.DMA((Gather.COPIES,))] * 2 + Reduce.scratch(model, True, True),
        compiler_params=pltpu.CompilerParams(
            collective_id=1, has_side_effects=True, vmem_limit_bytes=VMEM_LIMIT
        ),
        name="attend_layer",
    )(
        q, k, v, mk, mv, mem_bias, tail_bias, wo, hidden, b_out, gain, shift,
        cot, w_up,
    )


def gelu_parts(u):
    square = u * u
    t = jnp.tanh(0.7978845608 * (u + 0.044715 * (square * u)))
    half = 0.5 * (1.0 + t)
    slope = half + 0.5 * u * (1.0 - t * t) * (0.7978845608 * (1.0 + 0.134145 * square))
    return u * half, slope


def fold_rows(values):
    return jnp.sum(values.reshape(values.shape[0] // 8, 8, values.shape[1]), axis=0)


def feed_kernel(
    second_ref, w_up_hbm, w_up_t_hbm, w_down_hbm, cot_hbm, up_bias_ref, resid_ref, gain_ref,
    cot_ref,
    grad_resid_ref, sums_ref, branch_hbm, grad_w_ref, grad_b_up_ref,
    rows_buf, wu_ref, wut_ref, wd_ref, cot_buf, act_ref, back_ref, pre_ref, fold_ref, sum_fold, branch_buf,
    load_sem, branch_sem, send, recv,
    total, land, rsend, rrecv,
    w_total, w_land, w_send, w_recv, w_near_stage, w_near_land,
):
    head, seq = Group("head"), Group("seq")
    gather = Gather(seq, rows_buf, send, recv, 64)
    reduce = Reduce(seq, total, None, land, rsend, rrecv, 128, None, grad_resid_ref)
    w_reduce = Reduce(head, w_total, None, w_land, w_send, w_recv, 112, (w_near_stage, w_near_land), grad_w_ref)
    loads = [
        pltpu.make_async_copy(src, dst, load_sem.at[i])
        for i, (src, dst) in enumerate(
            (
                (cot_hbm, cot_buf), (w_down_hbm, wd_ref), (w_up_hbm, wu_ref), (w_up_t_hbm, wut_ref),
            )
        )
    ]
    for load in loads:
        load.start()
    own = seq.block(0, 0)
    rows_buf[own] = second_ref[...]
    fold_ref[...] = jnp.zeros_like(fold_ref)
    greet_all(head, seq)
    gather.arrive(0, 0)
    loads[0].wait()
    loads[1].wait()
    units = act_ref.shape[2]
    model = rows_buf.shape[2]
    bias_at = pl.ds(pl.multiple_of(own * units, units), units)

    def cot_times(i, carry):
        pairs = cot_buf[pl.ds(2 * i, 2)].reshape(2 * BLOCK, model)
        for at in range(0, units, 256):
            part = dot_nt(pairs, wd_ref[at : at + 256, :]).astype(LOW)
            back_ref[pl.ds(2 * i, 2), :, at : at + 256] = part.reshape(2, BLOCK, 256)
        return carry

    def feed(*place):
        block = seq.block(*place)
        pre_ref[...] = dot(rows_buf[block], wu_ref[...]) + up_bias_ref[:, bias_at]

        def bend(rows):
            activated, slope = gelu_parts(pre_ref[rows])
            grad_pre = back_ref[block, rows].astype(WIDE) * slope
            act_ref[block, rows] = activated.astype(LOW)
            back_ref[block, rows] = grad_pre.astype(LOW)
            fold_ref[...] += fold_rows(grad_pre)

        row_tiles(BLOCK, bend)
        k = FAR_FIRST.index(place)
        for at in range(0, model, 512):
            total[k, :, at : at + 512] = dot(back_ref[block], wut_ref[:, at : at + 512]).astype(LOW)

    lax.fori_loop(0, 4, cot_times, 0)
    loads[2].wait()
    loads[3].wait()
    feed(0, 0)
    gather.arrive(-1, 0)
    gather.arrive(1, 0)
    gather.arrive(0, 1)
    feed(-1, 0)
    gather.arrive(2, 0)
    feed(1, 0)
    gather.arrive(-1, 1)
    gather.arrive(1, 1)
    feed(0, 1)
    feed(2, 0)
    feed(-1, 1)
    feed(1, 1)
    gather.arrive(2, 1)
    feed(2, 1)
    reduce.settle(2, 1)
    reduce.settle(2, 0)
    grad_b_up_ref[...] = jnp.sum(fold_ref[...], axis=0, keepdims=True)

    def weights(k, carry):
        chip = chip_at(head, FAR_FIRST, k)

        def part(core):
            at = pl.ds(pl.multiple_of(chip * 2 * BLOCK + core * BLOCK, BLOCK), BLOCK)
            length = 8 * BLOCK
            up = dot_tn(
                rows_buf[:, :, at].reshape(length, BLOCK), back_ref[...].reshape(length, units)
            )
            down = dot_tn(
                cot_buf[:, :, at].reshape(length, BLOCK), act_ref[...].reshape(length, units)
            )
            return up.astype(LOW), down.astype(LOW)

        w_near_stage[k, :, :units], w_near_stage[k, :, units:] = part(1 - head.core)
        w_reduce.near_copy(k).start()
        w_total[k, :, :units], w_total[k, :, units:] = part(head.core)
        for j, place in enumerate(FAR_FIRST[:6]):
            @pl.when(k == j + 1)
            def _():
                w_reduce.settle(*place)

        @pl.when(k == 2)
        def _():
            reduce.settle(1, 1)
            reduce.settle(-1, 1)

        @pl.when(k == 5)
        def _():
            reduce.settle(1, 0)
            reduce.settle(-1, 0)

        return carry

    lax.fori_loop(0, 8, weights, 0)
    branch_copies = []

    def branch(i):
        slot = i % 2
        if i >= 2:
            branch_copies[i - 2].wait()
        for at in range(0, model, 512):
            branch_buf[slot, :, at : at + 512] = dot(act_ref[i], wd_ref[:, at : at + 512]).astype(LOW)
        copy = pltpu.make_async_copy(branch_buf.at[slot], branch_hbm.at[i], branch_sem.at[i])
        copy.start()
        branch_copies.append(copy)

    for i in range(4):
        branch(i)
    reduce.settle(0, 1)
    w_reduce.settle(0, 1)
    for i in range(4, 8):
        branch(i)
    reduce.settle(0, 0)
    sum_fold[...] = jnp.zeros_like(sum_fold)

    def back(rows):
        normal, rstd = normal_of(resid_ref[rows])
        incoming = grad_resid_ref[rows]
        scaled = incoming * gain_ref[...]
        inner = jnp.mean(scaled, axis=-1, keepdims=True)
        along = jnp.mean(scaled * normal, axis=-1, keepdims=True)
        cot = cot_ref[rows].astype(WIDE)
        grad = cot + rstd * (scaled - inner - normal * along)
        grad_resid_ref[rows] = grad
        for i, value in enumerate((grad, incoming * normal, incoming, cot)):
            sum_fold[i] += fold_rows(value)

    row_tiles(BLOCK, back)
    sums_ref[...] = jnp.sum(sum_fold[...], axis=1)
    w_reduce.settle(0, 0)
    for copy in branch_copies[-2:]:
        copy.wait()
    gather.drain()
    reduce.drain()
    w_reduce.drain()


def feed_layer(second, w_up, w_up_t, w_down, cot_all, up_bias, resid, gain, cot):
    rows, model = second.shape
    units = w_up.shape[1]
    gather_sems = [pltpu.SemaphoreType.DMA((Gather.COPIES,))] * 2
    return pl.pallas_call(
        feed_kernel,
        out_shape=(
            jax.ShapeDtypeStruct((rows, model), WIDE),
            jax.ShapeDtypeStruct((4, model), WIDE),
            jax.ShapeDtypeStruct((8, rows, model), LOW),
            jax.ShapeDtypeStruct((rows, 2 * units), WIDE),
            jax.ShapeDtypeStruct((1, units), WIDE),
        ),
        in_specs=[VMEM] + [ANY] * 4 + [VMEM] * 4,
        out_specs=(VMEM, VMEM, ANY, VMEM, VMEM),
        scratch_shapes=[
            pltpu.VMEM((8, rows, model), LOW),
            pltpu.VMEM((model, units), LOW),
            pltpu.VMEM((units, model), LOW),
            pltpu.VMEM((units, model), LOW),
            pltpu.VMEM((8, rows, model), LOW),
            pltpu.VMEM((8, rows, units), LOW),
            pltpu.VMEM((8, rows, units), LOW),
            pltpu.VMEM((rows, units), WIDE),
            pltpu.VMEM((8, units), WIDE),
            pltpu.VMEM((4, 8, model), WIDE),
            pltpu.VMEM((2, rows, model), LOW),
            pltpu.SemaphoreType.DMA((4,)),
            pltpu.SemaphoreType.DMA((8,)),
        ] + gather_sems + Reduce.scratch(model, False, False) + Reduce.scratch(2 * units, False, True),
        compiler_params=pltpu.CompilerParams(
            collective_id=2, has_side_effects=True, vmem_limit_bytes=VMEM_LIMIT
        ),
        name="feed_layer",
    )(second, w_up, w_up_t, w_down, cot_all, up_bias, resid, gain, cot)


def attend_back_chunk(
    chunk, q_ref, k_ref, kt_ref, v_ref, mk_ref, mkt_ref, mv_ref, mem_bias, tail_bias,
    attn_t_ref, lse_ref, grad_rows, dk_ref, dv_ref, dmk_ref, dmv_ref,
):
    start = pl.multiple_of(chunk * QROWS, QROWS)
    q2 = stack_heads(q_ref[pl.ds(start, QROWS), :] * HDIM ** (-0.5))
    g2 = stack_heads(grad_rows)
    product = grad_rows.astype(WIDE).T * attn_t_ref[:, pl.ds(start, QROWS)].astype(WIDE)
    inner = jnp.concatenate(
        [
            jnp.sum(product[:HDIM], axis=0, keepdims=True),
            jnp.sum(product[HDIM:], axis=0, keepdims=True),
        ],
        axis=1,
    )
    lse = lse_ref[chunk]

    def piece(scores, values, keys_t):
        probs = jnp.exp(scores - lse)
        grad_probs = dot_nt(values, g2)
        grad_scores = (probs * (grad_probs - inner)).astype(LOW)
        return (
            dot(probs.astype(LOW), g2),
            dot(grad_scores, q2),
            dot(keys_t[:HDIM], grad_scores[:, :QROWS]),
            dot(keys_t[HDIM:], grad_scores[:, QROWS:]),
        )

    dv, dk, first, second = piece(
        dot_nt(mk_ref[...], q2) + mem_bias, mv_ref[...], mkt_ref[...]
    )
    dmv_ref[...] += dv
    dmk_ref[...] += dk

    def block_step(block, bias, carry):
        first, second = carry
        at = pl.multiple_of(block * KROWS, KROWS)
        scores = dot_nt(k_ref[pl.ds(at, KROWS), :], q2)
        if bias is not None:
            scores = scores + bias
        dv, dk, add_first, add_second = piece(
            scores, v_ref[pl.ds(at, KROWS), :], kt_ref[:, pl.ds(at, KROWS)]
        )
        dv_ref[pl.ds(at, KROWS), :] += dv
        dk_ref[pl.ds(at, KROWS), :] += dk
        return first + add_first, second + add_second

    full = chunk * QROWS // KROWS
    carry = lax.fori_loop(0, full, lambda b, c: block_step(b, None, c), (first, second))
    first, second = block_step(full, causal_bias(chunk, full, tail_bias), carry)
    return jnp.concatenate([first, second], axis=0) * HDIM ** (-0.5)


def grad_kernel(
    grad_resid_ref, resid_ref, b_down_ref, branch_hbm, wo_ref,
    q_ref, k_ref, v_ref, mk_ref, mv_ref, mem_bias_ref, tail_bias_ref, attn_t_ref, lse_ref,
    out_ref, own_ref, own_t_ref, mem_ref, mem_t_ref, grad_wo_ref, sums_ref,
    rows_buf, kt_ref, mkt_ref, dk_ref, dv_ref, dmk_ref, dmv_ref, wo_sum, branch_sum, fold_ref,
    load_sem, send, recv, total, land, rsend, rrecv,
):
    head, seq = Group("head"), Group("seq")
    gather = Gather(head, rows_buf, send, recv, 64)
    reduce = Reduce(seq, total, None, land, rsend, rrecv, 128, None, branch_sum)
    loads = [
        pltpu.make_async_copy(branch_hbm.at[seq.block(*place)], total.at[k], load_sem.at[k])
        for k, place in enumerate(FAR_FIRST)
    ]
    for load in loads:
        load.start()
    own = head.block(0, 0)
    rows_buf[own] = grad_resid_ref[...].astype(LOW)
    greet_all(head, seq)
    gather.arrive(0, 0)
    loads[0].wait()
    reduce.settle(2, 1)
    loads[1].wait()
    reduce.settle(2, 0)
    transpose_into(kt_ref, k_ref)
    transpose_into(mkt_ref, mk_ref)
    for ref in (dk_ref, dv_ref, dmk_ref, dmv_ref, wo_sum, fold_ref):
        ref[...] = jnp.zeros_like(ref)
    width, model = wo_ref.shape
    for load in loads[2:]:
        load.wait()

    def step(k, carry):
        @pl.when(k == 0)
        def _():
            gather.sibling(0, 0)

        @pl.when(k == 1)
        def _():
            gather.arrive(-1, 0)
            gather.arrive(1, 0)
            reduce.settle(1, 1)
            reduce.settle(-1, 1)
            gather.arrive(0, 1)
            gather.sibling(-1, 0)

        @pl.when(k == 2)
        def _():
            reduce.settle(1, 0)
            reduce.settle(-1, 0)
            gather.sibling(1, 0)

        @pl.when(k == 3)
        def _():
            gather.arrive(2, 0)
            gather.sibling(0, 1)

        @pl.when(k == 4)
        def _():
            gather.arrive(-1, 1)
            gather.arrive(1, 1)
            gather.sibling(2, 0)

        @pl.when(k == 5)
        def _():
            reduce.settle(0, 1)
            gather.sibling(-1, 1)

        @pl.when(k == 6)
        def _():
            gather.arrive(2, 1)
            gather.sibling(1, 1)

        @pl.when(k == 7)
        def _():
            gather.sibling(2, 1)

        chip = chip_at(head, NEAR_FIRST, k)
        at = pl.ds(pl.multiple_of(chip * QROWS, QROWS), QROWS)
        rows = rows_buf[pl.ds(chip * 2, 2)].reshape(QROWS, model)
        grad_rows = dot_nt(rows, wo_ref[...]).astype(LOW)
        wo_sum[...] += dot(attn_t_ref[:, at], rows)
        dq = attend_back_chunk(
            chip, q_ref, k_ref, kt_ref, v_ref, mk_ref, mkt_ref, mv_ref,
            mem_bias_ref[...], tail_bias_ref[...], attn_t_ref, lse_ref,
            grad_rows, dk_ref, dv_ref, dmk_ref, dmv_ref,
        ).astype(LOW)
        own_t_ref[:width, at] = dq
        own_ref[at, :width] = dq.T
        return carry

    lax.fori_loop(0, 8, step, 0)

    def finish_keys(i, carry):
        at = pl.ds(pl.multiple_of(i * 256, 256), 256)
        dk = dk_ref[at, :].astype(LOW)
        dv = dv_ref[at, :].astype(LOW)
        own_ref[at, width : 2 * width] = dk
        own_ref[at, 2 * width :] = dv
        own_t_ref[width : 2 * width, at] = dk.T
        own_t_ref[2 * width :, at] = dv.T
        fold_ref[...] += fold_rows(own_ref[at, :].astype(WIDE))
        return carry

    lax.fori_loop(0, q_ref.shape[0] // 256, finish_keys, 0)
    for i, ref in enumerate((dmk_ref, dmv_ref)):
        low = ref[...].astype(LOW)
        mem_ref[:, i * width : (i + 1) * width] = low
        mem_t_ref[i * width : (i + 1) * width, :] = low.T
    fold_ref[:, width:] += fold_rows(mem_ref[...].astype(WIDE))
    sums_ref[...] = jnp.sum(fold_ref[...], axis=0, keepdims=True)
    grad_wo_ref[...] = wo_sum[...].astype(LOW)
    reduce.settle(0, 0)

    def finish(rows):
        out_ref[rows] = (resid_ref[rows] + branch_sum[rows] + b_down_ref[...]).astype(LOW)

    row_tiles(BLOCK, finish)
    gather.drain()
    reduce.drain()


def grad_layer(
    grad_resid, resid, b_down, branch, wo, q, k, v, mk, mv, mem_bias, tail_bias, attn_t, lse,
):
    rows, model = grad_resid.shape
    length, width = q.shape
    return pl.pallas_call(
        grad_kernel,
        out_shape=(
            jax.ShapeDtypeStruct((rows, model), LOW),
            jax.ShapeDtypeStruct((length, 3 * width), LOW),
            jax.ShapeDtypeStruct((3 * width, length), LOW),
            jax.ShapeDtypeStruct((MEMROWS, 2 * width), LOW),
            jax.ShapeDtypeStruct((2 * width, MEMROWS), LOW),
            jax.ShapeDtypeStruct((width, model), LOW),
            jax.ShapeDtypeStruct((1, 3 * width), WIDE),
        ),
        in_specs=[VMEM] * 3 + [ANY] + [VMEM] * 10,
        out_specs=(VMEM,) * 7,
        scratch_shapes=[
            pltpu.VMEM((16, rows, model), LOW),
            pltpu.VMEM((width, length), LOW),
            pltpu.VMEM((width, MEMROWS), LOW),
            pltpu.VMEM((length, width), WIDE),
            pltpu.VMEM((length, width), WIDE),
            pltpu.VMEM((MEMROWS, width), WIDE),
            pltpu.VMEM((MEMROWS, width), WIDE),
            pltpu.VMEM((width, model), WIDE),
            pltpu.VMEM((rows, model), WIDE),
            pltpu.VMEM((8, 3 * width), WIDE),
            pltpu.SemaphoreType.DMA((8,)),
        ] + [pltpu.SemaphoreType.DMA((Gather.COPIES,))] * 2 + Reduce.scratch(model, False, False),
        compiler_params=pltpu.CompilerParams(
            collective_id=3, has_side_effects=True, vmem_limit_bytes=VMEM_LIMIT
        ),
        name="grad_layer",
    )(
        grad_resid, resid, b_down, branch, wo, q, k, v, mk, mv, mem_bias, tail_bias, attn_t, lse,
    )


SUM_ROWS = 16


def close_kernel(
    own_ref, own_t_ref, mem_ref, mem_t_ref, grad_wo_ref, mem_normed_ref, normed_hbm, w_t_ref,
    gain_ref, shift_ref, bias_sums_ref, feed_sums_ref, b_up_ref,
    grad_normed_ref, grad_w_ref, small_ref,
    rows_buf, mem_pad, norm_sums, pay_ref, core_land, pay_half, pay_land, seq_land,
    core_send, core_recv, pay_send, pay_recv, seq_send, seq_recv, all_send, all_recv, load_sem,
    total, stage, land, send, recv, near_stage, near_land,
    w_total, w_stage, w_land, w_send, w_recv, g_send, g_recv,
):
    head, seq = Group("head"), Group("seq")
    reduce = Reduce(head, total, stage, land, send, recv, 112, (near_stage, near_land), grad_normed_ref)
    w_reduce = Reduce(seq, w_total, w_stage, w_land, w_send, w_recv, 128, None, w_total.at[7])
    gather = Gather(seq, grad_w_ref, g_send, g_recv, 128)
    plane = Plane(head)
    pay = Spread(plane, pay_send, pay_recv)
    across = Spread(seq, seq_send, seq_recv)
    back = Spread(plane, all_send, all_recv)
    load = pltpu.make_async_copy(normed_hbm, rows_buf, load_sem)
    load.start()
    width = grad_wo_ref.shape[0]
    model = rows_buf.shape[2]
    length = own_ref.shape[0]
    wide = model // 2
    share = model // head.size
    mem_pad[...] = jnp.zeros_like(mem_pad)
    mem_pad[pl.ds(width, 2 * width), :] = mem_t_ref[...]
    norm_sums[...] = jnp.zeros_like(norm_sums)
    greet_everyone(head, plane, seq)

    def chunk(k):
        chip = head.chip(*FAR_FIRST[k])

        def part(core):
            at = pl.ds(pl.multiple_of(chip * QROWS + core * BLOCK, BLOCK), BLOCK)
            return own_ref[at, :]

        mine, other = part(head.core), part(1 - head.core)
        for at in range(0, model, 512):
            near_stage[k, :, at : at + 512] = dot(other, w_t_ref[:, at : at + 512]).astype(LOW)
        reduce.near_copy(k).start()
        for at in range(0, model, 512):
            total[k, :, at : at + 512] = dot(mine, w_t_ref[:, at : at + 512])

    def weights(k, carry):
        target = chip_at(seq, FAR_FIRST, k)
        part, side = target // 2, target % 2
        columns = pl.ds(pl.multiple_of(side * wide, wide), wide)

        @pl.when(part < 3)
        def _():
            at = pl.ds(pl.multiple_of(part * width, width), width)
            term = dot(
                own_t_ref[at, :], rows_buf[:, :, columns].reshape(length, wide)
            ) + dot(mem_pad[at, :], mem_normed_ref[:, columns])
            w_total[k] = term
            flat = w_t_ref[at, columns].astype(WIDE)
            norm_sums[0:1, columns] += jnp.sum(flat * term, axis=0, keepdims=True)

        @pl.when(part == 3)
        def _():
            w_total[k] = grad_wo_ref[:, columns].astype(WIDE)

        return carry

    def shift_sums():
        sums = bias_sums_ref[...]
        high = sums.astype(LOW)
        rest = (sums - high.astype(WIDE)).astype(LOW)
        pair = jnp.concatenate([high, rest, jnp.zeros((14, sums.shape[1]), LOW)], axis=0)
        both = dot(pair, w_t_ref[...])
        norm_sums[1:2, :] = both[0:1] + both[1:2]

    def core_copy(i, src, dst):
        return pltpu.make_async_remote_copy(
            src_ref=src,
            dst_ref=dst,
            send_sem=core_send.at[i],
            recv_sem=core_recv.at[i],
            device_id=head.device(0, 0, 1),
            device_id_type=MESH,
        )

    def half_of(core):
        return pay_ref.at[:, pl.ds(pl.multiple_of(core * wide, wide), wide)]

    def pay_part(i):
        return pay_half.at[:, pl.ds(pl.multiple_of(i * share, share), share)]

    def pay_core():
        return core_copy(0, half_of(1 - head.core), core_land)

    def pay_whole():
        return core_copy(1, small_ref.at[head.core], small_ref.at[head.core])

    def pay_start():
        pay_ref[:MEMROWS, :] = dot(mem_ref[...], w_t_ref[width:, :]).astype(LOW)
        at_gain = norm_sums[0:1, :] - shift_ref[...] * norm_sums[1:2, :]
        rows = [at_gain / gain_ref[...], norm_sums[1:2, :], feed_sums_ref[...]]
        units = b_up_ref.shape[1]
        per_row = model // units
        for r in range(8 // per_row):
            row = [jnp.where(seq.me == r * per_row + c, b_up_ref[...], 0.0) for c in range(per_row)]
            rows.append(jnp.concatenate(row, axis=1))
        rows.append(jnp.zeros((SUM_ROWS - 6 - 8 // per_row, model), WIDE))
        pay_ref[MEMROWS:, :] = jnp.concatenate(rows, axis=0).astype(LOW)
        pay_core().start()

    def pay_send_parts():
        pay_core().wait_recv()
        pay_half[...] = (half_of(head.core)[...].astype(WIDE) + core_land[...].astype(WIDE)).astype(LOW)
        pay_land[plane.me] = pay_part(plane.me)[...]
        pay.start(pay_part, pay_land)

    def pay_sum():
        pay.wait(pay_land)
        sums = pay_land[0].astype(WIDE)
        for i in range(1, 8):
            sums += pay_land[i].astype(WIDE)
        small_ref[head.core, plane.me, :MEMROWS, :] = sums[:MEMROWS].astype(LOW)
        used = 6 + 8 * b_up_ref.shape[1] // model
        rows = [sums[MEMROWS : MEMROWS + used]]
        rows += [bias_sums_ref[:, i * width : (i + 1) * width] for i in range(3)]
        rows.append(jnp.zeros((SUM_ROWS - 3 - used, share), WIDE))
        seq_land[seq.me] = jnp.concatenate(rows, axis=0).astype(LOW)
        across.start(lambda i: seq_land.at[seq.me], seq_land)

    def pay_back():
        across.wait(seq_land)
        sums = seq_land[0].astype(WIDE)
        for i in range(1, 8):
            sums += seq_land[i].astype(WIDE)
        small_ref[head.core, plane.me, MEMROWS:, :] = sums.astype(LOW)
        back.start(lambda i: small_ref.at[head.core, plane.me], small_ref.at[head.core])

    def pay_end():
        back.wait(small_ref.at[head.core])
        pay_whole().start()

    chunk(0)
    chunk(1)
    load.wait()
    lax.fori_loop(0, 2, weights, 0)
    w_reduce.settle(2, 1)
    w_reduce.settle(2, 0)
    reduce.settle(2, 1)
    reduce.settle(2, 0)
    lax.fori_loop(2, 4, weights, 0)
    w_reduce.settle(1, 1)
    w_reduce.settle(-1, 1)
    chunk(2)
    chunk(3)
    lax.fori_loop(4, 6, weights, 0)
    w_reduce.settle(1, 0)
    w_reduce.settle(-1, 0)
    reduce.settle(1, 1)
    reduce.settle(-1, 1)
    lax.fori_loop(6, 7, weights, 0)
    w_reduce.settle(0, 1)
    lax.fori_loop(7, 8, weights, 0)
    shift_sums()
    pay_start()
    chunk(4)
    chunk(5)
    pay_send_parts()
    reduce.settle(1, 0)
    reduce.settle(-1, 0)
    w_reduce.settle(0, 0)
    grad_w_ref[seq.me] = w_total[7].astype(LOW)
    gather.arrive(0, 0)
    chunk(6)
    chunk(7)
    gather.arrive(-1, 0)
    gather.arrive(1, 0)
    gather.arrive(0, 1)
    pay_sum()
    reduce.settle(0, 1)
    gather.arrive(2, 0)
    gather.arrive(-1, 1)
    gather.arrive(1, 1)
    pay_back()
    reduce.settle(0, 0)
    pay_end()
    gather.arrive(2, 1)
    core_copy(1, small_ref.at[1 - head.core], small_ref.at[1 - head.core]).wait_recv()
    pay_core().wait_send()
    pay_whole().wait_send()
    pay.drain(pay_part, pay_land)
    across.drain(lambda i: seq_land.at[seq.me], seq_land)
    back.drain(lambda i: small_ref.at[head.core, plane.me], small_ref.at[head.core])
    gather.drain()
    w_reduce.drain()
    reduce.drain()


def close_layer(
    own, own_t, mem, mem_t, grad_wo, mem_normed, normed_all, w_t, gain, shift, bias_sums,
    feed_sums, b_up,
):
    rows, model = normed_all.shape[1:]
    width = grad_wo.shape[0]
    sems = [pltpu.SemaphoreType.DMA((Gather.COPIES,))] * 2
    pay_rows = MEMROWS + SUM_ROWS
    return pl.pallas_call(
        close_kernel,
        out_shape=(
            jax.ShapeDtypeStruct((rows, model), WIDE),
            jax.ShapeDtypeStruct((8, width, model // 2), LOW),
            jax.ShapeDtypeStruct((2, 8, pay_rows, model // 16), LOW),
        ),
        in_specs=[VMEM] * 6 + [ANY] + [VMEM] * 6,
        out_specs=(VMEM,) * 3,
        scratch_shapes=[
            pltpu.VMEM((16, rows, model), LOW),
            pltpu.VMEM((3 * width, MEMROWS), LOW),
            pltpu.VMEM((8, model), WIDE),
            pltpu.VMEM((pay_rows, model), LOW),
            pltpu.VMEM((pay_rows, model // 2), LOW),
            pltpu.VMEM((pay_rows, model // 2), LOW),
            pltpu.VMEM((8, pay_rows, model // 16), LOW),
            pltpu.VMEM((8, SUM_ROWS, model // 16), LOW),
            pltpu.SemaphoreType.DMA((2,)),
            pltpu.SemaphoreType.DMA((2,)),
            pltpu.SemaphoreType.DMA((8,)),
            pltpu.SemaphoreType.DMA((8,)),
            pltpu.SemaphoreType.DMA((8,)),
            pltpu.SemaphoreType.DMA((8,)),
            pltpu.SemaphoreType.DMA((8,)),
            pltpu.SemaphoreType.DMA((8,)),
            pltpu.SemaphoreType.DMA,
        ] + Reduce.scratch(model, True, True) + Reduce.scratch(model // 2, True, False) + sems,
        compiler_params=pltpu.CompilerParams(
            collective_id=4, has_side_effects=True, vmem_limit_bytes=VMEM_LIMIT
        ),
        name="close_layer",
    )(
        own, own_t, mem, mem_t, grad_wo, mem_normed, normed_all, w_t, gain, shift, bias_sums,
        feed_sums, b_up,
    )


def finish_kernel(
    grad_normed_hbm, hidden_hbm, grad_resid_hbm, gain_ref, grad_w_hbm, small_ref, memory_ref,
    feed_w_hbm, output_hbm,
    out_hbm, grad_hidden_hbm, grad_memory_ref, grad_qkv_hbm, b_query_ref, b_value_ref, grad_wo_hbm,
    b_out_ref, gain_one_ref, shift_one_ref, gain_two_ref, shift_two_ref,
    w_up_hbm, b_up_ref, w_down_hbm, b_down_ref,
    grad_w_ref, grad_normed_ref, hidden_ref, grad_resid_ref, feed_w_ref, output_ref,
    grad_qkv_ref, grad_wo_ref, w_down_ref, grad_hidden_ref, mem_wide, spread_ref, load_sem, out_sem,
):
    wide, units = grad_w_ref.shape[2], w_up_hbm.shape[1]
    loads = [
        pltpu.make_async_copy(src, dst, load_sem.at[i])
        for i, (src, dst) in enumerate(
            (
                (grad_w_hbm, grad_w_ref), (grad_normed_hbm, grad_normed_ref), (hidden_hbm, hidden_ref),
                (grad_resid_hbm, grad_resid_ref), (feed_w_hbm, feed_w_ref), (output_hbm, output_ref),
            )
        )
    ]
    for load in loads:
        load.start()
    outs = []

    def leave(src, dst):
        out = pltpu.make_async_copy(src, dst, out_sem.at[len(outs)])
        out.start()
        outs.append(out)

    share = small_ref.shape[3]
    for i in range(16):
        spread_ref[:, i * share : (i + 1) * share] = small_ref[i // 8, i % 8].astype(WIDE)

    def norm_back(values, incoming):
        normal, rstd = normal_of(values)
        scaled = incoming * gain_ref[...]
        inner = jnp.mean(scaled, axis=-1, keepdims=True)
        along = jnp.mean(scaled * normal, axis=-1, keepdims=True)
        return rstd * (scaled - inner - normal * along)

    def back(rows):
        grad_hidden = grad_resid_ref[rows] + norm_back(
            hidden_ref[rows].astype(WIDE), grad_normed_ref[rows]
        )
        grad_hidden_ref[rows] = grad_hidden[:, None, :]

    loads[0].wait()
    for i in range(3):
        for j in range(2):
            grad_qkv_ref[i, j * wide : (j + 1) * wide, :] = grad_w_ref[2 * i + j].astype(WIDE).T
        leave(grad_qkv_ref.at[i], grad_qkv_hbm.at[i])
    for j in range(2):
        grad_wo_ref[:, j * wide : (j + 1) * wide] = grad_w_ref[6 + j].astype(WIDE)
    leave(grad_wo_ref, grad_wo_hbm)
    for load in loads[1:]:
        load.wait()
    leave(output_ref, out_hbm)
    leave(feed_w_ref.at[:, pl.ds(0, units)], w_up_hbm)
    w_down_ref[...] = feed_w_ref[:, units:].T
    leave(w_down_ref, w_down_hbm)
    row_tiles(hidden_ref.shape[0], back, 32)
    leave(grad_hidden_ref, grad_hidden_hbm)
    slots = memory_ref.shape[0]
    mem_wide[...] = jnp.zeros_like(mem_wide)
    mem_wide[:slots, :] = memory_ref[...].astype(WIDE)

    def back_memory(rows):
        mem_wide[rows] = norm_back(mem_wide[rows], spread_ref[rows])

    row_tiles(MEMROWS, back_memory, 32)
    grad_memory_ref[...] = mem_wide[:slots, :][:, None, :]
    sums = [spread_ref[MEMROWS + i : MEMROWS + i + 1, :] for i in range(SUM_ROWS)]
    ordered = (gain_one_ref, shift_one_ref, b_out_ref, gain_two_ref, shift_two_ref, b_down_ref)
    for ref, row in zip(ordered, sums):
        ref[...] = row
    model = b_out_ref.shape[1]
    for i in range(4):
        b_up_ref[:, i * model : (i + 1) * model] = sums[6 + i]
    index = lax.axis_index("head")
    mine = small_ref[index % 2, index // 2].astype(WIDE)
    b_query_ref[...] = mine[MEMROWS + 10 : MEMROWS + 11, :]
    b_value_ref[...] = mine[MEMROWS + 12 : MEMROWS + 13, :]
    for out in outs:
        out.wait()


def finish_layer(
    grad_normed, hidden, grad_resid, gain, grad_w, small, memory, feed_w, output
):
    rows, model = hidden.shape
    width, units = grad_w.shape[1], feed_w.shape[1] // 2
    wide = lambda *shape: jax.ShapeDtypeStruct(shape, WIDE)
    return pl.pallas_call(
        finish_kernel,
        out_shape=(
            jax.ShapeDtypeStruct((rows, model), LOW), wide(rows, 1, model), wide(memory.shape[0], 1, model),
            wide(3, model, width), wide(1, width), wide(1, width), wide(width, model),
            wide(1, model), wide(1, model), wide(1, model), wide(1, model), wide(1, model),
            wide(rows, units), wide(1, 8 * units), wide(units, rows), wide(1, model),
        ),
        in_specs=[ANY] * 3 + [VMEM, ANY, VMEM, VMEM, ANY, ANY],
        out_specs=(ANY, ANY, VMEM, ANY, VMEM, VMEM, ANY) + (VMEM,) * 5 + (ANY, VMEM, ANY, VMEM),
        scratch_shapes=[
            pltpu.VMEM(grad_w.shape, LOW),
            pltpu.VMEM((rows, model), WIDE),
            pltpu.VMEM((rows, model), LOW),
            pltpu.VMEM((rows, model), WIDE),
            pltpu.VMEM(feed_w.shape, WIDE),
            pltpu.VMEM((rows, model), LOW),
            pltpu.VMEM((3, model, width), WIDE),
            pltpu.VMEM((width, model), WIDE),
            pltpu.VMEM((units, rows), WIDE),
            pltpu.VMEM((rows, 1, model), WIDE),
            pltpu.VMEM((MEMROWS, model), WIDE),
            pltpu.VMEM((MEMROWS + SUM_ROWS, model), WIDE),
            pltpu.SemaphoreType.DMA((6,)),
            pltpu.SemaphoreType.DMA((8,)),
        ],
        compiler_params=pltpu.CompilerParams(vmem_limit_bytes=VMEM_LIMIT),
        name="finish_layer",
    )(grad_normed, hidden, grad_resid, gain, grad_w, small, memory, feed_w, output)


def on_device(
    hidden, memory, counts, w_qkv, b_query, b_value, output_weight, b_out,
    gain_one, shift_one, gain_two, shift_two, w_up, up_bias, w_down, b_down, cotangent,
):
    hidden, memory, cot = hidden[:, 0], memory[:, 0], cotangent[:, 0]
    model = hidden.shape[1]
    width = w_qkv.shape[2]
    w_parts = jnp.transpose(w_qkv, (1, 0, 2))
    gain_one, shift_one, gain_two, shift_two, b_out, b_down, b_query, b_value, up_bias = (
        vector[None]
        for vector in (
            gain_one, shift_one, gain_two, shift_two, b_out, b_down, b_query, b_value, up_bias
        )
    )
    q, k, v, mk, mv, mem_normed, mem_bias, tail_bias, w_t, normed_all = open_layer(
        hidden, memory, counts, gain_one, shift_one, w_parts, b_query, b_value
    )
    attn_t, lse, resid, second, w_up_t, cot_all = attend_layer(
        q, k, v, mk, mv, mem_bias, tail_bias, output_weight, hidden, b_out, gain_two, shift_two,
        cot, w_up,
    )
    grad_resid, feed_sums, branch, feed_w, grad_b_up = feed_layer(
        second, w_up, w_up_t, w_down, cot_all, up_bias, resid, gain_two, cot
    )
    output, own, own_t, mem, mem_t, grad_wo, bias_sums = grad_layer(
        grad_resid, resid, b_down, branch, output_weight,
        q, k, v, mk, mv, mem_bias, tail_bias, attn_t, lse,
    )
    grad_normed, grad_w, small = close_layer(
        own, own_t, mem, mem_t, grad_wo, mem_normed, normed_all, w_t, gain_one, shift_one,
        bias_sums, feed_sums, grad_b_up,
    )
    outs = finish_layer(
        grad_normed, hidden, grad_resid, gain_one, grad_w, small, memory, feed_w, output
    )
    output, grad_hidden, grad_memory, grad_w_qkv, *rest = outs
    rest = [part[0] if part.shape[0] == 1 else part for part in rest]
    return (
        output[:, None],
        grad_hidden,
        grad_memory,
        jnp.transpose(grad_w_qkv, (1, 0, 2)),
        *rest,
    )


def solution(mesh):
    return jax.shard_map(
        on_device,
        mesh=mesh,
        in_specs=(
            P("head", "seq", None),
            P(None, "seq", None),
            P("seq", None),
            P(None, None, "head"),
            P("head"),
            P("head"),
            P("head", None),
            P(),
            P(),
            P(),
            P(),
            P(),
            P(None, "seq"),
            P(),
            P("seq", None),
            P(),
            P("head", "seq", None),
        ),
        out_specs=(
            P("head", "seq", None),
            P("head", "seq", None),
            P(None, "seq", None),
            P(None, None, "head"),
            P("head"),
            P("head"),
            P("head", None),
            P(),
            P(),
            P(),
            P(),
            P(),
            P("head", "seq"),
            P(),
            P("seq", "head"),
            P(),
        ),
        check_vma=False,
    )
```
